32 devices in a mesh: dp: 8 (over z, x), seq: 4 (over y, core).
Axes of the slice: x: 2, y: 2, z: 4, core: 2. Of those that a mesh axis runs over, the one named last changes fastest.
Arguments:
- hidden_in: bfloat16 [24576, 1024], P(('dp', 'seq')), may hold values from -6 to 6
- key_bias: float32 [8, 3072], P('dp', 'seq'), may hold values from -4 to 4
- w_qkv: bfloat16 [1024, 3072], P('dp'), may hold values from -0.1875 to 0.1875
- bias_q: bfloat16 [1024], P('dp'), may hold values from -3 to 3
- bias_v: bfloat16 [1024], P('dp'), may hold values from -0.75 to 0.75
- w_out: bfloat16 [1024, 1024], P('dp'), may hold values from -3 to 3
- bias_out: bfloat16 [1024], P('dp'), may hold values from -3 to 3
- gain_attn: bfloat16 [1024], P('dp'), may hold values from 0.25 to 1.75
- shift_attn: bfloat16 [1024], P('dp'), may hold values from -3 to 3
- w_up: bfloat16 [1024, 4096], P('dp'), may hold values from -0.1875 to 0.1875
- bias_up: bfloat16 [4096], P('dp'), may hold values from -3 to 3
- w_down: bfloat16 [4096, 1024], P('dp'), may hold values from -0.09375 to 0.09375
- bias_down: bfloat16 [1024], P('dp'), may hold values from -3 to 3
- gain_ffn: bfloat16 [1024], P('dp'), may hold values from 0.25 to 1.75
- shift_ffn: bfloat16 [1024], P('dp'), may hold values from -3 to 3
- grad_out: bfloat16 [24576, 1024], P(('dp', 'seq')), may hold values from -6 to 6
Outputs:
- output: bfloat16 [24576, 1024], P(('dp', 'seq'))
- grad_in: float32 [24576, 1024], P(('dp', 'seq'))
- grad_w_qkv: float32 [1024, 3072], P('dp')
- grad_bias_q: float32 [1024], P('dp')
- grad_bias_v: float32 [1024], P('dp')
- grad_w_out: float32 [1024, 1024], P('dp')
- grad_bias_out: float32 [1024], P('dp')
- grad_gain_attn: float32 [1024], P('dp')
- grad_shift_attn: float32 [1024], P('dp')
- grad_w_up: float32 [1024, 4096], P('dp')
- grad_bias_up: float32 [4096], P('dp')
- grad_w_down: float32 [4096, 1024], P('dp')
- grad_bias_down: float32 [1024], P('dp')
- grad_gain_ffn: float32 [1024], P('dp')
- grad_shift_ffn: float32 [1024], P('dp')
The draws below stay inside these ranges and needn't reach their ends.
All inputs are finite; a program needn't handle non-finite values.
Results may differ from the reference program's by a relative error of at most 0.02.
Values may be sent and summed in bfloat16 or wider, within the bound.
A program may use at most 192 MiB of HBM per device.

```python
import jax
import jax.numpy as jnp
from jax import lax

D = 1024
HEADS = 16
HEAD_DIM = 64
FF = 4096
LENGTH = 3072
SEQS = 8
TOKENS = 24576


def steps_of(rng, dims, shards, low, top_value):
    def one(axis_at, shards_of):
        draws = jax.random.uniform(jax.random.fold_in(jax.random.fold_in(rng, 6), axis_at), (shards_of,), jnp.float32, low / len(shards), top_value / len(shards))
        return jnp.repeat(jnp.exp(draws), dims[axis_at] // shards_of).reshape((-1,) + (1,) * (len(dims) - axis_at - 1))

    loudness = one(*shards[0])
    for cut in shards[1:]:
        loudness = loudness * one(*cut)
    return loudness


def noise(own_key, shape, scale, reach, split=(), kind=jnp.bfloat16):
    array = scale * jax.random.normal(own_key, shape, jnp.float32)
    if split:
        array = array * steps_of(own_key, shape, split, -0.22, 0.18)
    return jnp.clip(array, -reach, reach).astype(kind)


def setup_inputs(seed: int = 0) -> dict:
    keys = jax.random.split(jax.random.key(seed), 17)
    return {
        "hidden_in": noise(keys[0], (TOKENS, D), 1.0, 6.0, ((0, 32),)),
        "key_bias": noise(keys[1], (SEQS, LENGTH), 1.0, 4.0, ((0, 8), (1, 4)), jnp.float32),
        "w_qkv": noise(keys[2], (D, 3 * D), D ** -0.5, 0.1875, ((0, 8),)),
        "bias_q": noise(keys[3], (D,), 0.5, 3.0, ((0, 8),)),
        "bias_v": noise(keys[4], (D,), 0.05, 0.75, ((0, 8),)),
        "w_out": noise(keys[5], (D, D), 4 ** -0.5, 3.0, ((0, 8),)),
        "bias_out": noise(keys[6], (D,), 0.5, 3.0, ((0, 8),)),
        "gain_attn": jnp.clip(1.0 + 0.15 * jax.random.normal(keys[7], (D,), jnp.float32), 0.25, 1.75).astype(jnp.bfloat16),
        "shift_attn": noise(keys[8], (D,), 0.5, 3.0, ((0, 8),)),
        "w_up": noise(keys[9], (D, FF), D ** -0.5, 0.1875, ((0, 8),)),
        "bias_up": noise(keys[10], (FF,), 0.5, 3.0, ((0, 8),)),
        "w_down": noise(keys[11], (FF, D), FF ** -0.5, 0.09375, ((0, 8),)),
        "bias_down": noise(keys[12], (D,), 0.5, 3.0, ((0, 8),)),
        "gain_ffn": jnp.clip(1.0 + 0.15 * jax.random.normal(keys[13], (D,), jnp.float32), 0.25, 1.75).astype(jnp.bfloat16),
        "shift_ffn": noise(keys[14], (D,), 0.5, 3.0, ((0, 8),)),
        "grad_out": noise(keys[15], (TOKENS, D), 1.0, 6.0, ((0, 32),)),
    }


norm_eps = 1e-05

@jax.custom_vjp
def low(v):
    return lax.optimization_barrier(v.astype(jnp.bfloat16)).astype(jnp.float32)

@jax.custom_vjp
def low_back(v):
    return v

def low_keep(v):
    return (low(v), None)

def low_pass(kept, grad):
    return (grad,)

def back_keep(v):
    return (v, None)

def back_low(kept, grad):
    return (low(grad),)
low.defvjp(low_keep, low_pass)
low_back.defvjp(back_keep, back_low)

def matmul(left, right):
    return jnp.dot(left, right, preferred_element_type=jnp.float32, precision=lax.Precision.HIGHEST)

def layer_norm(hidden, gain_vec, shift_vec):
    row_mean = lax.optimization_barrier(jnp.mean(hidden, -1, keepdims=True))
    centered = hidden - row_mean
    row_var = lax.optimization_barrier(jnp.mean(centered * centered, -1, keepdims=True))
    return centered * lax.rsqrt(row_var + norm_eps) * gain_vec + shift_vec

def attend_block(query_blk, keys_all, values_all, bias_row):
    scores = jnp.einsum('bhe,lhe->hbl', query_blk, keys_all, precision=lax.Precision.HIGHEST) * HEAD_DIM ** (-0.5) + bias_row
    scores = low_back(scores)
    row_max = lax.optimization_barrier(jnp.max(scores, -1, keepdims=True))
    expo = jnp.exp(scores - row_max)
    probs = low(expo / lax.optimization_barrier(jnp.sum(expo, -1, keepdims=True)))
    return jnp.einsum('hbl,lhe->bhe', probs, values_all, precision=lax.Precision.HIGHEST)

def attend_sequence(carry_in, item_in):
    heads_all, bias_row = item_in
    block_rows = min(512, LENGTH)
    queries = heads_all[:, 0].reshape(LENGTH // block_rows, block_rows, HEADS, HEAD_DIM)
    keys_all = heads_all[:, 1]
    values_all = heads_all[:, 2]
    blocked = jax.checkpoint(lambda query_blk: attend_block(query_blk, keys_all, values_all, bias_row))
    context = lax.map(blocked, queries)
    return (carry_in, context.reshape(LENGTH, D))

def forward(hidden, key_bias, w_qkv, bias_q, bias_v, w_out, bias_out, gain_attn, shift_attn, w_up, bias_up, w_down, bias_down, gain_ffn, shift_ffn):
    no_bias = jnp.zeros((D,), jnp.float32)
    heads_in = low(low_back(matmul(hidden, w_qkv) + jnp.concatenate([bias_q, no_bias, bias_v])))
    heads_in = heads_in.reshape(SEQS, LENGTH, 3, HEADS, HEAD_DIM)
    _, context = lax.scan(attend_sequence, jnp.zeros((), jnp.float32), (heads_in, key_bias))
    context = low(low_back(context.reshape(TOKENS, D)))
    attended = hidden + low_back(matmul(context, w_out)) + bias_out
    normed = layer_norm(attended, gain_attn, shift_attn)
    pre_act = low_back(matmul(low(normed), w_up)) + bias_up
    activ = low(jax.nn.gelu(pre_act, approximate=False))
    branch_sum = normed + low_back(matmul(activ, w_down)) + bias_down
    return layer_norm(branch_sum, gain_ffn, shift_ffn)

def reference(hidden_in, key_bias, w_qkv, bias_q, bias_v, w_out, bias_out, gain_attn, shift_attn, w_up, bias_up, w_down, bias_down, gain_ffn, shift_ffn, grad_out):
    params = (w_qkv, bias_q, bias_v, w_out, bias_out, gain_attn, shift_attn, w_up, bias_up, w_down, bias_down, gain_ffn, shift_ffn)
    params = tuple((param.astype(jnp.float32) for param in params))
    hidden = hidden_in.astype(jnp.float32)

    def apply_layer(hidden_arg, *param_args):
        return forward(hidden_arg, key_bias, *param_args)
    result, pullback = jax.vjp(apply_layer, hidden, *params)
    grads = pullback(grad_out.astype(jnp.float32))
    return (result.astype(jnp.bfloat16), grads[0], grads[1], grads[2], grads[3], grads[4], grads[5], grads[6], grads[7], grads[8], grads[9], grads[10], grads[11], grads[12], grads[13])
```

```python
import functools

import jax
import jax.numpy as jnp
from jax import lax
from jax.experimental import pallas as pl
from jax.experimental.pallas import tpu as pltpu
from jax.sharding import PartitionSpec as P

HEAD_DIM = 64
LANES = 128
SCALE = HEAD_DIM**-0.5
norm_eps = 1e-05
F32 = jnp.float32
LOW = jnp.bfloat16


def layer_norm(hidden, gain_vec, shift_vec):
    row_mean = jnp.mean(hidden, -1, keepdims=True)
    centered = hidden - row_mean
    row_var = jnp.mean(centered * centered, -1, keepdims=True)
    return centered * lax.rsqrt(row_var + norm_eps) * gain_vec + shift_vec


def gelu_exact(pre_act):
    return jax.nn.gelu(pre_act, approximate=False)


def matmul(left, right):
    return jnp.dot(left, right, preferred_element_type=F32)


def matmul_left(left, right):
    return lax.dot_general(left, right, (((0,), (0,)), ((), ())), preferred_element_type=F32)


def matmul_right(left, right):
    return lax.dot_general(left, right, (((1,), (1,)), ((), ())), preferred_element_type=F32)


def thirds(value):
    first = value.astype(LOW)
    rest = value - first.astype(F32)
    second = rest.astype(LOW)
    third = (rest - second.astype(F32)).astype(LOW)
    return first.astype(F32), second.astype(F32), third.astype(F32)


def head_mask(rows, head):
    lane = lax.broadcasted_iota(jnp.int32, (rows, LANES), 1)
    return (lane < HEAD_DIM) if head == 0 else (lane >= HEAD_DIM)


def fill_keys(k_ref, v_ref, bias_ref, ka_ref, va_ref):
    rows = k_ref.shape[0]
    lane = lax.broadcasted_iota(jnp.int32, (rows, LANES), 1)
    first, second, third = thirds(bias_ref[...])
    extra = jnp.where(
        lane == 0, first, jnp.where(lane == 1, second, jnp.where(lane == 2, third, 1.0))
    )
    ka_ref[:, :LANES] = k_ref[...]
    ka_ref[:, LANES:] = jnp.where(lane < 6, extra, 0.0).astype(LOW)
    va_ref[:, :LANES] = v_ref[...]
    va_ref[:, LANES:] = jnp.where(lane < 3, 1.0, 0.0).astype(LOW)


def send_to(src, dst, send_sem, recv_sem, dp, seq):
    return pltpu.make_async_remote_copy(
        src_ref=src, dst_ref=dst, send_sem=send_sem, recv_sem=recv_sem,
        device_id=(dp, seq), device_id_type=pl.DeviceIdType.MESH,
    )


class Peers:
    def __init__(self, n, g):
        self.n, self.g, self.nz, self.ny = n, g, n // 2, g // 2
        self.d = lax.axis_index("dp")
        self.s = lax.axis_index("seq")
        self.z, self.x = self.d // 2, lax.rem(self.d, 2)
        self.y, self.c = self.s // 2, lax.rem(self.s, 2)
        self.xpeer = self.z * 2 + 1 - self.x
        self.cpeer = self.y * 2 + 1 - self.c

    def z_to(self, k):
        return lax.rem(self.z + k, self.nz) * 2 + self.x

    def z_from(self, k):
        return lax.rem(self.z + self.nz - k, self.nz) * 2 + self.x

    def side(self, dp):
        return (dp // 2) * 2 + 1 - self.x

    def y_to(self, k):
        return lax.rem(self.s + 2 * k, self.g)

    def y_from(self, k):
        return lax.rem(self.s + self.g - 2 * k, self.g)

    def s_to(self, k):
        return lax.rem(self.s + k, self.g)

    def s_from(self, k):
        return lax.rem(self.s + self.g - k, self.g)

    def barrier(self):
        sem = pltpu.get_barrier_semaphore()
        targets = [(self.z_to(k), self.s) for k in range(1, self.nz)]
        targets.append((self.xpeer, self.s))
        targets += [(self.d, self.s_to(k)) for k in range(1, self.g)]
        for target in targets:
            pl.semaphore_signal(
                sem, inc=1, device_id=target, device_id_type=pl.DeviceIdType.MESH
            )
        pl.semaphore_wait(sem, len(targets))


def pieces_of(half):
    return 2 if half % 64 == 0 and half >= 64 else 1


def weight_pieces(shapes):
    out = []
    for index, rows in enumerate(shapes):
        half = rows // 2
        count = pieces_of(half) if index else 1
        for part in range(count):
            out.append((index, part * (half // count), half // count))
    return out


def forward_kernel(
    hid_ref, wch_ref, kb_ref, wo_ref, wu_ref, wd_ref,
    ctx_out, own_ctx, q_out, k_out, v_out, qx_out, hid_out, wq_out, vec_out, wo_out, wu_out, wd_out,
    hid, wch, wq, kb, q_s, k_s, v_s, ka, va, ctx, qx,
    loc, hy, hc, hf, kbs, wz, wx, pz, px, pc, cs, kx,
    *, n, g, rows,
):
    me = Peers(n, g)
    d, s, nz, ny = me.d, me.s, me.nz, me.ny
    tok, width = hid_ref.shape
    length = tok * g
    deep = width // n
    gw = width // g
    pairs = gw // LANES
    cut = tok // 3
    shards = (wo_ref, wu_ref, wd_ref)
    fulls = (wo_out, wu_out, wd_out)
    pieces = weight_pieces([ref.shape[0] for ref in shards])
    me.barrier()

    local = [
        pltpu.make_async_copy(hid_ref, hid.at[s], loc.at[0]),
        pltpu.make_async_copy(wch_ref, wch.at[d], loc.at[1]),
        pltpu.make_async_copy(kb_ref, kb.at[s], loc.at[2]),
    ]
    keep = [
        pltpu.make_async_copy(shards[i], fulls[i].at[d], loc.at[3 + i]) for i in range(3)
    ]

    def y_copy(k, part, slot):
        span = pl.ds(part * cut, cut)
        return send_to(
            hid_ref.at[span], hid.at[slot, span], hy.at[0, k, part], hy.at[1, k, part], d,
            me.y_to(k),
        )

    def c_copy(slot):
        return send_to(hid_ref, hid.at[slot], hc.at[0], hc.at[1], d, me.cpeer)

    def f_copy(k, part, slot):
        span = pl.ds(part * cut, cut)
        return send_to(
            hid.at[slot, span], hid.at[slot, span], hf.at[0, k, part], hf.at[1, k, part], d,
            me.cpeer,
        )

    def kb_copy(k, slot):
        return send_to(kb_ref, kb.at[slot], kbs.at[0, k], kbs.at[1, k], d, me.s_to(k))

    def wz_copy(k, slot):
        return send_to(wch_ref, wch.at[slot], wz.at[0, k], wz.at[1, k], me.z_to(k), s)

    def wx_copy(k, src, slot):
        return send_to(src, wch.at[slot], wx.at[0, k], wx.at[1, k], me.xpeer, s)

    def c_of_y(k):
        return me.y_from(k) // 2 * 2 + 1 - me.c

    for copy in local:
        copy.start()
    for k in range(1, nz):
        wz_copy(k, d).start()
    wx_copy(0, wch_ref, d).start()
    for k in range(1, g):
        kb_copy(k, s).start()
    for part in range(3):
        for k in range(1, ny):
            y_copy(k, part, s).start()
    c_copy(s).start()
    for copy in keep:
        copy.start()

    def span_of(p):
        index, off, size = pieces[p]
        return index, pl.ds(pl.multiple_of(me.c * (shards[index].shape[0] // 2) + off, 16), size)

    def other_span(p):
        index, off, size = pieces[p]
        return index, pl.ds(
            pl.multiple_of((1 - me.c) * (shards[index].shape[0] // 2) + off, 16), size
        )

    def pz_copy(p, k, slot):
        index, span = span_of(p)
        return send_to(
            shards[index].at[span], fulls[index].at[slot, span], pz.at[0, p, k], pz.at[1, p, k],
            me.z_to(k), s,
        )

    def px_copy(p, k, slot):
        index, span = span_of(p)
        src = shards[index].at[span] if k == 0 else fulls[index].at[slot, span]
        return send_to(
            src, fulls[index].at[slot, span], px.at[0, p, k], px.at[1, p, k], me.xpeer, s
        )

    def pc_copy(p, k, side, slot, mine):
        index, span = span_of(p) if mine else other_span(p)
        return send_to(
            fulls[index].at[slot, span], fulls[index].at[slot, span], pc.at[0, p, k, side],
            pc.at[1, p, k, side], d, me.cpeer,
        )

    def piece_send(p):
        for k in range(1, nz):
            pz_copy(p, k, d).start()
        px_copy(p, 0, d).start()

    def piece_pass(p):
        for k in range(1, nz):
            slot = me.z_from(k)
            pz_copy(p, k, slot).wait_recv()
            px_copy(p, k, slot).start()
            pc_copy(p, k, 0, slot, True).start()

    def piece_share(p):
        for k in range(nz):
            slot = me.side(me.z_from(k)) if k else me.xpeer
            px_copy(p, k, slot).wait_recv()
            pc_copy(p, k, 1, slot, True).start()

    def piece_end(p):
        for k in range(1, nz):
            pc_copy(p, k, 0, me.z_from(k), False).wait_recv()
        for k in range(nz):
            pc_copy(p, k, 1, me.side(me.z_from(k)) if k else me.xpeer, False).wait_recv()
        for k in range(1, nz):
            pz_copy(p, k, d).wait_send()
            pc_copy(p, k, 0, me.z_from(k), True).wait_send()
        for k in range(nz):
            px_copy(p, k, me.z_from(k) if k else d).wait_send()
            pc_copy(p, k, 1, me.side(me.z_from(k)) if k else me.xpeer, True).wait_send()

    for k in range(1, nz):
        slot = me.z_from(k)
        wz_copy(k, slot).wait_recv()
        wx_copy(k, wch.at[slot], slot).start()
    for k in range(nz):
        slot = me.side(me.z_from(k)) if k else me.xpeer
        wx_copy(k, wch_ref, slot).wait_recv()
    for copy in local:
        copy.wait()
    piece_send(0)
    if len(pieces) > 1:
        piece_send(1)
    for j in range(n):
        wq[j * deep : (j + 1) * deep, :] = wch[j, :deep, :]
    bias_row = jnp.sum(wch[:, deep : deep + 16, :].astype(F32)[:, 0:1, :], 0)
    saves = [
        pltpu.make_async_copy(wq, wq_out, loc.at[6]),
        pltpu.make_async_copy(wch.at[:, pl.ds(deep, 16)], vec_out, loc.at[7]),
    ]
    for copy in saves:
        copy.start()

    tiles = tok // cut

    def project(step, carry):
        rel = step // tiles
        part = lax.rem(step, tiles)

        @pl.when(step == tiles)
        def _():
            c_copy(me.cpeer).wait_recv()

        for k in range(1, ny):
            @pl.when(step == 2 * k * tiles)
            def _(k=k):
                for sub in range(3):
                    y_copy(k, sub, me.y_from(k)).wait_recv()
                    f_copy(k, sub, me.y_from(k)).start()

            @pl.when(step == (2 * k + 1) * tiles)
            def _(k=k):
                for sub in range(3):
                    f_copy(k, sub, c_of_y(k)).wait_recv()

        y_at = lax.rem(me.y + ny - rel // 2, ny)
        c_at = lax.rem(me.c + rel, 2)
        slot = y_at * 2 + c_at
        got = matmul(hid[slot, pl.ds(part * cut, cut), :], wq[...]) + bias_row
        got = got.astype(LOW)
        span = pl.ds(pl.multiple_of(slot * tok + part * cut, cut), cut)
        for index, ref in enumerate((q_s, k_s, v_s)):
            for pair in range(pairs):
                at = index * gw + pair * LANES
                ref[pair, span, :] = got[:, at : at + LANES]
        return carry

    lax.fori_loop(0, g * tiles, project, 0)
    for k in range(1, g):
        kb_copy(k, me.s_from(k)).wait_recv()
    more = [
        pltpu.make_async_copy(hid, hid_out, loc.at[8]),
        pltpu.make_async_copy(q_s, q_out, loc.at[9]),
        pltpu.make_async_copy(k_s, k_out, loc.at[10]),
        pltpu.make_async_copy(v_s, v_out, loc.at[11]),
    ]
    for copy in more:
        copy.start()
    saves += more

    blocks = length // rows
    per = tok // rows
    steps = pairs * blocks

    def ctx_copy(pair, k, source):
        span = pl.ds(pl.multiple_of(me.s_to(k) * tok, tok), tok)
        return send_to(
            ctx.at[pair, span],
            ctx_out.at[:, pl.ds(pl.multiple_of(source * gw + pair * LANES, LANES), LANES)],
            cs.at[0, pair, k], cs.at[1, pair, k], d, me.s_to(k),
        )

    def ctx_keep(pair):
        return pltpu.make_async_copy(
            ctx.at[pair, pl.ds(pl.multiple_of(s * tok, tok), tok)],
            ctx_out.at[:, pl.ds(pl.multiple_of(s * gw + pair * LANES, LANES), LANES)],
            kx.at[pair],
        )

    events = {}
    every = max(1, steps // (len(pieces) + 1))
    for p in range(len(pieces)):
        if p >= 2:
            events.setdefault((p - 2) * every, []).append(lambda p=p: piece_send(p))
        events.setdefault((p + 1) * every - 1, []).append(lambda p=p: piece_pass(p))
        events.setdefault((p + 1) * every + 1, []).append(lambda p=p: piece_share(p))
    late = [e for t in sorted(events) if t >= steps for e in events[t]]

    def attend(step, carry):
        pair = step // blocks
        turn = lax.rem(step, blocks)
        k_own = lax.rem(1 + turn // per, g)
        owner = lax.rem(s + k_own, g)
        block = owner * per + lax.rem(turn, per)
        for t in sorted(events):
            if t < steps:
                @pl.when(step == t)
                def _(t=t):
                    for event in events[t]:
                        event()

        @pl.when(turn == 0)
        def _():
            lane = lax.broadcasted_iota(jnp.int32, (tok, LANES), 1)
            for j in range(g):
                span = slice(j * tok, (j + 1) * tok)
                column = jnp.broadcast_to(kb[j, 0:1, :], (LANES, tok)).T
                first, second, third = thirds(column)
                extra = jnp.where(
                    lane == 0, first,
                    jnp.where(lane == 1, second, jnp.where(lane == 2, third, 1.0)),
                )
                ka[span, :LANES] = k_s[pair, span, :]
                ka[span, LANES:] = jnp.where(lane < 6, extra, 0.0).astype(LOW)
                va[span, :LANES] = v_s[pair, span, :]
                va[span, LANES:] = jnp.where(lane < 3, 1.0, 0.0).astype(LOW)

        span = pl.ds(pl.multiple_of(block * rows, rows), rows)
        lane = lax.broadcasted_iota(jnp.int32, (rows, LANES), 1)
        queries = q_s[pair, span, :].astype(F32) * SCALE
        ones = jnp.where(lane < 3, 1.0, 0.0)
        outs = []
        for head in range(2):
            masked = jnp.where(head_mask(rows, head), queries, 0.0)
            wide = jnp.concatenate([masked, ones], 1).astype(LOW)
            scores = matmul_right(wide, ka[...])
            row_max = jnp.max(scores, -1, keepdims=True)
            expo = jnp.exp(scores - row_max).astype(LOW)
            both = matmul(expo, va[...])
            total = both[:, LANES : LANES + 1]
            outs.append(both[:, :LANES] / total)
            first, second, third = thirds(row_max + jnp.log(total))
            qx[pair, head, span, :] = jnp.where(
                lane == 3, -first,
                jnp.where(lane == 4, -second, jnp.where(lane == 5, -third, ones)),
            ).astype(LOW)
        ctx[pair, span, :] = jnp.where(head_mask(rows, 0), outs[0], outs[1]).astype(LOW)

        for p in range(pairs):
            for k in range(1, g):
                @pl.when(step == p * blocks + k * per - 1)
                def _(p=p, k=k):
                    ctx_copy(p, k, s).start()

            @pl.when(step == (p + 1) * blocks - 1)
            def _(p=p):
                ctx_keep(p).start()
        return carry

    lax.fori_loop(0, steps, attend, 0)
    last = [
        pltpu.make_async_copy(qx, qx_out, loc.at[12]),
        pltpu.make_async_copy(ctx, own_ctx, loc.at[13]),
    ]
    for copy in last:
        copy.start()
    for event in late:
        event()
    for k in range(1, g):
        kb_copy(k, s).wait_send()
    for k in range(1, ny):
        for part in range(3):
            y_copy(k, part, s).wait_send()
            f_copy(k, part, me.y_from(k)).wait_send()
    c_copy(s).wait_send()
    for k in range(1, nz):
        wz_copy(k, d).wait_send()
        slot = me.z_from(k)
        wx_copy(k, wch.at[slot], slot).wait_send()
    wx_copy(0, wch_ref, d).wait_send()
    for pair in range(pairs):
        ctx_keep(pair).wait()
        for k in range(1, g):
            ctx_copy(pair, k, me.s_from(k)).wait_recv()
            ctx_copy(pair, k, s).wait_send()
    for p in range(len(pieces)):
        piece_end(p)
    for copy in saves + last + keep:
        copy.wait()


def attend_forward(hidden, chunk, bias_rows, w_out, w_up, w_down):
    n, g = lax.axis_size("dp"), lax.axis_size("seq")
    tok, width = hidden.shape
    length, gw, deep = tok * g, width // g, width // n
    pairs = gw // LANES
    count = len(weight_pieces([w.shape[0] for w in (w_out, w_up, w_down)]))
    anyw = pl.BlockSpec(memory_space=pl.ANY)
    low = lambda *shape: jax.ShapeDtypeStruct(shape, LOW)
    out_shape = [
        low(tok, width), low(pairs, length, LANES), low(pairs, length, LANES),
        low(pairs, length, LANES), low(pairs, length, LANES), low(pairs, 2, length, LANES),
        low(g, tok, width), low(width, 3 * gw), low(n, 16, 3 * gw),
        low(n, *w_out.shape), low(n, *w_up.shape), low(n, *w_down.shape),
    ]
    dma = lambda *shape: pltpu.SemaphoreType.DMA(shape)
    nz, ny = n // 2, max(g // 2, 2)
    vmem = lambda shape, kind=LOW: pltpu.VMEM(shape, kind)
    return pl.pallas_call(
        functools.partial(forward_kernel, n=n, g=g, rows=256),
        in_specs=[anyw] * 6,
        out_specs=[anyw] * 12,
        out_shape=out_shape,
        scratch_shapes=[
            vmem((g, tok, width)), vmem((n, deep + 16, 3 * gw)), vmem((width, 3 * gw)),
            vmem((g, 8, tok), F32), vmem((pairs, length, LANES)), vmem((pairs, length, LANES)),
            vmem((pairs, length, LANES)), vmem((length, 2 * LANES)), vmem((length, 2 * LANES)),
            vmem((pairs, length, LANES)), vmem((pairs, 2, length, LANES)),
            dma(14), dma(2, ny, 3), dma(2), dma(2, ny, 3), dma(2, g), dma(2, nz), dma(2, nz),
            dma(2, count, nz), dma(2, count, nz), dma(2, count, nz, 2), dma(2, pairs, g),
            dma(pairs),
        ],
        compiler_params=pltpu.CompilerParams(
            vmem_limit_bytes=56 * 2**20, collective_id=0, has_side_effects=True
        ),
        cost_estimate=cost(length, 4),
    )(hidden, chunk, bias_rows, w_out, w_up, w_down)


def backward_kernel(
    q_ref, k_ref, v_ref, kt_ref, bias_ref, qx_ref, o_ref, do_ref,
    dq_ref, dk_ref, dv_ref, ka_ref, va_ref, dk_acc, dv_acc, *, chunk,
):
    step = pl.program_id(0)

    @pl.when(step == 0)
    def _():
        fill_keys(k_ref, v_ref, bias_ref, ka_ref, va_ref)
        dk_acc[...] = jnp.zeros_like(dk_acc)
        dv_acc[...] = jnp.zeros_like(dv_acc)

    rows = q_ref.shape[0]
    length = k_ref.shape[0]
    lane = lax.broadcasted_iota(jnp.int32, (rows, LANES), 1)
    queries = q_ref[...].astype(F32) * SCALE
    grads = do_ref[...].astype(F32)
    dots = grads * o_ref[...].astype(F32)
    q_wide, g_wide, q_mask, g_mask = [], [], [], []
    for head in range(2):
        mask = head_mask(rows, head)
        masked = jnp.where(mask, queries, 0.0).astype(LOW)
        g_masked = jnp.where(mask, grads, 0.0).astype(LOW)
        delta = jnp.sum(jnp.where(mask, dots, 0.0), -1, keepdims=True)
        first, second, third = thirds(delta)
        extra = jnp.where(
            lane == 0, -first, jnp.where(lane == 1, -second, jnp.where(lane == 2, -third, 0.0))
        ).astype(LOW)
        q_mask.append(masked)
        g_mask.append(g_masked)
        q_wide.append(jnp.concatenate([masked, qx_ref[head]], 1))
        g_wide.append(jnp.concatenate([g_masked, extra], 1))
    q_rows = jnp.concatenate(q_mask, 0)
    g_rows = jnp.concatenate(g_mask, 0)
    dq_t = [jnp.zeros((LANES, rows), F32) for _ in range(2)]
    for start in range(0, length, chunk):
        part = slice(start, start + chunk)
        p_list, ds_list = [], []
        for head in range(2):
            probs = jnp.exp(matmul_right(ka_ref[part, :], q_wide[head]))
            d_scores = (probs * matmul_right(va_ref[part, :], g_wide[head])).astype(LOW)
            p_list.append(probs.astype(LOW))
            ds_list.append(d_scores)
            dq_t[head] = dq_t[head] + matmul(kt_ref[:, part], d_scores)
        dv_acc[part, :] += matmul(jnp.concatenate(p_list, 1), g_rows)
        dk_acc[part, :] += matmul(jnp.concatenate(ds_list, 1), q_rows)
    row = lax.broadcasted_iota(jnp.int32, (LANES, rows), 0)
    both = jnp.where(row < HEAD_DIM, dq_t[0], dq_t[1]) * SCALE
    dq_ref[...] = both.T.astype(LOW)

    @pl.when(step == pl.num_programs(0) - 1)
    def _():
        dk_ref[...] = dk_acc[...].astype(LOW)
        dv_ref[...] = dv_acc[...].astype(LOW)


def cost(length, matmuls):
    return pl.CostEstimate(
        flops=2 * 2 * matmuls * length * length * 256,
        bytes_accessed=10 * length * LANES * 2,
        transcendentals=2 * length * length,
    )


def attend_backward(queries, keys, values, bias_wide, q_extra, context, context_grad):
    length = queries.shape[0]
    rows = 256
    chunk = 768 if length % 768 == 0 else 256
    tile = pl.BlockSpec((rows, LANES), lambda i: (i, 0))
    whole = pl.BlockSpec((length, LANES), lambda i: (0, 0))
    return pl.pallas_call(
        functools.partial(backward_kernel, chunk=chunk),
        grid=(length // rows,),
        in_specs=[
            tile, whole, whole, pl.BlockSpec((LANES, length), lambda i: (0, 0)), whole,
            pl.BlockSpec((2, rows, LANES), lambda i: (0, i, 0)), tile, tile,
        ],
        out_specs=[tile, whole, whole],
        out_shape=[jax.ShapeDtypeStruct((length, LANES), LOW)] * 3,
        scratch_shapes=[pltpu.VMEM((length, 2 * LANES), LOW)] * 2
        + [pltpu.VMEM((length, LANES), F32)] * 2,
        compiler_params=pltpu.CompilerParams(vmem_limit_bytes=48 * 2**20),
        cost_estimate=cost(length, 5),
    )(queries, keys, values, keys.T, bias_wide, q_extra, context, context_grad)


def swap(array, name, mask):
    return lax.ppermute(array, name, [(i, i ^ mask) for i in range(lax.axis_size(name))])


def bits(name):
    return lax.axis_size(name).bit_length() - 1


def bit_order(last):
    dp_bits = [("dp", k) for k in reversed(range(bits("dp")))]
    seq_bits = [("seq", k) for k in reversed(range(1, bits("seq")))]
    order = dp_bits + seq_bits
    if last in order:
        order.remove(last)
        order.append(last)
    return order + [("seq", 0)]


def place(name, k):
    return bits("dp") - 1 - k if name == "dp" else bits("dp") + bits("seq") - 1 - k


def my_bit(name, k):
    return (lax.axis_index(name) >> k) & 1


def double(array, name, k):
    other = swap(array, name, 1 << k)
    at = place(name, k)
    return jnp.where(
        my_bit(name, k) == 0,
        jnp.concatenate([array, other], at),
        jnp.concatenate([other, array], at),
    )


def reduce_weight(grad, last):
    count = bits("dp") + bits("seq")
    rows = grad.shape[0] >> count
    part = grad.astype(LOW).reshape((2,) * count + (rows, grad.shape[1]))
    for name, k in reversed(bit_order(last)):
        mine = my_bit(name, k)
        away = lax.dynamic_index_in_dim(part, 1 - mine, place(name, k))
        keep = lax.dynamic_index_in_dim(part, mine, place(name, k))
        part = (keep.astype(F32) + swap(away, name, 1 << k).astype(F32)).astype(LOW)
    for k in reversed(range(bits("seq"))):
        part = double(part, "seq", k)
    return part.reshape(-1, grad.shape[1]).astype(F32)


def scatter(part, name, order):
    tail = part.shape[1:]
    part = part.reshape((2,) * bits(name) + tail)
    for k in order:
        at = bits(name) - 1 - k
        mine = my_bit(name, k)
        away = lax.dynamic_index_in_dim(part, 1 - mine, at)
        keep = lax.dynamic_index_in_dim(part, mine, at)
        part = keep.astype(F32) + swap(away.astype(LOW), name, 1 << k).astype(F32)
    return part.reshape(tail)


def gather_seq(part):
    part = part.reshape((1,) * bits("seq") + part.shape)
    for k in reversed(range(bits("seq"))):
        other = swap(part, "seq", 1 << k)
        at = bits("seq") - 1 - k
        part = jnp.where(
            my_bit("seq", k) == 0,
            jnp.concatenate([part, other], at),
            jnp.concatenate([other, part], at),
        )
    return part.reshape((-1,) + part.shape[bits("seq"):])


def exchange(blocks):
    return [block if t == 0 else swap(block, "seq", t) for t, block in enumerate(blocks)]


def by_index(blocks):
    count = len(blocks)
    me = lax.axis_index("seq")
    return [lax.select_n(me, *[blocks[i ^ j] for i in range(count)]) for j in range(count)]


def columns(array, group, pair, group_width):
    return lax.dynamic_slice_in_dim(array, group * group_width + pair * LANES, LANES, 1)


def own_columns(piece, width, group_width):
    at = lax.axis_index("dp") * piece.shape[0]
    row = lax.dynamic_update_slice_in_dim(jnp.zeros((width,), LOW), piece, at, 0)
    return lax.dynamic_slice_in_dim(row, lax.axis_index("seq") * group_width, group_width, 0)


def local(
    hidden_in, key_bias, w_qkv, bias_q, bias_v, w_out, bias_out, gain_attn, shift_attn,
    w_up, bias_up, w_down, bias_down, gain_ffn, shift_ffn, grad_out,
):
    groups = lax.axis_size("seq")
    me = lax.axis_index("seq")
    tok_rows, width = hidden_in.shape
    group_width = width // groups
    pairs = group_width // LANES
    wide_y, wide_x, wide_z = ("seq", 1), ("dp", 0), ("dp", 1)
    deep = w_qkv.shape[0]

    vectors = (
        bias_q, bias_v, bias_out, gain_attn, shift_attn, bias_down, gain_ffn, shift_ffn, bias_up,
    )
    packed = jnp.concatenate(vectors)
    fill = -packed.shape[0] % (3 * group_width)
    packed = jnp.pad(packed, (0, fill)).reshape(-1, 3 * group_width)
    first_row = jnp.concatenate([
        own_columns(bias_q, width, group_width), jnp.zeros((group_width,), LOW),
        own_columns(bias_v, width, group_width),
    ])[None]
    own_w = jnp.concatenate(
        [lax.dynamic_slice_in_dim(w_qkv, i * width + me * group_width, group_width, 1) for i in range(3)], 1
    )
    blank = jnp.zeros((16 - 1 - packed.shape[0], 3 * group_width), LOW)
    chunk = jnp.concatenate([own_w, first_row, packed, blank], 0)
    bias_rows = jnp.broadcast_to(key_bias, (8, tok_rows))
    (context, own_context, q_all, k_all, v_all, q_extra, hidden_all, w_heads, vec_all, f_w_out,
     f_w_up, f_w_down) = attend_forward(hidden_in, chunk, bias_rows, w_out, w_up, w_down)
    f_w_out = f_w_out.reshape(-1, w_out.shape[1])
    f_w_up = f_w_up.reshape(-1, w_up.shape[1])
    f_w_down = f_w_down.reshape(-1, w_down.shape[1])
    hidden_all = hidden_all.reshape(-1, width)
    packed = vec_all[:, 1 : 1 + packed.shape[0]].reshape(vec_all.shape[0], -1).astype(F32)
    fulls, at = [], 0
    for vector in vectors:
        fulls.append(packed[:, at : at + vector.shape[0]].reshape(-1))
        at += vector.shape[0]
    (f_bias_q, f_bias_v, f_bias_out, f_gain_attn, f_shift_attn, f_bias_down, f_gain_ffn,
     f_shift_ffn, f_bias_up) = fulls
    bias_col = jnp.concatenate(by_index(exchange([key_bias[0]] * groups)))
    bias_wide = jnp.broadcast_to(bias_col[:, None], (bias_col.shape[0], LANES))

    attended = hidden_in.astype(F32) + matmul(context, f_w_out) + f_bias_out
    normed = layer_norm(attended, f_gain_attn, f_shift_attn)
    normed_low = normed.astype(LOW)
    pre_act = matmul(normed_low, f_w_up) + f_bias_up
    activ = gelu_exact(pre_act).astype(LOW)
    branch_sum = normed + matmul(activ, f_w_down) + f_bias_down
    output = layer_norm(branch_sum, f_gain_ffn, f_shift_ffn).astype(LOW)

    upstream = grad_out.astype(F32)
    _, norm_back = jax.vjp(layer_norm, branch_sum, f_gain_ffn, f_shift_ffn)
    d_branch, g_gain_ffn, g_shift_ffn = norm_back(upstream)
    g_bias_down = jnp.sum(d_branch, 0)
    d_branch_low = d_branch.astype(LOW)
    g_w_down = matmul_left(activ, d_branch_low).astype(LOW)
    d_activ = matmul_right(d_branch_low, f_w_down)
    _, gelu_back = jax.vjp(gelu_exact, pre_act)
    d_pre = gelu_back(d_activ)[0]
    g_bias_up = jnp.sum(d_pre, 0)
    d_pre_low = d_pre.astype(LOW)
    g_w_up = matmul_left(normed_low, d_pre_low).astype(LOW)
    d_normed = d_branch + matmul_right(d_pre_low, f_w_up)
    _, attn_norm_back = jax.vjp(layer_norm, attended, f_gain_attn, f_shift_attn)
    d_attended, g_gain_attn, g_shift_attn = attn_norm_back(d_normed)
    g_bias_out = jnp.sum(d_attended, 0)
    d_attended_low = d_attended.astype(LOW)
    g_w_out = matmul_left(context, d_attended_low).astype(LOW)
    d_context = matmul_right(d_attended_low, f_w_out).astype(LOW)
    d_context, g_w_down, g_w_up, g_w_out = lax.optimization_barrier(
        (d_context, g_w_down, g_w_up, g_w_out)
    )
    s_w_down = reduce_weight(g_w_down, wide_x)
    s_w_up = reduce_weight(g_w_up, wide_y)
    s_w_out = reduce_weight(g_w_out, wide_z)

    grads = [[], [], []]
    for pair in range(pairs):
        got = jnp.concatenate(by_index(exchange(
            [columns(d_context, me ^ t, pair, group_width) for t in range(groups)]
        )))
        done = attend_backward(
            q_all[pair], k_all[pair], v_all[pair], bias_wide, q_extra[pair], own_context[pair], got
        )
        for i in range(3):
            grads[i].append(done[i])
    d_heads = jnp.concatenate(grads[0] + grads[1] + grads[2], 1)
    d_in = matmul_right(d_heads, w_heads).astype(LOW).reshape(groups, tok_rows, width)
    grad_in = d_attended + scatter(d_in, "seq", range(bits("seq")))
    g_w_heads = matmul_left(hidden_all, d_heads).astype(LOW)
    s_w_heads = scatter(
        g_w_heads.reshape(-1, deep, 3 * group_width), "dp", range(bits("dp"))
    ).astype(LOW)
    s_w_qkv = gather_seq(s_w_heads).reshape(groups, deep, 3, group_width)
    s_w_qkv = s_w_qkv.transpose(1, 2, 0, 3).reshape(deep, -1).astype(F32)
    head_sums = jnp.sum(d_heads.astype(F32), 0)
    zero = jnp.zeros((width,), F32)
    g_bias_q = lax.dynamic_update_slice_in_dim(zero, head_sums[:group_width], me * group_width, 0)
    g_bias_v = lax.dynamic_update_slice_in_dim(
        zero, head_sums[2 * group_width :], me * group_width, 0
    )

    vector_grads = (
        g_bias_q, g_bias_v, g_bias_out, g_gain_attn, g_shift_attn, g_bias_down, g_gain_ffn,
        g_shift_ffn, g_bias_up,
    )
    shares = lax.axis_size("dp")
    rows = jnp.concatenate([g.reshape(shares, -1) for g in vector_grads], 1).astype(LOW)
    own = lax.dynamic_index_in_dim(
        lax.psum(rows, ("dp", "seq")), lax.axis_index("dp"), 0, False
    ).astype(F32)
    sums, at = [], 0
    for vector in vectors:
        sums.append(own[at : at + vector.shape[0]])
        at += vector.shape[0]
    (s_bias_q, s_bias_v, s_bias_out, s_gain_attn, s_shift_attn, s_bias_down, s_gain_ffn,
     s_shift_ffn, s_bias_up) = sums
    return (
        output, grad_in, s_w_qkv, s_bias_q, s_bias_v, s_w_out,
        s_bias_out, s_gain_attn, s_shift_attn, s_w_up, s_bias_up, s_w_down, s_bias_down,
        s_gain_ffn, s_shift_ffn,
    )


def solution(mesh):
    tokens = P(("dp", "seq"), None)
    matrix = P("dp", None)
    vector = P("dp")
    return jax.shard_map(
        local,
        mesh=mesh,
        in_specs=(
            tokens, P("dp", "seq"), matrix, vector, vector, matrix, vector, vector, vector,
            matrix, vector, matrix, vector, vector, vector, tokens,
        ),
        out_specs=(
            tokens, tokens, matrix, vector, vector, matrix, vector, vector, vector, matrix,
            vector, matrix, vector, vector, vector,
        ),
        check_vma=False,
    )
```

```python
import functools

import jax
import jax.numpy as jnp
from jax import lax
from jax.experimental import pallas as pl
from jax.experimental.pallas import tpu as pltpu
from jax.sharding import PartitionSpec as P

HEAD_DIM = 64
LANES = 128
SCALE = HEAD_DIM**-0.5
norm_eps = 1e-05
F32 = jnp.float32
LOW = jnp.bfloat16


def layer_norm(hidden, gain_vec, shift_vec):
    row_mean = jnp.mean(hidden, -1, keepdims=True)
    centered = hidden - row_mean
    row_var = jnp.mean(centered * centered, -1, keepdims=True)
    return centered * lax.rsqrt(row_var + norm_eps) * gain_vec + shift_vec


def gelu_exact(pre_act):
    return jax.nn.gelu(pre_act, approximate=False)


def matmul(left, right):
    return jnp.dot(left, right, preferred_element_type=F32)


def matmul_left(left, right):
    return lax.dot_general(left, right, (((0,), (0,)), ((), ())), preferred_element_type=F32)


def matmul_right(left, right):
    return lax.dot_general(left, right, (((1,), (1,)), ((), ())), preferred_element_type=F32)


def thirds(value):
    first = value.astype(LOW)
    rest = value - first.astype(F32)
    second = rest.astype(LOW)
    third = (rest - second.astype(F32)).astype(LOW)
    return first.astype(F32), second.astype(F32), third.astype(F32)


def head_mask(rows, head):
    lane = lax.broadcasted_iota(jnp.int32, (rows, LANES), 1)
    return (lane < HEAD_DIM) if head == 0 else (lane >= HEAD_DIM)


def send_to(src, dst, send_sem, recv_sem, dp, seq):
    return pltpu.make_async_remote_copy(
        src_ref=src, dst_ref=dst, send_sem=send_sem, recv_sem=recv_sem,
        device_id=(dp, seq), device_id_type=pl.DeviceIdType.MESH,
    )


class Peers:
    def __init__(self, n, g):
        self.n, self.g, self.nz, self.ny = n, g, n // 2, g // 2
        self.d = lax.axis_index("dp")
        self.s = lax.axis_index("seq")
        self.z, self.x = self.d // 2, lax.rem(self.d, 2)
        self.y, self.c = self.s // 2, lax.rem(self.s, 2)
        self.xpeer = self.z * 2 + 1 - self.x
        self.cpeer = self.y * 2 + 1 - self.c

    def z_to(self, k):
        return lax.rem(self.z + k, self.nz) * 2 + self.x

    def z_from(self, k):
        return lax.rem(self.z + self.nz - k, self.nz) * 2 + self.x

    def side(self, dp):
        return (dp // 2) * 2 + 1 - self.x

    def y_to(self, k):
        return lax.rem(self.s + 2 * k, self.g)

    def y_from(self, k):
        return lax.rem(self.s + self.g - 2 * k, self.g)

    def s_to(self, k):
        return lax.rem(self.s + k, self.g)

    def s_from(self, k):
        return lax.rem(self.s + self.g - k, self.g)

    def barrier(self):
        sem = pltpu.get_barrier_semaphore()
        targets = [(self.z_to(k), self.s) for k in range(1, self.nz)]
        targets.append((self.xpeer, self.s))
        targets += [(self.d, self.s_to(k)) for k in range(1, self.g)]
        for target in targets:
            pl.semaphore_signal(
                sem, inc=1, device_id=target, device_id_type=pl.DeviceIdType.MESH
            )
        pl.semaphore_wait(sem, len(targets))


def pieces_of(half):
    return 2 if half % 64 == 0 and half >= 64 else 1


def weight_pieces(shapes):
    out = []
    for index, rows in enumerate(shapes):
        half = rows // 2
        count = pieces_of(half) if index else 1
        for part in range(count):
            out.append((index, part * (half // count), half // count))
    return out


def forward_kernel(
    hid_ref, wch_ref, kb_ref, wo_ref, wu_ref, wd_ref,
    ctx_out, own_ctx, q_out, ka_out, v_out, qx_out, hid_out, wq_out, vec_out, wo_out, wu_out, wd_out,
    hid, wch, wq, kb, q_s, k_s, v_s, ka, va, ctx, qx,
    loc, hy, hc, hf, kbs, wz, wx, pz, px, pc, cs, kx,
    *, n, g, rows,
):
    me = Peers(n, g)
    d, s, nz, ny = me.d, me.s, me.nz, me.ny
    tok, width = hid_ref.shape
    length = tok * g
    deep = width // n
    gw = width // g
    pairs = gw // LANES
    cut = tok // 3
    shards = (wo_ref, wu_ref, wd_ref)
    fulls = (wo_out, wu_out, wd_out)
    pieces = weight_pieces([ref.shape[0] for ref in shards])
    me.barrier()

    local = [
        pltpu.make_async_copy(hid_ref, hid.at[s], loc.at[0]),
        pltpu.make_async_copy(wch_ref, wch.at[d], loc.at[1]),
        pltpu.make_async_copy(kb_ref, kb.at[s], loc.at[2]),
    ]
    keep = [
        pltpu.make_async_copy(shards[i], fulls[i].at[d], loc.at[3 + i]) for i in range(3)
    ]

    def y_copy(k, part, slot):
        span = pl.ds(part * cut, cut)
        return send_to(
            hid_ref.at[span], hid.at[slot, span], hy.at[0, k, part], hy.at[1, k, part], d,
            me.y_to(k),
        )

    def c_copy(slot):
        return send_to(hid_ref, hid.at[slot], hc.at[0], hc.at[1], d, me.cpeer)

    def f_copy(k, part, slot):
        span = pl.ds(part * cut, cut)
        return send_to(
            hid.at[slot, span], hid.at[slot, span], hf.at[0, k, part], hf.at[1, k, part], d,
            me.cpeer,
        )

    def kb_copy(k, slot):
        return send_to(kb_ref, kb.at[slot], kbs.at[0, k], kbs.at[1, k], d, me.s_to(k))

    def wz_copy(k, slot):
        return send_to(wch_ref, wch.at[slot], wz.at[0, k], wz.at[1, k], me.z_to(k), s)

    def wx_copy(k, src, slot):
        return send_to(src, wch.at[slot], wx.at[0, k], wx.at[1, k], me.xpeer, s)

    def c_of_y(k):
        return me.y_from(k) // 2 * 2 + 1 - me.c

    for copy in local:
        copy.start()
    for k in range(1, nz):
        wz_copy(k, d).start()
    wx_copy(0, wch_ref, d).start()
    for k in range(1, g):
        kb_copy(k, s).start()
    for part in range(3):
        for k in range(1, ny):
            y_copy(k, part, s).start()
    c_copy(s).start()
    for copy in keep:
        copy.start()

    def span_of(p):
        index, off, size = pieces[p]
        return index, pl.ds(pl.multiple_of(me.c * (shards[index].shape[0] // 2) + off, 16), size)

    def other_span(p):
        index, off, size = pieces[p]
        return index, pl.ds(
            pl.multiple_of((1 - me.c) * (shards[index].shape[0] // 2) + off, 16), size
        )

    def pz_copy(p, k, slot):
        index, span = span_of(p)
        return send_to(
            shards[index].at[span], fulls[index].at[slot, span], pz.at[0, p, k], pz.at[1, p, k],
            me.z_to(k), s,
        )

    def px_copy(p, k, slot):
        index, span = span_of(p)
        src = shards[index].at[span] if k == 0 else fulls[index].at[slot, span]
        return send_to(
            src, fulls[index].at[slot, span], px.at[0, p, k], px.at[1, p, k], me.xpeer, s
        )

    def pc_copy(p, k, side, slot, mine):
        index, span = span_of(p) if mine else other_span(p)
        return send_to(
            fulls[index].at[slot, span], fulls[index].at[slot, span], pc.at[0, p, k, side],
            pc.at[1, p, k, side], d, me.cpeer,
        )

    def piece_send(p):
        for k in range(1, nz):
            pz_copy(p, k, d).start()
        px_copy(p, 0, d).start()

    def piece_pass(p):
        for k in range(1, nz):
            slot = me.z_from(k)
            pz_copy(p, k, slot).wait_recv()
            px_copy(p, k, slot).start()
            pc_copy(p, k, 0, slot, True).start()

    def piece_share(p):
        for k in range(nz):
            slot = me.side(me.z_from(k)) if k else me.xpeer
            px_copy(p, k, slot).wait_recv()
            pc_copy(p, k, 1, slot, True).start()

    def piece_end(p):
        for k in range(1, nz):
            pc_copy(p, k, 0, me.z_from(k), False).wait_recv()
        for k in range(nz):
            pc_copy(p, k, 1, me.side(me.z_from(k)) if k else me.xpeer, False).wait_recv()
        for k in range(1, nz):
            pz_copy(p, k, d).wait_send()
            pc_copy(p, k, 0, me.z_from(k), True).wait_send()
        for k in range(nz):
            px_copy(p, k, me.z_from(k) if k else d).wait_send()
            pc_copy(p, k, 1, me.side(me.z_from(k)) if k else me.xpeer, True).wait_send()

    for k in range(1, nz):
        slot = me.z_from(k)
        wz_copy(k, slot).wait_recv()
        wx_copy(k, wch.at[slot], slot).start()
    for k in range(nz):
        slot = me.side(me.z_from(k)) if k else me.xpeer
        wx_copy(k, wch_ref, slot).wait_recv()
    for copy in local:
        copy.wait()
    piece_send(0)
    if len(pieces) > 1:
        piece_send(1)
    for j in range(n):
        wq[j * deep : (j + 1) * deep, :] = wch[j, :deep, :]
    bias_row = jnp.sum(wch[:, deep : deep + 16, :].astype(F32)[:, 0:1, :], 0)
    saves = [
        pltpu.make_async_copy(wq, wq_out, loc.at[6]),
        pltpu.make_async_copy(wch.at[:, pl.ds(deep, 16)], vec_out, loc.at[7]),
    ]
    for copy in saves:
        copy.start()

    tiles = tok // cut

    def project(step, carry):
        rel = step // tiles
        part = lax.rem(step, tiles)

        @pl.when(step == tiles)
        def _():
            c_copy(me.cpeer).wait_recv()

        for k in range(1, ny):
            @pl.when(step == 2 * k * tiles)
            def _(k=k):
                for sub in range(3):
                    y_copy(k, sub, me.y_from(k)).wait_recv()
                    f_copy(k, sub, me.y_from(k)).start()

            @pl.when(step == (2 * k + 1) * tiles)
            def _(k=k):
                for sub in range(3):
                    f_copy(k, sub, c_of_y(k)).wait_recv()

        y_at = lax.rem(me.y + ny - rel // 2, ny)
        c_at = lax.rem(me.c + rel, 2)
        slot = y_at * 2 + c_at
        got = matmul(hid[slot, pl.ds(part * cut, cut), :], wq[...]) + bias_row
        got = got.astype(LOW)
        span = pl.ds(pl.multiple_of(slot * tok + part * cut, cut), cut)
        for index, ref in enumerate((q_s, k_s, v_s)):
            for pair in range(pairs):
                at = index * gw + pair * LANES
                ref[pair, span, :] = got[:, at : at + LANES]
        return carry

    lax.fori_loop(0, g * tiles, project, 0)
    for k in range(1, g):
        kb_copy(k, me.s_from(k)).wait_recv()
    more = [
        pltpu.make_async_copy(hid, hid_out, loc.at[8]),
        pltpu.make_async_copy(q_s, q_out, loc.at[9]),
        pltpu.make_async_copy(v_s, v_out, loc.at[11]),
    ]
    for copy in more:
        copy.start()
    saves += more

    blocks = length // rows
    per = tok // rows
    steps = pairs * blocks

    def ctx_copy(pair, k, source):
        span = pl.ds(pl.multiple_of(me.s_to(k) * tok, tok), tok)
        return send_to(
            ctx.at[pair, span],
            ctx_out.at[:, pl.ds(pl.multiple_of(source * gw + pair * LANES, LANES), LANES)],
            cs.at[0, pair, k], cs.at[1, pair, k], d, me.s_to(k),
        )

    def ctx_keep(pair):
        return pltpu.make_async_copy(
            ctx.at[pair, pl.ds(pl.multiple_of(s * tok, tok), tok)],
            ctx_out.at[:, pl.ds(pl.multiple_of(s * gw + pair * LANES, LANES), LANES)],
            kx.at[pair],
        )

    def ka_keep(pair):
        return pltpu.make_async_copy(ka, ka_out.at[pair], loc.at[10])

    events = {}
    every = max(1, steps // (len(pieces) + 1))
    for p in range(len(pieces)):
        if p >= 2:
            events.setdefault((p - 2) * every, []).append(lambda p=p: piece_send(p))
        events.setdefault((p + 1) * every - 1, []).append(lambda p=p: piece_pass(p))
        events.setdefault((p + 1) * every + 1, []).append(lambda p=p: piece_share(p))
    late = [e for t in sorted(events) if t >= steps for e in events[t]]

    def attend(step, carry):
        pair = step // blocks
        turn = lax.rem(step, blocks)
        k_own = lax.rem(1 + turn // per, g)
        owner = lax.rem(s + k_own, g)
        block = owner * per + lax.rem(turn, per)
        for t in sorted(events):
            if t < steps:
                @pl.when(step == t)
                def _(t=t):
                    for event in events[t]:
                        event()

        @pl.when((turn == 0) & (step > 0))
        def _():
            ka_keep(pair - 1).wait()

        @pl.when(turn == 0)
        def _():
            lane = lax.broadcasted_iota(jnp.int32, (tok, LANES), 1)
            for j in range(g):
                span = slice(j * tok, (j + 1) * tok)
                column = jnp.broadcast_to(kb[j, 0:1, :], (LANES, tok)).T
                first, second, third = thirds(column)
                extra = jnp.where(
                    lane == 0, first,
                    jnp.where(lane == 1, second, jnp.where(lane == 2, third, 1.0)),
                )
                ka[span, :LANES] = k_s[pair, span, :]
                ka[span, LANES:] = jnp.where(lane < 6, extra, 0.0).astype(LOW)
                va[span, :LANES] = v_s[pair, span, :]
                va[span, LANES:] = jnp.where(lane < 3, 1.0, 0.0).astype(LOW)
            ka_keep(pair).start()

        span = pl.ds(pl.multiple_of(block * rows, rows), rows)
        lane = lax.broadcasted_iota(jnp.int32, (rows, LANES), 1)
        queries = q_s[pair, span, :].astype(F32) * SCALE
        ones = jnp.where(lane < 3, 1.0, 0.0)
        outs = []
        for head in range(2):
            masked = jnp.where(head_mask(rows, head), queries, 0.0)
            wide = jnp.concatenate([masked, ones], 1).astype(LOW)
            scores = matmul_right(wide, ka[...])
            row_max = jnp.max(scores, -1, keepdims=True)
            expo = jnp.exp(scores - row_max).astype(LOW)
            both = matmul(expo, va[...])
            total = both[:, LANES : LANES + 1]
            outs.append(both[:, :LANES] / total)
            first, second, third = thirds(row_max + jnp.log(total))
            qx[pair, head, span, :] = jnp.where(
                lane == 3, -first,
                jnp.where(lane == 4, -second, jnp.where(lane == 5, -third, ones)),
            ).astype(LOW)
        ctx[pair, span, :] = jnp.where(head_mask(rows, 0), outs[0], outs[1]).astype(LOW)

        for p in range(pairs):
            for k in range(1, g):
                @pl.when(step == p * blocks + k * per - 1)
                def _(p=p, k=k):
                    ctx_copy(p, k, s).start()

            @pl.when(step == (p + 1) * blocks - 1)
            def _(p=p):
                ctx_keep(p).start()
        return carry

    lax.fori_loop(0, steps, attend, 0)
    ka_keep(pairs - 1).wait()
    last = [
        pltpu.make_async_copy(qx, qx_out, loc.at[12]),
        pltpu.make_async_copy(ctx, own_ctx, loc.at[13]),
    ]
    for copy in last:
        copy.start()
    for event in late:
        event()
    for k in range(1, g):
        kb_copy(k, s).wait_send()
    for k in range(1, ny):
        for part in range(3):
            y_copy(k, part, s).wait_send()
            f_copy(k, part, me.y_from(k)).wait_send()
    c_copy(s).wait_send()
    for k in range(1, nz):
        wz_copy(k, d).wait_send()
        slot = me.z_from(k)
        wx_copy(k, wch.at[slot], slot).wait_send()
    wx_copy(0, wch_ref, d).wait_send()
    for pair in range(pairs):
        ctx_keep(pair).wait()
        for k in range(1, g):
            ctx_copy(pair, k, me.s_from(k)).wait_recv()
            ctx_copy(pair, k, s).wait_send()
    for p in range(len(pieces)):
        piece_end(p)
    for copy in saves + last + keep:
        copy.wait()


def attend_forward(hidden, chunk, bias_rows, w_out, w_up, w_down):
    n, g = lax.axis_size("dp"), lax.axis_size("seq")
    tok, width = hidden.shape
    length, gw, deep = tok * g, width // g, width // n
    pairs = gw // LANES
    count = len(weight_pieces([w.shape[0] for w in (w_out, w_up, w_down)]))
    anyw = pl.BlockSpec(memory_space=pl.ANY)
    low = lambda *shape: jax.ShapeDtypeStruct(shape, LOW)
    out_shape = [
        low(tok, width), low(pairs, length, LANES), low(pairs, length, LANES),
        low(pairs, length, 2 * LANES), low(pairs, length, LANES), low(pairs, 2, length, LANES),
        low(g, tok, width), low(width, 3 * gw), low(n, 16, 3 * gw),
        low(n, *w_out.shape), low(n, *w_up.shape), low(n, *w_down.shape),
    ]
    dma = lambda *shape: pltpu.SemaphoreType.DMA(shape)
    nz, ny = n // 2, max(g // 2, 2)
    vmem = lambda shape, kind=LOW: pltpu.VMEM(shape, kind)
    return pl.pallas_call(
        functools.partial(forward_kernel, n=n, g=g, rows=256),
        in_specs=[anyw] * 6,
        out_specs=[anyw] * 12,
        out_shape=out_shape,
        scratch_shapes=[
            vmem((g, tok, width)), vmem((n, deep + 16, 3 * gw)), vmem((width, 3 * gw)),
            vmem((g, 8, tok), F32), vmem((pairs, length, LANES)), vmem((pairs, length, LANES)),
            vmem((pairs, length, LANES)), vmem((length, 2 * LANES)), vmem((length, 2 * LANES)),
            vmem((pairs, length, LANES)), vmem((pairs, 2, length, LANES)),
            dma(14), dma(2, ny, 3), dma(2), dma(2, ny, 3), dma(2, g), dma(2, nz), dma(2, nz),
            dma(2, count, nz), dma(2, count, nz), dma(2, count, nz, 2), dma(2, pairs, g),
            dma(pairs),
        ],
        compiler_params=pltpu.CompilerParams(
            vmem_limit_bytes=56 * 2**20, collective_id=0, has_side_effects=True
        ),
        cost_estimate=cost(length, 4),
    )(hidden, chunk, bias_rows, w_out, w_up, w_down)


def piece_rows(n):
    return max(16, 512 // n)


def grad_pieces(shapes, n, wide):
    out = []
    for index, (rows, cols) in enumerate(shapes):
        half = rows // 2
        size = min(half, piece_rows(n))
        for off in range(0, half, size):
            for col in range(0, cols, wide):
                out.append((index, off, col))
    return out


def backward_kernel(
    dctx_ref, q_ref, ka_ref, v_ref, qx_ref, o_ref, hid_ref, wq_ref, vec_ref, go_ref, gu_ref,
    gd_ref,
    din_out, sum_out, sq_out, c_land, x_land,
    q_s, ka, va, kt, qx, o_s, do_s, dh, dk_acc, dv_acc, hid, wq, vec,
    part_c, part_k, part_y, part_b, din, own_b, c_b, s_b, x_b, t_b, z_b, u_b, y_b, f_b,
    q_b, xq, tq, zq, rq,
    loc, ld, sd, sk, sy, sc, sx, sz, sg, sf, sl, sxq, szq, sgq,
    *, n, g, rows, chunk,
):
    me = Peers(n, g)
    d, s, nz, ny = me.d, me.s, me.nz, me.ny
    tok, width = dctx_ref.shape
    length = tok * g
    deep = width // n
    gw = width // g
    pairs = gw // LANES
    grads = (go_ref, gu_ref, gd_ref)
    wide = own_b.shape[3]
    size = own_b.shape[2]
    pieces = grad_pieces([ref.shape[1:] for ref in grads], n, wide)
    count = len(pieces)
    blocks = length // rows
    per = tok // rows
    steps = pairs * blocks
    me.barrier()

    def dctx_copy(pair, k, slot):
        cols = pl.ds(pl.multiple_of(me.s_to(k) * gw + pair * LANES, LANES), LANES)
        return send_to(
            dctx_ref.at[:, cols], do_s.at[pair, pl.ds(pl.multiple_of(slot * tok, tok), tok)],
            sd.at[0, pair, k], sd.at[1, pair, k], d, me.s_to(k),
        )

    def dctx_own(pair):
        cols = pl.ds(pl.multiple_of(s * gw + pair * LANES, LANES), LANES)
        return pltpu.make_async_copy(
            dctx_ref.at[:, cols], do_s.at[pair, pl.ds(pl.multiple_of(s * tok, tok), tok)],
            sl.at[pair],
        )

    def pair_loads(pair):
        return [
            pltpu.make_async_copy(q_ref.at[pair], q_s, loc.at[0]),
            pltpu.make_async_copy(ka_ref.at[pair], ka, loc.at[1]),
            pltpu.make_async_copy(v_ref.at[pair], va.at[:, pl.ds(0, LANES)], loc.at[2]),
            pltpu.make_async_copy(qx_ref.at[pair], qx, loc.at[3]),
            pltpu.make_async_copy(o_ref.at[pair], o_s, loc.at[4]),
        ]

    tail_loads = [
        pltpu.make_async_copy(hid_ref, hid, loc.at[5]),
        pltpu.make_async_copy(wq_ref, wq, loc.at[6]),
        pltpu.make_async_copy(vec_ref, vec, loc.at[7]),
    ]

    def part_of(p, core):
        index, off, col = pieces[p]
        ref = grads[index]
        row = pl.multiple_of(core * (ref.shape[1] // 2) + off, 16)
        return ref.at[:, pl.ds(row, size), pl.ds(col, wide)]

    def core_copy(p):
        return send_to(
            part_of(p, 1 - me.c), c_land.at[p], sc.at[0, p], sc.at[1, p], d, me.cpeer
        )

    def core_landed(p):
        return send_to(
            c_land.at[p], c_land.at[p], sc.at[0, p], sc.at[1, p], d, me.cpeer
        )

    def own_load(p):
        return pltpu.make_async_copy(part_of(p, me.c), own_b.at[p % 2], ld.at[0, p % 2])

    def side_copy(p):
        slot = lax.rem(p, 3)
        return send_to(
            s_b.at[slot, pl.ds(0, nz)], x_land.at[p], sx.at[0, p], sx.at[1, p], me.xpeer, s
        )

    def line_copy(p, k):
        slot = lax.rem(p, 3)
        return send_to(
            t_b.at[slot, lax.rem(me.z + k, nz)], z_b.at[p, k], sz.at[0, p, k], sz.at[1, p, k],
            me.z_to(k), s,
        )

    def up_copy(p, k):
        return send_to(
            u_b.at[p], y_b.at[p, k], sy.at[0, p, k], sy.at[1, p, k], d, me.y_to(k)
        )

    def fin_copy(p):
        return send_to(
            f_b.at[p], sum_out.at[p, me.c], sf.at[0, p], sf.at[1, p], d, me.cpeer
        )

    def fin_landed(p):
        return send_to(
            f_b.at[p], sum_out.at[p, 1 - me.c], sf.at[0, p], sf.at[1, p], d, me.cpeer
        )

    def fin_keep(p):
        return pltpu.make_async_copy(f_b.at[p], sum_out.at[p, me.c], sg.at[p])

    def e2_load(p):
        own_load(p).start()
        core_landed(p).wait_recv()
        pltpu.make_async_copy(c_land.at[p], c_b.at[p % 2], ld.at[1, p % 2]).start()

    def e2(p):
        slot, two = lax.rem(p, 3), lax.rem(p, 2)
        pltpu.make_async_copy(c_land.at[p], own_b.at[two], ld.at[0, two]).wait()
        pltpu.make_async_copy(c_land.at[p], c_b.at[two], ld.at[1, two]).wait()

        @pl.when(p >= 3)
        def _():
            side_copy(p - 3).wait_send()

        def add(j, carry):
            for part in range(2):
                at = 2 * j + (1 - me.x if part == 0 else me.x)
                total = own_b[two, at].astype(F32) + c_b[two, at].astype(F32)
                s_b[slot, part * nz + j] = total.astype(LOW)
            return carry

        lax.fori_loop(0, nz, add, 0)
        side_copy(p).start()

    def e3(p):
        slot = lax.rem(p, 3)
        side_copy(p).wait_recv()
        load = pltpu.make_async_copy(x_land.at[p], x_b, loc.at[8])
        load.start()

        @pl.when(p >= 3)
        def _():
            for k in range(1, nz):
                line_copy(p - 3, k).wait_send()

        load.wait()

        def add(j, carry):
            total = s_b[slot, nz + j].astype(F32) + x_b[j].astype(F32)
            t_b[slot, j] = total.astype(LOW)
            return carry

        lax.fori_loop(0, nz, add, 0)
        for k in range(1, nz):
            line_copy(p, k).start()

    def e4(p):
        slot = lax.rem(p, 3)
        for k in range(1, nz):
            line_copy(p, k).wait_recv()
        total = t_b[slot, me.z].astype(F32)
        for k in range(1, nz):
            total = total + z_b[p, k].astype(F32)
        u_b[p] = total.astype(LOW)
        for k in range(1, ny):
            up_copy(p, k).start()

    def e5(p):
        for k in range(1, ny):
            up_copy(p, k).wait_recv()
        total = u_b[p].astype(F32)
        for k in range(1, ny):
            total = total + y_b[p, k].astype(F32)
        f_b[p] = total.astype(LOW)
        fin_copy(p).start()
        fin_keep(p).start()

    for pair in range(pairs):
        dctx_own(pair).start()
        for k in range(1, g):
            dctx_copy(pair, k, s).start()
    for copy in tail_loads:
        copy.start()
    for p in range(count):
        core_copy(p).start()
    lane_l = lax.broadcasted_iota(jnp.int32, (tok, LANES), 1)
    for j in range(g):
        va[j * tok : (j + 1) * tok, LANES:] = jnp.where(lane_l < 3, 1.0, 0.0).astype(LOW)

    def t2(p):
        return 2 * p + 2

    def t3(p):
        return (5 * p) // 2 + 6

    def attend(step, carry):
        pair = step // blocks
        turn = lax.rem(step, blocks)
        rel = turn // per
        owner = lax.rem(s + g - rel, g)
        block = owner * per + lax.rem(turn, per)

        @pl.when(turn == 0)
        def _():
            loads = pair_loads(pair)
            for copy in loads:
                copy.start()
            dk_acc[...] = jnp.zeros_like(dk_acc)
            dv_acc[...] = jnp.zeros_like(dv_acc)
            dctx_own(pair).wait()
            for copy in loads:
                copy.wait()
            for j in range(length // chunk):
                part = slice(j * chunk, (j + 1) * chunk)
                kt[:, part] = ka[part, :LANES].astype(F32).T.astype(LOW)

        for p in range(count):
            @pl.when(step == t2(p) - 1)
            def _(p=p):
                e2_load(p)

        for lag, event in ((0, e3), (3, e4), (5, e5)):
            at = step - 6 - lag
            p = (2 * jnp.maximum(at, 0) + 1) // 5
            p = jnp.where((5 * p) // 2 == at, p, p + 1)

            @pl.when((at >= 0) & ((5 * p) // 2 == at) & (p < count))
            def _(p=p, event=event):
                event(p)

        @pl.when((lax.rem(step, 2) == 0) & (step >= 2) & (step < t2(count)))
        def _():
            e2((step - 2) // 2)

        for k in range(1, g):
            @pl.when(turn == k * per)
            def _(k=k):
                dctx_copy(pair, k, me.s_from(k)).wait_recv()

        span = pl.ds(pl.multiple_of(block * rows, rows), rows)
        lane = lax.broadcasted_iota(jnp.int32, (rows, LANES), 1)
        queries = q_s[span, :].astype(F32) * SCALE
        upstream = do_s[pair, span, :].astype(F32)
        dots = upstream * o_s[span, :].astype(F32)
        q_wide, g_wide, q_mask, g_mask = [], [], [], []
        for head in range(2):
            mask = head_mask(rows, head)
            masked = jnp.where(mask, queries, 0.0).astype(LOW)
            g_masked = jnp.where(mask, upstream, 0.0).astype(LOW)
            delta = jnp.sum(jnp.where(mask, dots, 0.0), -1, keepdims=True)
            first, second, third = thirds(delta)
            extra = jnp.where(
                lane == 0, -first, jnp.where(lane == 1, -second, jnp.where(lane == 2, -third, 0.0))
            ).astype(LOW)
            q_mask.append(masked)
            g_mask.append(g_masked)
            q_wide.append(jnp.concatenate([masked, qx[head, span, :]], 1))
            g_wide.append(jnp.concatenate([g_masked, extra], 1))
        q_rows = jnp.concatenate(q_mask, 0)
        g_rows = jnp.concatenate(g_mask, 0)
        dq_t = [jnp.zeros((LANES, rows), F32) for _ in range(2)]
        for start in range(0, length, chunk):
            part = slice(start, start + chunk)
            p_list, ds_list = [], []
            for head in range(2):
                probs = jnp.exp(matmul_right(ka[part, :], q_wide[head]))
                d_scores = (probs * matmul_right(va[part, :], g_wide[head])).astype(LOW)
                p_list.append(probs.astype(LOW))
                ds_list.append(d_scores)
                dq_t[head] = dq_t[head] + matmul(kt[:, part], d_scores)
            dv_acc[part, :] += matmul(jnp.concatenate(p_list, 1), g_rows)
            dk_acc[part, :] += matmul(jnp.concatenate(ds_list, 1), q_rows)
        row = lax.broadcasted_iota(jnp.int32, (LANES, rows), 0)
        both = jnp.where(row < HEAD_DIM, dq_t[0], dq_t[1]) * SCALE
        dh[pair, span, :] = both.T.astype(LOW)

        @pl.when(turn == blocks - 1)
        def _():
            dh[pairs + pair] = dk_acc[...].astype(LOW)
            dh[2 * pairs + pair] = dv_acc[...].astype(LOW)
        return carry

    lax.fori_loop(0, steps, attend, 0)
    for copy in tail_loads:
        copy.wait()
    for p in range(count):
        if t2(p) >= steps:
            if t2(p) - 1 >= steps:
                e2_load(p)
            e2(p)

    def heads_of(slot, tile):
        span = pl.ds(pl.multiple_of(slot * tok + tile * rows, rows), rows)
        return jnp.concatenate([dh[i, span, :] for i in range(3 * pairs)], 1)

    def core_part(k):
        slot = lax.rem(me.y + k, ny) * 2 + 1 - me.c

        def tile_of(tile, carry):
            span = pl.ds(pl.multiple_of(tile * rows, rows), rows)
            part_c[k, span, :] = matmul_right(heads_of(slot, tile), wq[...]).astype(LOW)
            return carry

        lax.fori_loop(0, per, tile_of, 0)
        part_copy(k).start()

    def part_copy(k):
        return send_to(part_c.at[k], part_k.at[k], sk.at[0, k], sk.at[1, k], d, me.cpeer)

    def far_copy(k):
        return send_to(
            part_b.at[k - 1], part_y.at[k - 1], sgq.at[0, 0, k], sgq.at[1, 0, k], d, me.y_to(k)
        )

    for k in range(1, ny):
        core_part(k)
    core_part(0)
    for k in range(1, ny):
        part_copy(k).wait_recv()
        slot = lax.rem(me.y + k, ny) * 2 + me.c

        def far_tile(tile, carry, k=k, slot=slot):
            span = pl.ds(pl.multiple_of(tile * rows, rows), rows)
            total = matmul_right(heads_of(slot, tile), wq[...]) + part_k[k, span, :].astype(F32)
            part_b[k - 1, span, :] = total.astype(LOW)
            return carry

        lax.fori_loop(0, per, far_tile, 0)
        far_copy(k).start()

    sums = [jnp.zeros((1, LANES), F32) for _ in range(3 * pairs)]
    for i in range(3 * pairs):
        for j in range(g):
            span = slice(j * tok, (j + 1) * tok)
            sums[i] = sums[i] + jnp.sum(dh[i, span, :].astype(F32), 0, keepdims=True)
    sums = jnp.concatenate(sums, 1)
    row16 = lax.broadcasted_iota(jnp.int32, (16, 3 * gw), 0)
    for j in range(n):
        q_b[j, deep:, :] = (vec[j].astype(F32) + jnp.where(row16 == 0, sums, 0.0)).astype(LOW)

    def qx_copy(j):
        return send_to(
            q_b.at[2 * j + 1 - me.x], xq.at[j], sxq.at[0, j], sxq.at[1, j], me.xpeer, s
        )

    def qz_copy(k):
        return send_to(
            tq.at[lax.rem(me.z + k, nz)], zq.at[k], szq.at[0, k], szq.at[1, k], me.z_to(k), s
        )

    def q_out_copy(k, source):
        return send_to(rq, sq_out.at[source], sgq.at[0, 1, k], sgq.at[1, 1, k], d, me.s_to(k))

    tile_w = 256
    for base in range(0, width, tile_w):
        total = jnp.zeros((tile_w, 3 * gw), F32)
        for j in range(g):
            right = jnp.concatenate(
                [dh[i, j * tok : (j + 1) * tok, :] for i in range(3 * pairs)], 1
            )
            total = total + matmul_left(hid[j, :, base : base + tile_w], right)
        for at in range(0, tile_w, deep):
            q_b[(base + at) // deep, :deep, :] = total[at : at + deep, :].astype(LOW)
        for j in range(base // deep // 2, (base + tile_w) // deep // 2):
            qx_copy(j).start()
    remaining = count

    def own_tile(tile, carry):
        span = pl.ds(pl.multiple_of(tile * rows, rows), rows)
        din[span, :] = matmul_right(heads_of(s, tile), wq[...])
        return carry

    lax.fori_loop(0, per, own_tile, 0)

    for event, lag in ((e3, 0), (e4, 3), (e5, 5)):
        for p in range(remaining):
            if t3(p) + lag >= steps:
                event(p)

    for j in range(nz):
        qx_copy(j).wait_recv()
        kept = q_b[2 * j + me.x].astype(F32) + xq[j].astype(F32)
        tq[j] = kept.astype(LOW)
    for k in range(1, nz):
        qz_copy(k).start()
    part_copy(0).wait_recv()
    for k in range(1, nz):
        qz_copy(k).wait_recv()
    total = tq[me.z].astype(F32)
    for k in range(1, nz):
        total = total + zq[k].astype(F32)
    rq[...] = total.astype(LOW)
    for k in range(1, g):
        q_out_copy(k, s).start()
    keep_q = pltpu.make_async_copy(rq, sq_out.at[s], loc.at[9])
    keep_q.start()
    for k in range(1, ny):
        far_copy(k).wait_recv()

    def sum_tile(tile, carry):
        span = pl.ds(pl.multiple_of(tile * rows, rows), rows)
        total = din[span, :] + part_k[0, span, :].astype(F32)
        for k in range(1, ny):
            total = total + part_y[k - 1, span, :].astype(F32)
        din[span, :] = total
        return carry

    lax.fori_loop(0, per, sum_tile, 0)
    keep_d = pltpu.make_async_copy(din, din_out, loc.at[10])
    keep_d.start()

    for p in range(count):
        core_copy(p).wait_send()
        fin_landed(p).wait_recv()
        fin_copy(p).wait_send()
        fin_keep(p).wait()
        for k in range(1, ny):
            up_copy(p, k).wait_send()
        if p >= count - 3:
            side_copy(p).wait_send()
            for k in range(1, nz):
                line_copy(p, k).wait_send()
    for pair in range(pairs):
        for k in range(1, g):
            dctx_copy(pair, k, s).wait_send()
    for k in range(ny):
        part_copy(k).wait_send()
    for k in range(1, ny):
        far_copy(k).wait_send()
    for j in range(nz):
        qx_copy(j).wait_send()
    for k in range(1, nz):
        qz_copy(k).wait_send()
    for k in range(1, g):
        q_out_copy(k, me.s_from(k)).wait_recv()
        q_out_copy(k, s).wait_send()
    keep_q.wait()
    keep_d.wait()


def cost(length, matmuls):
    return pl.CostEstimate(
        flops=2 * 2 * matmuls * length * length * 256,
        bytes_accessed=10 * length * LANES * 2,
        transcendentals=2 * length * length,
    )


def attend_backward(d_context, queries, keys, values, q_extra, context, hidden, w_heads, vecs,
                    g_out, g_up, g_down):
    n, g = lax.axis_size("dp"), lax.axis_size("seq")
    tok, width = d_context.shape
    length, gw, deep = tok * g, width // g, width // n
    pairs = gw // LANES
    nz, ny = n // 2, max(g // 2, 2)
    wide = min(1024, width)
    size = piece_rows(n)
    shares = [g.reshape(n, -1, g.shape[1]) for g in (g_out, g_up, g_down)]
    count = len(grad_pieces([share.shape[1:] for share in shares], n, wide))
    anyw = pl.BlockSpec(memory_space=pl.ANY)
    low = lambda *shape: jax.ShapeDtypeStruct(shape, LOW)
    vmem = lambda *shape: pltpu.VMEM(shape, LOW)
    vmem32 = lambda *shape: pltpu.VMEM(shape, F32)
    dma = lambda *shape: pltpu.SemaphoreType.DMA(shape)
    chunk = 768 if length % 768 == 0 else 256
    tall = deep + 16
    return pl.pallas_call(
        functools.partial(backward_kernel, n=n, g=g, rows=256, chunk=chunk),
        in_specs=[anyw] * 12,
        out_specs=[anyw] * 5,
        out_shape=[
            jax.ShapeDtypeStruct((tok, width), F32), low(count, 2, size, wide),
            low(g, tall, 3 * gw), low(count, n, size, wide), low(count, nz, size, wide),
        ],
        scratch_shapes=[
            vmem(length, LANES), vmem(length, 2 * LANES), vmem(length, 2 * LANES),
            vmem(LANES, length), vmem(2, length, LANES), vmem(length, LANES),
            vmem(pairs, length, LANES), vmem(3 * pairs, length, LANES), vmem32(length, LANES),
            vmem32(length, LANES), vmem(g, tok, width), vmem(width, 3 * gw), vmem(n, 16, 3 * gw),
            vmem(ny, tok, width), vmem(ny, tok, width), vmem(ny - 1, tok, width),
            vmem(ny - 1, tok, width), vmem32(tok, width),
            vmem(2, n, size, wide), vmem(2, n, size, wide), vmem(3, n, size, wide),
            vmem(nz, size, wide), vmem(3, nz, size, wide), vmem(count, nz, size, wide),
            vmem(count, size, wide), vmem(count, ny, size, wide), vmem(count, size, wide),
            vmem(n, tall, 3 * gw), vmem(nz, tall, 3 * gw), vmem(nz, tall, 3 * gw),
            vmem(nz, tall, 3 * gw), vmem(tall, 3 * gw),
            dma(11), dma(2, 2), dma(2, pairs, g), dma(2, ny), dma(2, count, ny), dma(2, count),
            dma(2, count), dma(2, count, nz), dma(count), dma(2, count), dma(pairs), dma(2, nz),
            dma(2, nz), dma(2, 2, g),
        ],
        compiler_params=pltpu.CompilerParams(
            vmem_limit_bytes=63 * 2**20, collective_id=1, has_side_effects=True
        ),
        cost_estimate=cost(length, 10),
    )(d_context, queries, keys, values, q_extra, context, hidden, w_heads, vecs, *shares)


def gelu_parts(pre):
    size = jnp.abs(pre)
    t = 1.0 / (1.0 + (0.3275911 * 0.7071067811865476) * size)
    bell = jnp.exp(-0.5 * pre * pre)
    poly = t * (0.127414796 + t * (-0.142248368 + t * (
        0.7107068705 + t * (-0.7265760135 + t * 0.5307027145))))
    tail = poly * bell
    phi = jnp.where(pre >= 0, 1.0 - tail, tail)
    return phi, bell * 0.3989422804014327


def up_kernel(x_ref, wu_ref, bu_ref, wd_ref, act_ref, slope_ref, sum_ref):
    pre = matmul(x_ref[...], wu_ref[...]) + bu_ref[...]
    phi, density = gelu_parts(pre)
    activ = (pre * phi).astype(LOW)
    act_ref[...] = activ
    slope_ref[...] = (phi + pre * density).astype(LOW)
    part = matmul(activ, wd_ref[...])

    @pl.when(pl.program_id(0) == 0)
    def _():
        sum_ref[...] = part

    @pl.when(pl.program_id(0) > 0)
    def _():
        sum_ref[...] += part


def feed_forward(normed_low, w_up, bias_up, w_down):
    tok, width = normed_low.shape
    ff = w_up.shape[1]
    tile = 512
    whole = pl.BlockSpec((tok, width), lambda i: (0, 0))
    col = pl.BlockSpec((tok, tile), lambda i: (0, i))
    return pl.pallas_call(
        up_kernel,
        grid=(ff // tile,),
        in_specs=[
            whole, pl.BlockSpec((width, tile), lambda i: (0, i)),
            pl.BlockSpec((1, tile), lambda i: (0, i)), pl.BlockSpec((tile, width), lambda i: (i, 0)),
        ],
        out_specs=[col, col, whole],
        out_shape=[
            jax.ShapeDtypeStruct((tok, ff), LOW), jax.ShapeDtypeStruct((tok, ff), LOW),
            jax.ShapeDtypeStruct((tok, width), F32),
        ],
        compiler_params=pltpu.CompilerParams(vmem_limit_bytes=48 * 2**20),
    )(normed_low, w_up, bias_up[None], w_down)


def down_kernel(
    x_ref, e_ref, wu_ref, wd_ref, act_ref, slope_ref, gu_ref, gd_ref, gb_ref, sum_ref,
):
    up = e_ref[...]
    d_pre = matmul_right(up, wd_ref[...]) * slope_ref[...].astype(F32)
    gb_ref[...] = jnp.sum(d_pre, 0, keepdims=True)
    d_low = d_pre.astype(LOW)
    gd_ref[...] = matmul_left(act_ref[...], up).astype(LOW)
    gu_ref[...] = matmul_left(x_ref[...], d_low).astype(LOW)
    part = matmul_right(d_low, wu_ref[...])

    @pl.when(pl.program_id(0) == 0)
    def _():
        sum_ref[...] = part

    @pl.when(pl.program_id(0) > 0)
    def _():
        sum_ref[...] += part


def feed_backward(normed_low, d_low, w_up, w_down, activ, slope):
    tok, width = normed_low.shape
    ff = w_up.shape[1]
    tile = 512
    whole = pl.BlockSpec((tok, width), lambda i: (0, 0))
    col = pl.BlockSpec((tok, tile), lambda i: (0, i))
    up = pl.BlockSpec((width, tile), lambda i: (0, i))
    down = pl.BlockSpec((tile, width), lambda i: (i, 0))
    return pl.pallas_call(
        down_kernel,
        grid=(ff // tile,),
        in_specs=[whole, whole, up, down, col, col],
        out_specs=[up, down, pl.BlockSpec((1, tile), lambda i: (0, i)), whole],
        out_shape=[
            jax.ShapeDtypeStruct((width, ff), LOW), jax.ShapeDtypeStruct((ff, width), LOW),
            jax.ShapeDtypeStruct((1, ff), F32), jax.ShapeDtypeStruct((tok, width), F32),
        ],
        compiler_params=pltpu.CompilerParams(vmem_limit_bytes=48 * 2**20),
    )(normed_low, d_low, w_up, w_down, activ, slope)


def own_columns(piece, width, group_width):
    at = lax.axis_index("dp") * piece.shape[0]
    row = lax.dynamic_update_slice_in_dim(jnp.zeros((width,), LOW), piece, at, 0)
    return lax.dynamic_slice_in_dim(row, lax.axis_index("seq") * group_width, group_width, 0)


def local(
    hidden_in, key_bias, w_qkv, bias_q, bias_v, w_out, bias_out, gain_attn, shift_attn,
    w_up, bias_up, w_down, bias_down, gain_ffn, shift_ffn, grad_out,
):
    groups = lax.axis_size("seq")
    me = lax.axis_index("seq")
    tok_rows, width = hidden_in.shape
    group_width = width // groups
    deep = w_qkv.shape[0]
    shares = lax.axis_size("dp")

    vectors = (
        bias_q, bias_v, bias_out, gain_attn, shift_attn, bias_down, gain_ffn, shift_ffn, bias_up,
    )
    packed = jnp.concatenate(vectors)
    fill = -packed.shape[0] % (3 * group_width)
    packed = jnp.pad(packed, (0, fill)).reshape(-1, 3 * group_width)
    first_row = jnp.concatenate([
        own_columns(bias_q, width, group_width), jnp.zeros((group_width,), LOW),
        own_columns(bias_v, width, group_width),
    ])[None]
    own_w = jnp.concatenate(
        [lax.dynamic_slice_in_dim(w_qkv, i * width + me * group_width, group_width, 1) for i in range(3)], 1
    )
    blank = jnp.zeros((16 - 1 - packed.shape[0], 3 * group_width), LOW)
    chunk = jnp.concatenate([own_w, first_row, packed, blank], 0)
    bias_rows = jnp.broadcast_to(key_bias, (8, tok_rows))
    (context, own_context, q_all, ka_all, v_all, q_extra, hidden_all, w_heads, vec_all, f_w_out,
     f_w_up, f_w_down) = attend_forward(hidden_in, chunk, bias_rows, w_out, w_up, w_down)
    f_w_out = f_w_out.reshape(-1, w_out.shape[1])
    f_w_up = f_w_up.reshape(-1, w_up.shape[1])
    f_w_down = f_w_down.reshape(-1, w_down.shape[1])
    packed = vec_all[:, 1 : 1 + packed.shape[0]].reshape(vec_all.shape[0], -1).astype(F32)
    fulls, at = [], 0
    for vector in vectors:
        fulls.append(packed[:, at : at + vector.shape[0]].reshape(-1))
        at += vector.shape[0]
    (f_bias_q, f_bias_v, f_bias_out, f_gain_attn, f_shift_attn, f_bias_down, f_gain_ffn,
     f_shift_ffn, f_bias_up) = fulls

    attended = hidden_in.astype(F32) + matmul(context, f_w_out) + f_bias_out
    normed = layer_norm(attended, f_gain_attn, f_shift_attn)
    normed_low = normed.astype(LOW)
    activ, slope, branch = feed_forward(normed_low, f_w_up, f_bias_up, f_w_down)
    branch_sum = normed + branch + f_bias_down
    output = layer_norm(branch_sum, f_gain_ffn, f_shift_ffn).astype(LOW)

    upstream = grad_out.astype(F32)
    _, norm_back = jax.vjp(layer_norm, branch_sum, f_gain_ffn, f_shift_ffn)
    d_branch, g_gain_ffn, g_shift_ffn = norm_back(upstream)
    g_bias_down = jnp.sum(d_branch, 0)
    d_branch_low = d_branch.astype(LOW)
    g_w_up, g_w_down, g_bias_up, d_up = feed_backward(
        normed_low, d_branch_low, f_w_up, f_w_down, activ, slope
    )
    d_normed = d_branch + d_up
    _, attn_norm_back = jax.vjp(layer_norm, attended, f_gain_attn, f_shift_attn)
    d_attended, g_gain_attn, g_shift_attn = attn_norm_back(d_normed)
    g_bias_out = jnp.sum(d_attended, 0)
    d_attended_low = d_attended.astype(LOW)
    g_w_out = matmul_left(context, d_attended_low).astype(LOW)
    d_context = matmul_right(d_attended_low, f_w_out).astype(LOW)

    vector_grads = (
        g_bias_out, g_gain_attn, g_shift_attn, g_bias_down, g_gain_ffn, g_shift_ffn, g_bias_up,
    )
    rows = jnp.concatenate([g.reshape(shares, -1) for g in vector_grads], 1).astype(LOW)
    filled = rows.shape[1]
    tall = -(-filled // (3 * group_width))
    vecs = jnp.pad(rows, ((0, 0), (0, tall * 3 * group_width - filled)))
    vecs = jnp.pad(vecs.reshape(shares, tall, -1), ((0, 0), (1, 15 - tall), (0, 0)))
    d_in, sums, heads, _, _ = attend_backward(
        d_context, q_all, ka_all, v_all, q_extra, own_context, hidden_all, w_heads, vecs,
        g_w_out, g_w_up, g_w_down,
    )
    grad_in = d_attended + d_in
    own_sums = []
    wide, size = sums.shape[3], sums.shape[2]
    pieces = grad_pieces([w.shape for w in (w_out, w_up, w_down)], shares, wide)
    for index, w in enumerate((w_out, w_up, w_down)):
        mine = [p for p, piece in enumerate(pieces) if piece[0] == index]
        part = sums[mine[0] : mine[-1] + 1].reshape(
            -1, w.shape[1] // wide, 2, size, wide
        )
        own_sums.append(part.transpose(2, 0, 3, 1, 4).reshape(w.shape).astype(F32))
    s_w_out, s_w_up, s_w_down = own_sums
    s_w_qkv = heads[:, :deep].reshape(groups, deep, 3, group_width)
    s_w_qkv = s_w_qkv.transpose(1, 2, 0, 3).reshape(deep, -1).astype(F32)
    head_rows = heads[:, deep].astype(F32)
    at = lax.axis_index("dp") * bias_q.shape[0]
    s_bias_q = lax.dynamic_slice_in_dim(
        head_rows[:, :group_width].reshape(-1), at, bias_q.shape[0], 0
    )
    s_bias_v = lax.dynamic_slice_in_dim(
        head_rows[:, 2 * group_width :].reshape(-1), at, bias_v.shape[0], 0
    )
    own = jnp.sum(heads[:, deep + 1 : deep + 1 + tall].astype(F32), 0).reshape(-1)
    own_vectors, at = [], 0
    for vector in vectors[2:]:
        own_vectors.append(own[at : at + vector.shape[0]])
        at += vector.shape[0]
    (s_bias_out, s_gain_attn, s_shift_attn, s_bias_down, s_gain_ffn, s_shift_ffn,
     s_bias_up) = own_vectors
    return (
        output, grad_in, s_w_qkv, s_bias_q, s_bias_v, s_w_out, s_bias_out, s_gain_attn,
        s_shift_attn, s_w_up, s_bias_up, s_w_down, s_bias_down, s_gain_ffn, s_shift_ffn,
    )


def solution(mesh):
    tokens = P(("dp", "seq"), None)
    matrix = P("dp", None)
    vector = P("dp")
    return jax.shard_map(
        local,
        mesh=mesh,
        in_specs=(
            tokens, P("dp", "seq"), matrix, vector, vector, matrix, vector, vector, vector,
            matrix, vector, matrix, vector, vector, vector, tokens,
        ),
        out_specs=(
            tokens, tokens, matrix, vector, vector, matrix, vector, vector, vector, matrix,
            vector, matrix, vector, vector, vector,
        ),
        check_vma=False,
    )
```

```python
import functools

import jax
import jax.numpy as jnp
from jax import lax
from jax.experimental import pallas as pl
from jax.experimental.pallas import tpu as pltpu
from jax.sharding import PartitionSpec as P

HEAD_DIM = 64
LANES = 128
SCALE = HEAD_DIM**-0.5
norm_eps = 1e-05
PIECE_GAP = 3.5
F32 = jnp.float32
LOW = jnp.bfloat16


def layer_norm(hidden, gain_vec, shift_vec):
    row_mean = jnp.mean(hidden, -1, keepdims=True)
    centered = hidden - row_mean
    row_var = jnp.mean(centered * centered, -1, keepdims=True)
    return centered * lax.rsqrt(row_var + norm_eps) * gain_vec + shift_vec


def gelu_exact(pre_act):
    return jax.nn.gelu(pre_act, approximate=False)


def matmul(left, right):
    return jnp.dot(left, right, preferred_element_type=F32)


def matmul_left(left, right):
    return lax.dot_general(left, right, (((0,), (0,)), ((), ())), preferred_element_type=F32)


def matmul_right(left, right):
    return lax.dot_general(left, right, (((1,), (1,)), ((), ())), preferred_element_type=F32)


def thirds(value):
    first = value.astype(LOW)
    rest = value - first.astype(F32)
    second = rest.astype(LOW)
    third = (rest - second.astype(F32)).astype(LOW)
    return first.astype(F32), second.astype(F32), third.astype(F32)


def head_mask(rows, head):
    lane = lax.broadcasted_iota(jnp.int32, (rows, LANES), 1)
    return (lane < HEAD_DIM) if head == 0 else (lane >= HEAD_DIM)


def send_to(src, dst, send_sem, recv_sem, dp, seq):
    return pltpu.make_async_remote_copy(
        src_ref=src, dst_ref=dst, send_sem=send_sem, recv_sem=recv_sem,
        device_id=(dp, seq), device_id_type=pl.DeviceIdType.MESH,
    )


class Peers:
    def __init__(self, n, g):
        self.n, self.g, self.nz, self.ny = n, g, n // 2, g // 2
        self.d = lax.axis_index("dp")
        self.s = lax.axis_index("seq")
        self.z, self.x = self.d // 2, lax.rem(self.d, 2)
        self.y, self.c = self.s // 2, lax.rem(self.s, 2)
        self.xpeer = self.z * 2 + 1 - self.x
        self.cpeer = self.y * 2 + 1 - self.c

    def z_to(self, k):
        return lax.rem(self.z + k, self.nz) * 2 + self.x

    def z_from(self, k):
        return lax.rem(self.z + self.nz - k, self.nz) * 2 + self.x

    def side(self, dp):
        return (dp // 2) * 2 + 1 - self.x

    def y_to(self, k):
        return lax.rem(self.s + 2 * k, self.g)

    def y_from(self, k):
        return lax.rem(self.s + self.g - 2 * k, self.g)

    def s_to(self, k):
        return lax.rem(self.s + k, self.g)

    def s_from(self, k):
        return lax.rem(self.s + self.g - k, self.g)

    def barrier(self):
        sem = pltpu.get_barrier_semaphore()
        targets = [(self.z_to(k), self.s) for k in range(1, self.nz)]
        targets.append((self.xpeer, self.s))
        targets += [(self.d, self.s_to(k)) for k in range(1, self.g)]
        for target in targets:
            pl.semaphore_signal(
                sem, inc=1, device_id=target, device_id_type=pl.DeviceIdType.MESH
            )
        pl.semaphore_wait(sem, len(targets))


def weight_pieces(shapes, g):
    out = []
    for index, (rows, cols) in enumerate(shapes):
        quarter = rows % (16 * g) == 0 and index == 2
        own = rows // g if quarter else rows // 2
        size = min(own, max(16, 65536 // cols))
        for off in range(0, own, size):
            out.append((index, off, size, own, quarter))
    return sorted(out, key=lambda piece: not piece[4])


def forward_kernel(
    hid_ref, wch_ref, kb_ref, wo_ref, wu_ref, wd_ref,
    ctx_out, own_ctx, q_out, ka_out, v_out, qx_out, hid_out, wq_out, vec_out, wo_out, wu_out, wd_out,
    hid, wch, wq, kb, q_s, k_s, v_s, ka, va, ctx, qx,
    loc, hy, hc, hf, kbs, wz, wx, pz, px, pc, py, pf, cs, kx,
    *, n, g, rows,
):
    me = Peers(n, g)
    d, s, nz, ny = me.d, me.s, me.nz, me.ny
    tok, width = hid_ref.shape
    length = tok * g
    deep = width // n
    gw = width // g
    pairs = gw // LANES
    cut = tok // 3
    shards = (wo_ref, wu_ref, wd_ref)
    fulls = (wo_out, wu_out, wd_out)
    pieces = weight_pieces([ref.shape for ref in shards], g)
    me.barrier()

    local = [
        pltpu.make_async_copy(hid_ref, hid.at[s], loc.at[0]),
        pltpu.make_async_copy(wch_ref, wch.at[d], loc.at[1]),
        pltpu.make_async_copy(kb_ref, kb.at[s], loc.at[2]),
    ]
    keep = [
        pltpu.make_async_copy(shards[i], fulls[i].at[d], loc.at[3 + i]) for i in range(3)
    ]

    def y_copy(k, part, slot):
        span = pl.ds(part * cut, cut)
        return send_to(
            hid_ref.at[span], hid.at[slot, span], hy.at[0, k, part], hy.at[1, k, part], d,
            me.y_to(k),
        )

    def c_copy(slot):
        return send_to(hid_ref, hid.at[slot], hc.at[0], hc.at[1], d, me.cpeer)

    def f_copy(k, part, slot):
        span = pl.ds(part * cut, cut)
        return send_to(
            hid.at[slot, span], hid.at[slot, span], hf.at[0, k, part], hf.at[1, k, part], d,
            me.cpeer,
        )

    def kb_copy(k, slot):
        return send_to(kb_ref, kb.at[slot], kbs.at[0, k], kbs.at[1, k], d, me.s_to(k))

    def wz_copy(k, slot):
        return send_to(wch_ref, wch.at[slot], wz.at[0, k], wz.at[1, k], me.z_to(k), s)

    def wx_copy(k, src, slot):
        return send_to(src, wch.at[slot], wx.at[0, k], wx.at[1, k], me.xpeer, s)

    def c_of_y(k):
        return me.y_from(k) // 2 * 2 + 1 - me.c

    for copy in local:
        copy.start()
    for k in range(1, nz):
        wz_copy(k, d).start()
    wx_copy(0, wch_ref, d).start()
    for k in range(1, g):
        kb_copy(k, s).start()
    for part in range(3):
        for k in range(1, ny):
            y_copy(k, part, s).start()
    c_copy(s).start()
    for copy in keep:
        copy.start()

    def span_of(p, seq):
        index, off, size, own, quarter = pieces[p]
        part = seq if quarter else lax.rem(seq, 2)
        return index, pl.ds(pl.multiple_of(part * own + off, 16), size)

    def block_of(k, side):
        slot = me.z_from(k) if k else d
        if side:
            slot = me.side(slot)
        return slot

    def pz_copy(p, k, slot):
        index, span = span_of(p, s)
        return send_to(
            shards[index].at[span], fulls[index].at[slot, span], pz.at[0, p, k], pz.at[1, p, k],
            me.z_to(k), s,
        )

    def px_copy(p, k, slot):
        index, span = span_of(p, s)
        src = shards[index].at[span] if k == 0 else fulls[index].at[slot, span]
        return send_to(
            src, fulls[index].at[slot, span], px.at[0, p, k], px.at[1, p, k], me.xpeer, s
        )

    def pc_copy(p, k, side, seq):
        index, span = span_of(p, seq)
        ref = fulls[index].at[block_of(k, side), span]
        return send_to(
            ref, ref, pc.at[0, p, k, side], pc.at[1, p, k, side], d, me.cpeer
        )

    def py_copy(p, j, k, side, seq):
        index, span = span_of(p, seq)
        ref = fulls[index].at[block_of(k, side), span]
        return send_to(
            ref, ref, py.at[0, p, j, k, side], py.at[1, p, j, k, side], d, me.y_to(j)
        )

    def pf_copy(p, j, k, side, seq):
        index, span = span_of(p, seq)
        ref = fulls[index].at[block_of(k, side), span]
        return send_to(
            ref, ref, pf.at[0, p, j, k, side], pf.at[1, p, j, k, side], d, me.cpeer
        )

    moves = [(k, 0) for k in range(1, nz)] + [(k, 1) for k in range(nz)]

    def spread(p, k, side):
        if pieces[p][4]:
            for j in range(1, ny):
                py_copy(p, j, k, side, s).start()
        pc_copy(p, k, side, s).start()

    def piece_send(p):
        for k in range(1, nz):
            pz_copy(p, k, d).start()
        px_copy(p, 0, d).start()

    def piece_pass(p):
        for k in range(1, nz):
            slot = me.z_from(k)
            pz_copy(p, k, slot).wait_recv()
            px_copy(p, k, slot).start()
            spread(p, k, 0)

    def piece_share(p):
        for k in range(nz):
            px_copy(p, k, block_of(k, 1)).wait_recv()
            spread(p, k, 1)

    def piece_far(p):
        if pieces[p][4]:
            for j in range(1, ny):
                for k, side in moves:
                    py_copy(p, j, k, side, me.y_from(j)).wait_recv()
                    pf_copy(p, j, k, side, me.y_from(j)).start()

    def piece_end(p):
        for k, side in moves:
            pc_copy(p, k, side, me.cpeer).wait_recv()
            pc_copy(p, k, side, s).wait_send()
            if pieces[p][4]:
                for j in range(1, ny):
                    pf_copy(p, j, k, side, c_of_y(j)).wait_recv()
                    pf_copy(p, j, k, side, me.y_from(j)).wait_send()
                    py_copy(p, j, k, side, s).wait_send()
        for k in range(1, nz):
            pz_copy(p, k, d).wait_send()
        for k in range(nz):
            px_copy(p, k, block_of(k, 0)).wait_send()

    for k in range(1, nz):
        slot = me.z_from(k)
        wz_copy(k, slot).wait_recv()
        wx_copy(k, wch.at[slot], slot).start()
    for k in range(nz):
        slot = me.side(me.z_from(k)) if k else me.xpeer
        wx_copy(k, wch_ref, slot).wait_recv()
    for copy in local:
        copy.wait()
    piece_send(0)
    if len(pieces) > 1:
        piece_send(1)
    for j in range(n):
        wq[j * deep : (j + 1) * deep, :] = wch[j, :deep, :]
    bias_row = jnp.sum(wch[:, deep : deep + 16, :].astype(F32)[:, 0:1, :], 0)
    saves = [
        pltpu.make_async_copy(wq, wq_out, loc.at[6]),
        pltpu.make_async_copy(wch.at[:, pl.ds(deep, 16)], vec_out, loc.at[7]),
    ]
    for copy in saves:
        copy.start()

    tiles = tok // cut

    def project(step, carry):
        rel = step // tiles
        part = lax.rem(step, tiles)

        @pl.when(step == tiles)
        def _():
            c_copy(me.cpeer).wait_recv()

        for k in range(1, ny):
            @pl.when(step == 2 * k * tiles)
            def _(k=k):
                if k == 1 and len(pieces) > 2:
                    piece_send(2)
                for sub in range(3):
                    y_copy(k, sub, me.y_from(k)).wait_recv()
                    f_copy(k, sub, me.y_from(k)).start()

            @pl.when(step == (2 * k + 1) * tiles)
            def _(k=k):
                for sub in range(3):
                    f_copy(k, sub, c_of_y(k)).wait_recv()

        y_at = lax.rem(me.y + ny - rel // 2, ny)
        c_at = lax.rem(me.c + rel, 2)
        slot = y_at * 2 + c_at
        got = matmul(hid[slot, pl.ds(part * cut, cut), :], wq[...]) + bias_row
        got = got.astype(LOW)
        span = pl.ds(pl.multiple_of(slot * tok + part * cut, cut), cut)
        for index, ref in enumerate((q_s, k_s, v_s)):
            for pair in range(pairs):
                at = index * gw + pair * LANES
                ref[pair, span, :] = got[:, at : at + LANES]
        return carry

    lax.fori_loop(0, g * tiles, project, 0)
    for k in range(1, g):
        kb_copy(k, me.s_from(k)).wait_recv()
    more = [
        pltpu.make_async_copy(hid, hid_out, loc.at[8]),
        pltpu.make_async_copy(q_s, q_out, loc.at[9]),
        pltpu.make_async_copy(v_s, v_out, loc.at[11]),
    ]
    for copy in more:
        copy.start()
    saves += more

    blocks = length // rows
    per = tok // rows
    steps = pairs * blocks

    def ctx_copy(pair, k, source):
        span = pl.ds(pl.multiple_of(me.s_to(k) * tok, tok), tok)
        return send_to(
            ctx.at[pair, span],
            ctx_out.at[:, pl.ds(pl.multiple_of(source * gw + pair * LANES, LANES), LANES)],
            cs.at[0, pair, k], cs.at[1, pair, k], d, me.s_to(k),
        )

    def ctx_keep(pair):
        return pltpu.make_async_copy(
            ctx.at[pair, pl.ds(pl.multiple_of(s * tok, tok), tok)],
            ctx_out.at[:, pl.ds(pl.multiple_of(s * gw + pair * LANES, LANES), LANES)],
            kx.at[pair],
        )

    def ka_keep(pair):
        return pltpu.make_async_copy(ka, ka_out.at[pair], loc.at[10])

    events = {}
    gap = PIECE_GAP
    for p in range(len(pieces)):
        if p >= 3:
            events.setdefault(int(gap * (p - 3)), []).append(lambda p=p: piece_send(p))
        at = int(max(0, gap * (p - 1) + 1))
        events.setdefault(at, []).append(lambda p=p: piece_pass(p))
        events.setdefault(at + 3, []).append(lambda p=p: piece_share(p))
        events.setdefault(at + 7, []).append(lambda p=p: piece_far(p))
    late = [e for t in sorted(events) if t >= steps for e in events[t]]

    def attend(step, carry):
        pair = step // blocks
        turn = lax.rem(step, blocks)
        k_own = lax.rem(1 + turn // per, g)
        owner = lax.rem(s + k_own, g)
        block = owner * per + lax.rem(turn, per)
        for t in sorted(events):
            if t < steps:
                @pl.when(step == t)
                def _(t=t):
                    for event in events[t]:
                        event()

        @pl.when((turn == 0) & (step > 0))
        def _():
            ka_keep(pair - 1).wait()

        @pl.when(turn == 0)
        def _():
            lane = lax.broadcasted_iota(jnp.int32, (tok, LANES), 1)
            for j in range(g):
                span = slice(j * tok, (j + 1) * tok)
                column = jnp.broadcast_to(kb[j, 0:1, :], (LANES, tok)).T
                first, second, third = thirds(column)
                extra = jnp.where(
                    lane == 0, first,
                    jnp.where(lane == 1, second, jnp.where(lane == 2, third, 1.0)),
                )
                ka[span, :LANES] = k_s[pair, span, :]
                ka[span, LANES:] = jnp.where(lane < 6, extra, 0.0).astype(LOW)
                va[span, :LANES] = v_s[pair, span, :]
                va[span, LANES:] = jnp.where(lane < 3, 1.0, 0.0).astype(LOW)
            ka_keep(pair).start()

        span = pl.ds(pl.multiple_of(block * rows, rows), rows)
        lane = lax.broadcasted_iota(jnp.int32, (rows, LANES), 1)
        queries = q_s[pair, span, :].astype(F32) * SCALE
        ones = jnp.where(lane < 3, 1.0, 0.0)
        outs = []
        for head in range(2):
            masked = jnp.where(head_mask(rows, head), queries, 0.0)
            wide = jnp.concatenate([masked, ones], 1).astype(LOW)
            scores = matmul_right(wide, ka[...])
            row_max = jnp.max(scores, -1, keepdims=True)
            expo = jnp.exp(scores - row_max).astype(LOW)
            both = matmul(expo, va[...])
            total = both[:, LANES : LANES + 1]
            outs.append(both[:, :LANES] / total)
            first, second, third = thirds(row_max + jnp.log(total))
            qx[pair, head, span, :] = jnp.where(
                lane == 3, -first,
                jnp.where(lane == 4, -second, jnp.where(lane == 5, -third, ones)),
            ).astype(LOW)
        ctx[pair, span, :] = jnp.where(head_mask(rows, 0), outs[0], outs[1]).astype(LOW)

        for p in range(pairs):
            for k in range(1, g):
                @pl.when(step == p * blocks + k * per - 1)
                def _(p=p, k=k):
                    ctx_copy(p, k, s).start()

            @pl.when(step == (p + 1) * blocks - 1)
            def _(p=p):
                ctx_keep(p).start()
        return carry

    lax.fori_loop(0, steps, attend, 0)
    ka_keep(pairs - 1).wait()
    last = [
        pltpu.make_async_copy(qx, qx_out, loc.at[12]),
        pltpu.make_async_copy(ctx, own_ctx, loc.at[13]),
    ]
    for copy in last:
        copy.start()
    for event in late:
        event()
    for k in range(1, g):
        kb_copy(k, s).wait_send()
    for k in range(1, ny):
        for part in range(3):
            y_copy(k, part, s).wait_send()
            f_copy(k, part, me.y_from(k)).wait_send()
    c_copy(s).wait_send()
    for k in range(1, nz):
        wz_copy(k, d).wait_send()
        slot = me.z_from(k)
        wx_copy(k, wch.at[slot], slot).wait_send()
    wx_copy(0, wch_ref, d).wait_send()
    for pair in range(pairs):
        ctx_keep(pair).wait()
        for k in range(1, g):
            ctx_copy(pair, k, me.s_from(k)).wait_recv()
            ctx_copy(pair, k, s).wait_send()
    for p in range(len(pieces)):
        piece_end(p)
    for copy in saves + last + keep:
        copy.wait()


def attend_forward(hidden, chunk, bias_rows, w_out, w_up, w_down):
    n, g = lax.axis_size("dp"), lax.axis_size("seq")
    tok, width = hidden.shape
    length, gw, deep = tok * g, width // g, width // n
    pairs = gw // LANES
    count = len(weight_pieces([w.shape for w in (w_out, w_up, w_down)], g))
    anyw = pl.BlockSpec(memory_space=pl.ANY)
    low = lambda *shape: jax.ShapeDtypeStruct(shape, LOW)
    out_shape = [
        low(tok, width), low(pairs, length, LANES), low(pairs, length, LANES),
        low(pairs, length, 2 * LANES), low(pairs, length, LANES), low(pairs, 2, length, LANES),
        low(g, tok, width), low(width, 3 * gw), low(n, 16, 3 * gw),
        low(n, *w_out.shape), low(n, *w_up.shape), low(n, *w_down.shape),
    ]
    dma = lambda *shape: pltpu.SemaphoreType.DMA(shape)
    nz, ny = n // 2, max(g // 2, 2)
    vmem = lambda shape, kind=LOW: pltpu.VMEM(shape, kind)
    return pl.pallas_call(
        functools.partial(forward_kernel, n=n, g=g, rows=256),
        in_specs=[anyw] * 6,
        out_specs=[anyw] * 12,
        out_shape=out_shape,
        scratch_shapes=[
            vmem((g, tok, width)), vmem((n, deep + 16, 3 * gw)), vmem((width, 3 * gw)),
            vmem((g, 8, tok), F32), vmem((pairs, length, LANES)), vmem((pairs, length, LANES)),
            vmem((pairs, length, LANES)), vmem((length, 2 * LANES)), vmem((length, 2 * LANES)),
            vmem((pairs, length, LANES)), vmem((pairs, 2, length, LANES)),
            dma(14), dma(2, ny, 3), dma(2), dma(2, ny, 3), dma(2, g), dma(2, nz), dma(2, nz),
            dma(2, count, nz), dma(2, count, nz), dma(2, count, nz, 2),
            dma(2, count, ny, nz, 2), dma(2, count, ny, nz, 2), dma(2, pairs, g), dma(pairs),
        ],
        compiler_params=pltpu.CompilerParams(
            vmem_limit_bytes=56 * 2**20, collective_id=0, has_side_effects=True
        ),
        cost_estimate=cost(length, 4),
    )(hidden, chunk, bias_rows, w_out, w_up, w_down)


def piece_rows(n):
    return max(16, 512 // n)


def grad_pieces(shapes, n, g, wide):
    halves, quarters = [], []
    for index, (rows, cols) in enumerate(shapes):
        quarter = rows % (16 * g) == 0 and index == 2
        own = rows // g if quarter else rows // 2
        size = min(own, piece_rows(n))
        for off in range(0, own, size):
            for col in range(0, cols, wide):
                (quarters if quarter else halves).append((index, off, col, quarter))
    out = halves[:3]
    rest = halves[3:]
    for piece in quarters:
        out.append(piece)
        out += rest[:1]
        rest = rest[1:]
    return out + rest


def grad_times(pieces):
    times, lines, x_free, z_free = [], [], 0.0, 0.0
    y_free = 5.0
    at = 2
    for piece in pieces:
        first = None
        if piece[3]:
            first = 3 if not lines else lines[-1] + 2
            lines.append(first)
            y_free = max(y_free, first) + 5.0
            at = max(at, int(y_free) + 1)
        start = max(at, int(x_free - 1.0))
        x_free = max(x_free, start) + 2.5
        side = int(x_free + 0.9)
        z_free = max(z_free, side) + 2.5
        line = int(z_free + 0.9)
        times.append((first, start, side, line, line + 2))
        at = start + 2
    return times


def backward_kernel(
    dctx_ref, q_ref, ka_ref, v_ref, qx_ref, o_ref, hid_ref, wq_ref, vec_ref, go_ref, gu_ref,
    gd_ref,
    din_out, so_out, su_out, sd_out, sq_out, extra_out, c_land, x_land,
    q_s, ka, va, kt, qx, o_s, do_s, dh, dk_acc, dv_acc, hid, wq, vec,
    part_c, part_k, part_y, part_b, din, own_b, c_b, s_b, x_b, t_b, z_b, u_b, y_b, f_b,
    q_b, xq, tq, zq, rq, far_b, far_l,
    loc, ld, sd, sk, sy, sc, sx, sz, sg, sf, sl, sxq, szq, sgq, sfar, sfr,
    *, n, g, rows, chunk,
):
    me = Peers(n, g)
    d, s, nz, ny = me.d, me.s, me.nz, me.ny
    tok, width = dctx_ref.shape
    length = tok * g
    deep = width // n
    gw = width // g
    pairs = gw // LANES
    grads = (go_ref, gu_ref, gd_ref)
    wide = own_b.shape[3]
    size = own_b.shape[2]
    outs = (so_out, su_out, sd_out)
    pieces = grad_pieces([ref.shape[1:] for ref in grads], n, g, wide)
    times = grad_times(pieces)
    count = len(pieces)
    lands, spots = [], {}
    for p, piece in enumerate(pieces):
        for r in range(ny if piece[3] else 1):
            spots[p, r] = len(lands)
            lands.append((p, r))
    fars = [p for p in range(count) if pieces[p][3]]
    blocks = length // rows
    per = tok // rows
    steps = pairs * blocks
    me.barrier()

    def dctx_copy(pair, k, slot):
        cols = pl.ds(pl.multiple_of(me.s_to(k) * gw + pair * LANES, LANES), LANES)
        return send_to(
            dctx_ref.at[:, cols], do_s.at[pair, pl.ds(pl.multiple_of(slot * tok, tok), tok)],
            sd.at[0, pair, k], sd.at[1, pair, k], d, me.s_to(k),
        )

    def dctx_own(pair):
        cols = pl.ds(pl.multiple_of(s * gw + pair * LANES, LANES), LANES)
        return pltpu.make_async_copy(
            dctx_ref.at[:, cols], do_s.at[pair, pl.ds(pl.multiple_of(s * tok, tok), tok)],
            sl.at[pair],
        )

    def pair_loads(pair):
        return [
            pltpu.make_async_copy(q_ref.at[pair], q_s, loc.at[0]),
            pltpu.make_async_copy(ka_ref.at[pair], ka, loc.at[1]),
            pltpu.make_async_copy(v_ref.at[pair], va.at[:, pl.ds(0, LANES)], loc.at[2]),
            pltpu.make_async_copy(qx_ref.at[pair], qx, loc.at[3]),
            pltpu.make_async_copy(o_ref.at[pair], o_s, loc.at[4]),
        ]

    tail_loads = [
        pltpu.make_async_copy(hid_ref, hid, loc.at[5]),
        pltpu.make_async_copy(wq_ref, wq, loc.at[6]),
        pltpu.make_async_copy(vec_ref, vec, loc.at[7]),
    ]

    def row_of(p, core, y_at):
        index, off, col, quarter = pieces[p]
        own = grads[index].shape[1] // 2
        at = core * own + off
        if quarter:
            at = at + y_at * (own // ny)
        return pl.multiple_of(at, 16)

    def part_of(p, r, core):
        index, off, col, quarter = pieces[p]
        row = row_of(p, core, lax.rem(me.y + r, ny))
        return grads[index].at[:, pl.ds(row, size), pl.ds(col, wide)]

    def core_copy(p, r):
        i = spots[p, r]
        return send_to(
            part_of(p, r, 1 - me.c), c_land.at[i], sc.at[0, i], sc.at[1, i], d, me.cpeer
        )

    def own_load(p, r):
        i = spots[p, r] % 2
        return pltpu.make_async_copy(part_of(p, r, me.c), own_b.at[i], ld.at[0, i])

    def core_load(p, r):
        i = spots[p, r] % 2
        return pltpu.make_async_copy(c_land.at[spots[p, r]], c_b.at[i], ld.at[1, i])

    def y_copy(p, r):
        i = fars.index(p)
        return send_to(
            far_b.at[i], far_l.at[i, r - 1], sfar.at[0, i, r], sfar.at[1, i, r], d, me.y_to(r)
        )

    def side_copy(p):
        return send_to(
            s_b.at[p % 3, pl.ds(0, nz)], x_land.at[p], sx.at[0, p], sx.at[1, p], me.xpeer, s
        )

    def line_copy(p, k):
        return send_to(
            t_b.at[p % 3, lax.rem(me.z + k, nz)], z_b.at[p, k - 1], sz.at[0, p, k], sz.at[1, p, k],
            me.z_to(k), s,
        )

    def up_copy(p, k):
        return send_to(
            u_b.at[p], y_b.at[p, k], sy.at[0, p, k], sy.at[1, p, k], d, me.y_to(k)
        )

    def done_at(p, seq):
        index, off, col, quarter = pieces[p]
        row = row_of(p, lax.rem(seq, 2), seq // 2)
        return outs[index].at[pl.ds(row, size), pl.ds(col, wide)]

    def fin_hops(p):
        return range(1, g) if pieces[p][3] else (0,)

    def fin_copy(p, k, seq):
        to = me.s_to(k) if k else me.cpeer
        return send_to(f_b.at[p], done_at(p, seq), sf.at[0, p, k], sf.at[1, p, k], d, to)

    def fin_keep(p):
        return pltpu.make_async_copy(f_b.at[p], done_at(p, s), sg.at[p])

    def load(p, r):
        own_load(p, r).start()
        core_copy(p, r).wait_recv()
        core_load(p, r).start()

    def far_sum(p):
        for r in range(1, ny):
            i = spots[p, r] % 2
            own_load(p, r).wait()
            core_load(p, r).wait()

            def add(j, carry, i=i):
                total = own_b[i, j].astype(F32) + c_b[i, j].astype(F32)
                far_b[fars.index(p), j] = total.astype(LOW)
                return carry

            lax.fori_loop(0, n, add, 0)
            y_copy(p, r).start()

    def e2(p):
        slot, i = p % 3, spots[p, 0] % 2
        own_load(p, 0).wait()
        core_load(p, 0).wait()
        if pieces[p][3]:
            for r in range(1, ny):
                y_copy(p, r).wait_recv()
        if p >= 3:
            side_copy(p - 3).wait_send()

        def add(j, carry):
            for part in range(2):
                at = 2 * j + (1 - me.x if part == 0 else me.x)
                total = own_b[i, at].astype(F32) + c_b[i, at].astype(F32)
                if pieces[p][3]:
                    for r in range(1, ny):
                        total = total + far_l[fars.index(p), r - 1, at].astype(F32)
                s_b[slot, part * nz + j] = total.astype(LOW)
            return carry

        lax.fori_loop(0, nz, add, 0)
        side_copy(p).start()

    def e3(p):
        slot = p % 3
        side_copy(p).wait_recv()
        get = pltpu.make_async_copy(x_land.at[p], x_b, loc.at[8])
        get.start()
        if p >= 3:
            for k in range(1, nz):
                line_copy(p - 3, k).wait_send()
        get.wait()

        def add(j, carry):
            total = s_b[slot, nz + j].astype(F32) + x_b[j].astype(F32)
            t_b[slot, j] = total.astype(LOW)
            return carry

        lax.fori_loop(0, nz, add, 0)
        for k in range(1, nz):
            line_copy(p, k).start()

    def finish(p):
        for k in fin_hops(p):
            fin_copy(p, k, s).start()
        fin_keep(p).start()

    def e4(p):
        slot = p % 3
        for k in range(1, nz):
            line_copy(p, k).wait_recv()
        total = t_b[slot, me.z].astype(F32)
        for k in range(1, nz):
            total = total + z_b[p, k - 1].astype(F32)
        if pieces[p][3]:
            f_b[p] = total.astype(LOW)
            finish(p)
        else:
            u_b[p] = total.astype(LOW)
            for k in range(1, ny):
                up_copy(p, k).start()

    def e5(p):
        if pieces[p][3]:
            return
        for k in range(1, ny):
            up_copy(p, k).wait_recv()
        total = u_b[p].astype(F32)
        for k in range(1, ny):
            total = total + y_b[p, k].astype(F32)
        f_b[p] = total.astype(LOW)
        finish(p)

    plan = []
    for p in range(count):
        first, start, side, line, end = times[p]
        if first is not None:
            for r in range(1, ny):
                plan.append((first - 1, 5, lambda p=p, r=r: load(p, r)))
            plan.append((first, 4, lambda p=p: far_sum(p)))
        plan.append((start - 1, 5, lambda p=p: load(p, 0)))
        plan.append((start, 3, lambda p=p: e2(p)))
        plan.append((side, 2, lambda p=p: e3(p)))
        plan.append((line, 1, lambda p=p: e4(p)))
        plan.append((end, 0, lambda p=p: e5(p)))
    plan.sort(key=lambda item: item[:2])

    for pair in range(pairs):
        dctx_own(pair).start()
        for k in range(1, g):
            dctx_copy(pair, k, s).start()
    for copy in tail_loads:
        copy.start()
    for p, r in sorted(lands, key=lambda i: times[i[0]][1] if i[1] == 0 else times[i[0]][0]):
        core_copy(p, r).start()
    lane_l = lax.broadcasted_iota(jnp.int32, (tok, LANES), 1)
    for j in range(g):
        va[j * tok : (j + 1) * tok, LANES:] = jnp.where(lane_l < 3, 1.0, 0.0).astype(LOW)

    def attend(step, carry):
        pair = step // blocks
        turn = lax.rem(step, blocks)
        rel = turn // per
        owner = lax.rem(s + g - rel, g)
        block = owner * per + lax.rem(turn, per)

        @pl.when(turn == 0)
        def _():
            loads = pair_loads(pair)
            for copy in loads:
                copy.start()
            dk_acc[...] = jnp.zeros_like(dk_acc)
            dv_acc[...] = jnp.zeros_like(dv_acc)
            dctx_own(pair).wait()
            for copy in loads:
                copy.wait()
            for j in range(length // chunk):
                part = slice(j * chunk, (j + 1) * chunk)
                kt[:, part] = ka[part, :LANES].astype(F32).T.astype(LOW)

        for t in sorted({item[0] for item in plan}):
            if t < steps:
                @pl.when(step == t)
                def _(t=t):
                    for at, order, event in plan:
                        if at == t:
                            event()

        for k in range(1, g):
            @pl.when(turn == k * per)
            def _(k=k):
                dctx_copy(pair, k, me.s_from(k)).wait_recv()

        span = pl.ds(pl.multiple_of(block * rows, rows), rows)
        lane = lax.broadcasted_iota(jnp.int32, (rows, LANES), 1)
        queries = q_s[span, :].astype(F32) * SCALE
        upstream = do_s[pair, span, :].astype(F32)
        dots = upstream * o_s[span, :].astype(F32)
        q_wide, g_wide, q_mask, g_mask = [], [], [], []
        for head in range(2):
            mask = head_mask(rows, head)
            masked = jnp.where(mask, queries, 0.0).astype(LOW)
            g_masked = jnp.where(mask, upstream, 0.0).astype(LOW)
            delta = jnp.sum(jnp.where(mask, dots, 0.0), -1, keepdims=True)
            first, second, third = thirds(delta)
            extra = jnp.where(
                lane == 0, -first, jnp.where(lane == 1, -second, jnp.where(lane == 2, -third, 0.0))
            ).astype(LOW)
            q_mask.append(masked)
            g_mask.append(g_masked)
            q_wide.append(jnp.concatenate([masked, qx[head, span, :]], 1))
            g_wide.append(jnp.concatenate([g_masked, extra], 1))
        q_rows = jnp.concatenate(q_mask, 0)
        g_rows = jnp.concatenate(g_mask, 0)
        dq_t = [jnp.zeros((LANES, rows), F32) for _ in range(2)]
        for start in range(0, length, chunk):
            part = slice(start, start + chunk)
            p_list, ds_list = [], []
            for head in range(2):
                probs = jnp.exp(matmul_right(ka[part, :], q_wide[head]))
                d_scores = (probs * matmul_right(va[part, :], g_wide[head])).astype(LOW)
                p_list.append(probs.astype(LOW))
                ds_list.append(d_scores)
                dq_t[head] = dq_t[head] + matmul(kt[:, part], d_scores)
            dv_acc[part, :] += matmul(jnp.concatenate(p_list, 1), g_rows)
            dk_acc[part, :] += matmul(jnp.concatenate(ds_list, 1), q_rows)
        row = lax.broadcasted_iota(jnp.int32, (LANES, rows), 0)
        both = jnp.where(row < HEAD_DIM, dq_t[0], dq_t[1]) * SCALE
        dh[pair, span, :] = both.T.astype(LOW)

        @pl.when(turn == blocks - 1)
        def _():
            dh[pairs + pair] = dk_acc[...].astype(LOW)
            dh[2 * pairs + pair] = dv_acc[...].astype(LOW)
        return carry

    lax.fori_loop(0, steps, attend, 0)
    for copy in tail_loads:
        copy.wait()
    for at, order, event in plan:
        if at >= steps and order in (3, 4, 5):
            event()

    def heads_of(slot, tile):
        span = pl.ds(pl.multiple_of(slot * tok + tile * rows, rows), rows)
        return jnp.concatenate([dh[i, span, :] for i in range(3 * pairs)], 1)

    def part_copy(k, tile):
        span = pl.ds(pl.multiple_of(tile * rows, rows), rows)
        return send_to(
            part_c.at[k, span], part_k.at[k, span], sk.at[0, k, tile], sk.at[1, k, tile], d,
            me.cpeer,
        )

    def far_copy(k, tile):
        span = pl.ds(pl.multiple_of(tile * rows, rows), rows)
        return send_to(
            part_b.at[k - 1, span], part_y.at[k - 1, span], sfr.at[0, k, tile], sfr.at[1, k, tile],
            d, me.y_to(k),
        )

    def core_part(k):
        slot = lax.rem(me.y + k, ny) * 2 + 1 - me.c

        def tile_of(tile, carry):
            span = pl.ds(pl.multiple_of(tile * rows, rows), rows)
            part_c[k, span, :] = matmul_right(heads_of(slot, tile), wq[...]).astype(LOW)
            part_copy(k, tile).start()
            return carry

        lax.fori_loop(0, per, tile_of, 0)

    for k in range(1, ny):
        core_part(k)
    for k in range(1, ny):
        slot = lax.rem(me.y + k, ny) * 2 + me.c

        def far_tile(tile, carry, k=k, slot=slot):
            span = pl.ds(pl.multiple_of(tile * rows, rows), rows)
            total = matmul_right(heads_of(slot, tile), wq[...])
            part_copy(k, tile).wait_recv()
            total = total + part_k[k, span, :].astype(F32)
            part_b[k - 1, span, :] = total.astype(LOW)
            far_copy(k, tile).start()
            return carry

        lax.fori_loop(0, per, far_tile, 0)

    sums = [jnp.zeros((1, LANES), F32) for _ in range(3 * pairs)]
    for i in range(3 * pairs):
        for j in range(g):
            span = slice(j * tok, (j + 1) * tok)
            sums[i] = sums[i] + jnp.sum(dh[i, span, :].astype(F32), 0, keepdims=True)
    sums = jnp.concatenate(sums, 1)
    row16 = lax.broadcasted_iota(jnp.int32, (16, 3 * gw), 0)
    for j in range(n):
        q_b[j, deep:, :] = (vec[j].astype(F32) + jnp.where(row16 == 0, sums, 0.0)).astype(LOW)

    def qx_copy(j):
        return send_to(
            q_b.at[2 * j + 1 - me.x], xq.at[j], sxq.at[0, j], sxq.at[1, j], me.xpeer, s
        )

    def qz_copy(k):
        return send_to(
            tq.at[lax.rem(me.z + k, nz)], zq.at[k], szq.at[0, k], szq.at[1, k], me.z_to(k), s
        )

    def q_parts(source):
        parts = [(rq.at[pl.ds(deep, 16)], extra_out.at[source])]
        for i in range(3):
            at = pl.ds(pl.multiple_of(i * width + source * gw, LANES), gw)
            parts.append((rq.at[pl.ds(0, deep), pl.ds(i * gw, gw)], sq_out.at[:, at]))
        return parts

    def q_out_copies(k, source):
        return [
            send_to(src, dst, sgq.at[0, i, k], sgq.at[1, i, k], d, me.s_to(k))
            for i, (src, dst) in enumerate(q_parts(source))
        ]

    tile_w = 256
    for base in range(0, width, tile_w):
        total = jnp.zeros((tile_w, 3 * gw), F32)
        for j in range(g):
            right = jnp.concatenate(
                [dh[i, j * tok : (j + 1) * tok, :] for i in range(3 * pairs)], 1
            )
            total = total + matmul_left(hid[j, :, base : base + tile_w], right)
        for at in range(0, tile_w, deep):
            q_b[(base + at) // deep, :deep, :] = total[at : at + deep, :].astype(LOW)
        for j in range(base // deep // 2, (base + tile_w) // deep // 2):
            qx_copy(j).start()
    core_part(0)

    def own_tile(tile, carry):
        span = pl.ds(pl.multiple_of(tile * rows, rows), rows)
        din[span, :] = matmul_right(heads_of(s, tile), wq[...])
        return carry

    lax.fori_loop(0, per, own_tile, 0)

    for at, order, event in plan:
        if at >= steps and order in (0, 1, 2):
            event()

    for j in range(nz):
        qx_copy(j).wait_recv()
        kept = q_b[2 * j + me.x].astype(F32) + xq[j].astype(F32)
        tq[j] = kept.astype(LOW)
    for k in range(1, nz):
        qz_copy(k).start()
    for k in range(1, nz):
        qz_copy(k).wait_recv()
    total = tq[me.z].astype(F32)
    for k in range(1, nz):
        total = total + zq[k].astype(F32)
    rq[...] = total.astype(LOW)
    for k in range(1, g):
        for copy in q_out_copies(k, s):
            copy.start()
    keep_q = [
        pltpu.make_async_copy(src, dst, loc.at[11 + i])
        for i, (src, dst) in enumerate(q_parts(s))
    ]
    for copy in keep_q:
        copy.start()

    def sum_tile(tile, carry):
        span = pl.ds(pl.multiple_of(tile * rows, rows), rows)
        part_copy(0, tile).wait_recv()
        for k in range(1, ny):
            far_copy(k, tile).wait_recv()
        total = din[span, :] + part_k[0, span, :].astype(F32)
        for k in range(1, ny):
            total = total + part_y[k - 1, span, :].astype(F32)
        din[span, :] = total
        return carry

    lax.fori_loop(0, per, sum_tile, 0)
    keep_d = pltpu.make_async_copy(din, din_out, loc.at[10])
    keep_d.start()

    for p, r in lands:
        core_copy(p, r).wait_send()
        if r:
            y_copy(p, r).wait_send()
    for p in range(count):
        for k in fin_hops(p):
            fin_copy(p, k, me.s_from(k) if k else me.cpeer).wait_recv()
            fin_copy(p, k, s).wait_send()
        fin_keep(p).wait()
        if not pieces[p][3]:
            for k in range(1, ny):
                up_copy(p, k).wait_send()
        if p >= count - 3:
            side_copy(p).wait_send()
            for k in range(1, nz):
                line_copy(p, k).wait_send()
    for pair in range(pairs):
        for k in range(1, g):
            dctx_copy(pair, k, s).wait_send()
    for tile in range(per):
        for k in range(ny):
            part_copy(k, tile).wait_send()
        for k in range(1, ny):
            far_copy(k, tile).wait_send()
    for j in range(nz):
        qx_copy(j).wait_send()
    for k in range(1, nz):
        qz_copy(k).wait_send()
    for k in range(1, g):
        for copy in q_out_copies(k, me.s_from(k)):
            copy.wait_recv()
        for copy in q_out_copies(k, s):
            copy.wait_send()
    for copy in keep_q:
        copy.wait()
    keep_d.wait()


def cost(length, matmuls):
    return pl.CostEstimate(
        flops=2 * 2 * matmuls * length * length * 256,
        bytes_accessed=10 * length * LANES * 2,
        transcendentals=2 * length * length,
    )


def attend_backward(d_context, queries, keys, values, q_extra, context, hidden, w_heads, vecs,
                    g_out, g_up, g_down):
    n, g = lax.axis_size("dp"), lax.axis_size("seq")
    tok, width = d_context.shape
    length, gw, deep = tok * g, width // g, width // n
    pairs = gw // LANES
    nz, ny = n // 2, max(g // 2, 2)
    wide = min(1024, width)
    size = piece_rows(n)
    shares = [g.reshape(n, -1, g.shape[1]) for g in (g_out, g_up, g_down)]
    pieces = grad_pieces([share.shape[1:] for share in shares], n, g, wide)
    count = len(pieces)
    far = max(1, sum(piece[3] for piece in pieces))
    lands = count + (g // 2 - 1) * sum(piece[3] for piece in pieces)
    anyw = pl.BlockSpec(memory_space=pl.ANY)
    low = lambda *shape: jax.ShapeDtypeStruct(shape, LOW)
    vmem = lambda *shape: pltpu.VMEM(shape, LOW)
    vmem32 = lambda *shape: pltpu.VMEM(shape, F32)
    dma = lambda *shape: pltpu.SemaphoreType.DMA(shape)
    chunk = 768 if length % 768 == 0 else 256
    tall = deep + 16
    return pl.pallas_call(
        functools.partial(backward_kernel, n=n, g=g, rows=256, chunk=chunk),
        in_specs=[anyw] * 12,
        out_specs=[anyw] * 8,
        out_shape=[
            jax.ShapeDtypeStruct((tok, width), F32), *(low(*share.shape[1:]) for share in shares),
            low(deep, 3 * width), low(g, 16, 3 * gw), low(lands, n, size, wide),
            low(count, nz, size, wide),
        ],
        scratch_shapes=[
            vmem(length, LANES), vmem(length, 2 * LANES), vmem(length, 2 * LANES),
            vmem(LANES, length), vmem(2, length, LANES), vmem(length, LANES),
            vmem(pairs, length, LANES), vmem(3 * pairs, length, LANES), vmem32(length, LANES),
            vmem32(length, LANES), vmem(g, tok, width), vmem(width, 3 * gw), vmem(n, 16, 3 * gw),
            vmem(ny, tok, width), vmem(ny, tok, width), vmem(ny - 1, tok, width),
            vmem(ny - 1, tok, width), vmem32(tok, width),
            vmem(2, n, size, wide), vmem(2, n, size, wide), vmem(3, n, size, wide),
            vmem(nz, size, wide), vmem(3, nz, size, wide), vmem(count, nz - 1, size, wide),
            vmem(count, size, wide), vmem(count, ny, size, wide), vmem(count, size, wide),
            vmem(n, tall, 3 * gw), vmem(nz, tall, 3 * gw), vmem(nz, tall, 3 * gw),
            vmem(nz, tall, 3 * gw), vmem(tall, 3 * gw), vmem(far, n, size, wide),
            vmem(far, ny - 1, n, size, wide),
            dma(15), dma(2, 2), dma(2, pairs, g), dma(2, ny, tok // 256), dma(2, count, ny),
            dma(2, lands), dma(2, count), dma(2, count, nz), dma(count), dma(2, count, g),
            dma(pairs), dma(2, nz), dma(2, nz), dma(2, 4, g), dma(2, far, ny),
            dma(2, ny, tok // 256),
        ],
        compiler_params=pltpu.CompilerParams(
            vmem_limit_bytes=63 * 2**20, collective_id=1, has_side_effects=True
        ),
        cost_estimate=cost(length, 10),
    )(d_context, queries, keys, values, q_extra, context, hidden, w_heads, vecs, *shares)


def gelu_parts(pre):
    size = jnp.abs(pre)
    t = 1.0 / (1.0 + (0.3275911 * 0.7071067811865476) * size)
    bell = jnp.exp(-0.5 * pre * pre)
    poly = t * (0.127414796 + t * (-0.142248368 + t * (
        0.7107068705 + t * (-0.7265760135 + t * 0.5307027145))))
    tail = poly * bell
    phi = jnp.where(pre >= 0, 1.0 - tail, tail)
    return phi, bell * 0.3989422804014327


def up_kernel(x_ref, wu_ref, bu_ref, wd_ref, act_ref, slope_ref, sum_ref):
    pre = matmul(x_ref[...], wu_ref[...]) + bu_ref[...]
    phi, density = gelu_parts(pre)
    activ = (pre * phi).astype(LOW)
    act_ref[...] = activ
    slope_ref[...] = (phi + pre * density).astype(LOW)
    part = matmul(activ, wd_ref[...])

    @pl.when(pl.program_id(0) == 0)
    def _():
        sum_ref[...] = part

    @pl.when(pl.program_id(0) > 0)
    def _():
        sum_ref[...] += part


def feed_forward(normed_low, w_up, bias_up, w_down):
    tok, width = normed_low.shape
    ff = w_up.shape[1]
    tile = 512
    whole = pl.BlockSpec((tok, width), lambda i: (0, 0))
    col = pl.BlockSpec((tok, tile), lambda i: (0, i))
    return pl.pallas_call(
        up_kernel,
        grid=(ff // tile,),
        in_specs=[
            whole, pl.BlockSpec((width, tile), lambda i: (0, i)),
            pl.BlockSpec((1, tile), lambda i: (0, i)), pl.BlockSpec((tile, width), lambda i: (i, 0)),
        ],
        out_specs=[col, col, whole],
        out_shape=[
            jax.ShapeDtypeStruct((tok, ff), LOW), jax.ShapeDtypeStruct((tok, ff), LOW),
            jax.ShapeDtypeStruct((tok, width), F32),
        ],
        compiler_params=pltpu.CompilerParams(vmem_limit_bytes=48 * 2**20),
    )(normed_low, w_up, bias_up[None], w_down)


def down_kernel(
    x_ref, e_ref, wu_ref, wd_ref, act_ref, slope_ref, gu_ref, gd_ref, gb_ref, sum_ref,
):
    up = e_ref[...]
    d_pre = matmul_right(up, wd_ref[...]) * slope_ref[...].astype(F32)
    gb_ref[...] = jnp.sum(d_pre, 0, keepdims=True)
    d_low = d_pre.astype(LOW)
    gd_ref[...] = matmul_left(act_ref[...], up).astype(LOW)
    gu_ref[...] = matmul_left(x_ref[...], d_low).astype(LOW)
    part = matmul_right(d_low, wu_ref[...])

    @pl.when(pl.program_id(0) == 0)
    def _():
        sum_ref[...] = part

    @pl.when(pl.program_id(0) > 0)
    def _():
        sum_ref[...] += part


def feed_backward(normed_low, d_low, w_up, w_down, activ, slope):
    tok, width = normed_low.shape
    ff = w_up.shape[1]
    tile = 512
    whole = pl.BlockSpec((tok, width), lambda i: (0, 0))
    col = pl.BlockSpec((tok, tile), lambda i: (0, i))
    up = pl.BlockSpec((width, tile), lambda i: (0, i))
    down = pl.BlockSpec((tile, width), lambda i: (i, 0))
    return pl.pallas_call(
        down_kernel,
        grid=(ff // tile,),
        in_specs=[whole, whole, up, down, col, col],
        out_specs=[up, down, pl.BlockSpec((1, tile), lambda i: (0, i)), whole],
        out_shape=[
            jax.ShapeDtypeStruct((width, ff), LOW), jax.ShapeDtypeStruct((ff, width), LOW),
            jax.ShapeDtypeStruct((1, ff), F32), jax.ShapeDtypeStruct((tok, width), F32),
        ],
        compiler_params=pltpu.CompilerParams(vmem_limit_bytes=48 * 2**20),
    )(normed_low, d_low, w_up, w_down, activ, slope)


def own_columns(piece, width, group_width):
    count = width // piece.shape[0]
    mine = lax.broadcasted_iota(jnp.int32, (count, piece.shape[0]), 0) == lax.axis_index("dp")
    row = jnp.where(mine, piece[None], jnp.zeros((), LOW)).reshape(-1)
    return lax.dynamic_slice_in_dim(row, lax.axis_index("seq") * group_width, group_width, 0)


def laid(parts, total):
    out, at = None, 0
    for part in parts:
        if part is not None:
            one = jnp.pad(part, (at, total - at - part.shape[0]))
            out = one if out is None else out + one
            at += part.shape[0]
    return out


def local(
    hidden_in, key_bias, w_qkv, bias_q, bias_v, w_out, bias_out, gain_attn, shift_attn,
    w_up, bias_up, w_down, bias_down, gain_ffn, shift_ffn, grad_out,
):
    groups = lax.axis_size("seq")
    me = lax.axis_index("seq")
    tok_rows, width = hidden_in.shape
    group_width = width // groups
    deep = w_qkv.shape[0]
    shares = lax.axis_size("dp")

    vectors = (
        bias_q, bias_v, bias_out, gain_attn, shift_attn, bias_down, gain_ffn, shift_ffn, bias_up,
    )
    line = 3 * group_width
    filled = sum(vector.shape[0] for vector in vectors)
    tall = -(-filled // line)
    packed = laid(vectors, 15 * line)
    first_row = laid([own_columns(bias_q, width, group_width)], line) + jnp.pad(
        own_columns(bias_v, width, group_width), (2 * group_width, 0)
    )
    rows16 = jnp.concatenate([first_row, packed]).reshape(16, line)
    own_w = jnp.concatenate(
        [lax.dynamic_slice_in_dim(w_qkv, i * width + me * group_width, group_width, 1) for i in range(3)], 1
    )
    chunk = jnp.concatenate([own_w, rows16], 0)
    bias_rows = jnp.broadcast_to(key_bias, (8, tok_rows))
    (context, own_context, q_all, ka_all, v_all, q_extra, hidden_all, w_heads, vec_all, f_w_out,
     f_w_up, f_w_down) = attend_forward(hidden_in, chunk, bias_rows, w_out, w_up, w_down)
    f_w_out = f_w_out.reshape(-1, w_out.shape[1])
    f_w_up = f_w_up.reshape(-1, w_up.shape[1])
    f_w_down = f_w_down.reshape(-1, w_down.shape[1])
    packed = vec_all[:, 1 : 1 + tall].reshape(vec_all.shape[0], -1).astype(F32)
    fulls, at = [], 0
    for vector in vectors:
        fulls.append(packed[:, at : at + vector.shape[0]].reshape(-1))
        at += vector.shape[0]
    (f_bias_q, f_bias_v, f_bias_out, f_gain_attn, f_shift_attn, f_bias_down, f_gain_ffn,
     f_shift_ffn, f_bias_up) = fulls

    attended = hidden_in.astype(F32) + matmul(context, f_w_out) + f_bias_out
    normed = layer_norm(attended, f_gain_attn, f_shift_attn)
    normed_low = normed.astype(LOW)
    activ, slope, branch = feed_forward(normed_low, f_w_up, f_bias_up, f_w_down)
    branch_sum = normed + branch + f_bias_down
    output = layer_norm(branch_sum, f_gain_ffn, f_shift_ffn).astype(LOW)

    upstream = grad_out.astype(F32)
    _, norm_back = jax.vjp(layer_norm, branch_sum, f_gain_ffn, f_shift_ffn)
    d_branch, g_gain_ffn, g_shift_ffn = norm_back(upstream)
    g_bias_down = jnp.sum(d_branch, 0)
    d_branch_low = d_branch.astype(LOW)
    g_w_up, g_w_down, g_bias_up, d_up = feed_backward(
        normed_low, d_branch_low, f_w_up, f_w_down, activ, slope
    )
    d_normed = d_branch + d_up
    _, attn_norm_back = jax.vjp(layer_norm, attended, f_gain_attn, f_shift_attn)
    d_attended, g_gain_attn, g_shift_attn = attn_norm_back(d_normed)
    g_bias_out = jnp.sum(d_attended, 0)
    d_attended_low = d_attended.astype(LOW)
    g_w_out = matmul_left(context, d_attended_low).astype(LOW)
    d_context = matmul_right(d_attended_low, f_w_out).astype(LOW)

    vector_grads = (
        g_bias_out, g_gain_attn, g_shift_attn, g_bias_down, g_gain_ffn, g_shift_ffn, g_bias_up,
    )
    rows = jnp.concatenate([g.reshape(shares, -1) for g in vector_grads], 1).astype(LOW)
    filled = rows.shape[1]
    tall = -(-filled // (3 * group_width))
    vecs = jnp.pad(rows, ((0, 0), (0, tall * 3 * group_width - filled)))
    vecs = jnp.pad(vecs.reshape(shares, tall, -1), ((0, 0), (1, 15 - tall), (0, 0)))
    d_in, s_w_out, s_w_up, s_w_down, s_w_qkv, heads, _, _ = attend_backward(
        d_context, q_all, ka_all, v_all, q_extra, own_context, hidden_all, w_heads, vecs,
        g_w_out, g_w_up, g_w_down,
    )
    grad_in = d_attended + d_in
    s_w_out, s_w_up, s_w_down, s_w_qkv = (
        grad.astype(F32) for grad in (s_w_out, s_w_up, s_w_down, s_w_qkv)
    )
    head_rows = heads[:, 0].astype(F32)
    at = lax.axis_index("dp") * bias_q.shape[0]
    s_bias_q = lax.dynamic_slice_in_dim(
        head_rows[:, :group_width].reshape(-1), at, bias_q.shape[0], 0
    )
    s_bias_v = lax.dynamic_slice_in_dim(
        head_rows[:, 2 * group_width :].reshape(-1), at, bias_v.shape[0], 0
    )
    own = jnp.sum(heads[:, 1 : 1 + tall].astype(F32), 0).reshape(-1)
    own_vectors, at = [], 0
    for vector in vectors[2:]:
        own_vectors.append(own[at : at + vector.shape[0]])
        at += vector.shape[0]
    (s_bias_out, s_gain_attn, s_shift_attn, s_bias_down, s_gain_ffn, s_shift_ffn,
     s_bias_up) = own_vectors
    return (
        output, grad_in, s_w_qkv, s_bias_q, s_bias_v, s_w_out, s_bias_out, s_gain_attn,
        s_shift_attn, s_w_up, s_bias_up, s_w_down, s_bias_down, s_gain_ffn, s_shift_ffn,
    )


def solution(mesh):
    tokens = P(("dp", "seq"), None)
    matrix = P("dp", None)
    vector = P("dp")
    return jax.shard_map(
        local,
        mesh=mesh,
        in_specs=(
            tokens, P("dp", "seq"), matrix, vector, vector, matrix, vector, vector, vector,
            matrix, vector, matrix, vector, vector, vector, tokens,
        ),
        out_specs=(
            tokens, tokens, matrix, vector, vector, matrix, vector, vector, vector, matrix,
            vector, matrix, vector, vector, vector,
        ),
        check_vma=False,
    )
```

```python
import functools

import jax
import jax.numpy as jnp
from jax import lax
from jax.experimental import pallas as pl
from jax.experimental.pallas import tpu as pltpu
from jax.sharding import PartitionSpec as P

HEAD_DIM = 64
LANES = 128
SCALE = HEAD_DIM**-0.5
norm_eps = 1e-05
PIECE_STEPS = 3.2
PIECE_GAP = 3.5
F32 = jnp.float32
LOW = jnp.bfloat16


def layer_norm(hidden, gain_vec, shift_vec):
    row_mean = jnp.mean(hidden, -1, keepdims=True)
    centered = hidden - row_mean
    row_var = jnp.mean(centered * centered, -1, keepdims=True)
    return centered * lax.rsqrt(row_var + norm_eps) * gain_vec + shift_vec


def gelu_exact(pre_act):
    return jax.nn.gelu(pre_act, approximate=False)


def matmul(left, right):
    return jnp.dot(left, right, preferred_element_type=F32)


def matmul_left(left, right):
    return lax.dot_general(left, right, (((0,), (0,)), ((), ())), preferred_element_type=F32)


def matmul_right(left, right):
    return lax.dot_general(left, right, (((1,), (1,)), ((), ())), preferred_element_type=F32)


def thirds(value):
    first = value.astype(LOW)
    rest = value - first.astype(F32)
    second = rest.astype(LOW)
    third = (rest - second.astype(F32)).astype(LOW)
    return first.astype(F32), second.astype(F32), third.astype(F32)


def head_mask(rows, head):
    lane = lax.broadcasted_iota(jnp.int32, (rows, LANES), 1)
    return (lane < HEAD_DIM) if head == 0 else (lane >= HEAD_DIM)


def send_to(src, dst, send_sem, recv_sem, dp, seq):
    return pltpu.make_async_remote_copy(
        src_ref=src, dst_ref=dst, send_sem=send_sem, recv_sem=recv_sem,
        device_id=(dp, seq), device_id_type=pl.DeviceIdType.MESH,
    )


class Peers:
    def __init__(self, n, g):
        self.n, self.g, self.nz, self.ny = n, g, n // 2, g // 2
        self.d = lax.axis_index("dp")
        self.s = lax.axis_index("seq")
        self.z, self.x = self.d // 2, lax.rem(self.d, 2)
        self.y, self.c = self.s // 2, lax.rem(self.s, 2)
        self.xpeer = self.z * 2 + 1 - self.x
        self.cpeer = self.y * 2 + 1 - self.c

    def z_to(self, k):
        return lax.rem(self.z + k, self.nz) * 2 + self.x

    def z_from(self, k):
        return lax.rem(self.z + self.nz - k, self.nz) * 2 + self.x

    def side(self, dp):
        return (dp // 2) * 2 + 1 - self.x

    def y_to(self, k):
        return lax.rem(self.s + 2 * k, self.g)

    def y_from(self, k):
        return lax.rem(self.s + self.g - 2 * k, self.g)

    def s_to(self, k):
        return lax.rem(self.s + k, self.g)

    def s_from(self, k):
        return lax.rem(self.s + self.g - k, self.g)

    def barrier(self):
        sem = pltpu.get_barrier_semaphore()
        targets = [(self.z_to(k), self.s) for k in range(1, self.nz)]
        targets.append((self.xpeer, self.s))
        targets += [(self.d, self.s_to(k)) for k in range(1, self.g)]
        for target in targets:
            pl.semaphore_signal(
                sem, inc=1, device_id=target, device_id_type=pl.DeviceIdType.MESH
            )
        pl.semaphore_wait(sem, len(targets))


def weight_pieces(shapes, g):
    out = []
    for index, (rows, cols) in enumerate(shapes):
        quarter = rows % (16 * g) == 0 and index == 2
        own = rows // g if quarter else rows // 2
        size = min(own, max(16, 65536 // cols))
        for off in range(0, own, size):
            out.append((index, off, size, own, quarter))
    return sorted(out, key=lambda piece: not piece[4])


def forward_kernel(
    hid_ref, wch_ref, kb_ref, wo_ref, wu_ref, wd_ref,
    ctx_out, own_ctx, q_out, ka_out, v_out, qx_out, hid_out, wq_out, vec_out, wo_out, wu_out, wd_out,
    hid, wch, wq, kb, q_s, k_s, v_s, ka, va, ctx, qx,
    loc, hy, hc, hf, kbs, wz, wx, pz, px, pc, py, pf, cs, kx,
    *, n, g, rows,
):
    me = Peers(n, g)
    d, s, nz, ny = me.d, me.s, me.nz, me.ny
    tok, width = hid_ref.shape
    length = tok * g
    deep = width // n
    gw = width // g
    pairs = gw // LANES
    cut = tok // 3
    shards = (wo_ref, wu_ref, wd_ref)
    fulls = (wo_out, wu_out, wd_out)
    pieces = weight_pieces([ref.shape for ref in shards], g)
    me.barrier()

    local = [
        pltpu.make_async_copy(hid_ref, hid.at[s], loc.at[0]),
        pltpu.make_async_copy(wch_ref, wch.at[d], loc.at[1]),
        pltpu.make_async_copy(kb_ref, kb.at[s], loc.at[2]),
    ]
    keep = [
        pltpu.make_async_copy(shards[i], fulls[i].at[d], loc.at[3 + i]) for i in range(3)
    ]

    def y_copy(k, part, slot):
        span = pl.ds(part * cut, cut)
        return send_to(
            hid_ref.at[span], hid.at[slot, span], hy.at[0, k, part], hy.at[1, k, part], d,
            me.y_to(k),
        )

    def c_copy(slot):
        return send_to(hid_ref, hid.at[slot], hc.at[0], hc.at[1], d, me.cpeer)

    def f_copy(k, part, slot):
        span = pl.ds(part * cut, cut)
        return send_to(
            hid.at[slot, span], hid.at[slot, span], hf.at[0, k, part], hf.at[1, k, part], d,
            me.cpeer,
        )

    def kb_copy(k, slot):
        return send_to(kb_ref, kb.at[slot], kbs.at[0, k], kbs.at[1, k], d, me.s_to(k))

    def wz_copy(k, slot):
        return send_to(wch_ref, wch.at[slot], wz.at[0, k], wz.at[1, k], me.z_to(k), s)

    def wx_copy(k, src, slot):
        return send_to(src, wch.at[slot], wx.at[0, k], wx.at[1, k], me.xpeer, s)

    def c_of_y(k):
        return me.y_from(k) // 2 * 2 + 1 - me.c

    for copy in local:
        copy.start()
    for k in range(1, nz):
        wz_copy(k, d).start()
    wx_copy(0, wch_ref, d).start()
    for k in range(1, g):
        kb_copy(k, s).start()
    for part in range(3):
        for k in range(1, ny):
            y_copy(k, part, s).start()
    c_copy(s).start()
    for copy in keep:
        copy.start()

    def span_of(p, seq):
        index, off, size, own, quarter = pieces[p]
        part = seq if quarter else lax.rem(seq, 2)
        return index, pl.ds(pl.multiple_of(part * own + off, 16), size)

    def block_of(k, side):
        slot = me.z_from(k) if k else d
        if side:
            slot = me.side(slot)
        return slot

    def pz_copy(p, k, slot):
        index, span = span_of(p, s)
        return send_to(
            shards[index].at[span], fulls[index].at[slot, span], pz.at[0, p, k], pz.at[1, p, k],
            me.z_to(k), s,
        )

    def px_copy(p, k, slot):
        index, span = span_of(p, s)
        src = shards[index].at[span] if k == 0 else fulls[index].at[slot, span]
        return send_to(
            src, fulls[index].at[slot, span], px.at[0, p, k], px.at[1, p, k], me.xpeer, s
        )

    def pc_copy(p, k, side, seq):
        index, span = span_of(p, seq)
        ref = fulls[index].at[block_of(k, side), span]
        return send_to(
            ref, ref, pc.at[0, p, k, side], pc.at[1, p, k, side], d, me.cpeer
        )

    def py_copy(p, j, k, side, seq):
        index, span = span_of(p, seq)
        ref = fulls[index].at[block_of(k, side), span]
        return send_to(
            ref, ref, py.at[0, p, j, k, side], py.at[1, p, j, k, side], d, me.y_to(j)
        )

    def pf_copy(p, j, k, side, seq):
        index, span = span_of(p, seq)
        ref = fulls[index].at[block_of(k, side), span]
        return send_to(
            ref, ref, pf.at[0, p, j, k, side], pf.at[1, p, j, k, side], d, me.cpeer
        )

    moves = [(k, 0) for k in range(1, nz)] + [(k, 1) for k in range(nz)]

    def spread(p, k, side):
        if pieces[p][4]:
            for j in range(1, ny):
                py_copy(p, j, k, side, s).start()
        pc_copy(p, k, side, s).start()

    def piece_send(p):
        for k in range(1, nz):
            pz_copy(p, k, d).start()
        px_copy(p, 0, d).start()

    def piece_pass(p):
        for k in range(1, nz):
            slot = me.z_from(k)
            pz_copy(p, k, slot).wait_recv()
            px_copy(p, k, slot).start()
            spread(p, k, 0)

    def piece_share(p):
        for k in range(nz):
            px_copy(p, k, block_of(k, 1)).wait_recv()
            spread(p, k, 1)

    def piece_far(p):
        if pieces[p][4]:
            for j in range(1, ny):
                for k, side in moves:
                    py_copy(p, j, k, side, me.y_from(j)).wait_recv()
                    pf_copy(p, j, k, side, me.y_from(j)).start()

    def piece_end(p):
        for k, side in moves:
            pc_copy(p, k, side, me.cpeer).wait_recv()
            pc_copy(p, k, side, s).wait_send()
            if pieces[p][4]:
                for j in range(1, ny):
                    pf_copy(p, j, k, side, c_of_y(j)).wait_recv()
                    pf_copy(p, j, k, side, me.y_from(j)).wait_send()
                    py_copy(p, j, k, side, s).wait_send()
        for k in range(1, nz):
            pz_copy(p, k, d).wait_send()
        for k in range(nz):
            px_copy(p, k, block_of(k, 0)).wait_send()

    for k in range(1, nz):
        slot = me.z_from(k)
        wz_copy(k, slot).wait_recv()
        wx_copy(k, wch.at[slot], slot).start()
    for k in range(nz):
        slot = me.side(me.z_from(k)) if k else me.xpeer
        wx_copy(k, wch_ref, slot).wait_recv()
    for copy in local:
        copy.wait()
    piece_send(0)
    if len(pieces) > 1:
        piece_send(1)
    for j in range(n):
        wq[j * deep : (j + 1) * deep, :] = wch[j, :deep, :]
    bias_row = jnp.sum(wch[:, deep : deep + 16, :].astype(F32)[:, 0:1, :], 0)
    saves = [
        pltpu.make_async_copy(wq, wq_out, loc.at[6]),
        pltpu.make_async_copy(wch.at[:, pl.ds(deep, 16)], vec_out, loc.at[7]),
    ]
    for copy in saves:
        copy.start()

    tiles = tok // cut

    def project(step, carry):
        rel = step // tiles
        part = lax.rem(step, tiles)

        @pl.when(step == tiles)
        def _():
            c_copy(me.cpeer).wait_recv()

        for k in range(1, ny):
            @pl.when(step == 2 * k * tiles)
            def _(k=k):
                if k == 1 and len(pieces) > 2:
                    piece_send(2)
                for sub in range(3):
                    y_copy(k, sub, me.y_from(k)).wait_recv()
                    f_copy(k, sub, me.y_from(k)).start()

            @pl.when(step == (2 * k + 1) * tiles)
            def _(k=k):
                for sub in range(3):
                    f_copy(k, sub, c_of_y(k)).wait_recv()

        y_at = lax.rem(me.y + ny - rel // 2, ny)
        c_at = lax.rem(me.c + rel, 2)
        slot = y_at * 2 + c_at
        got = matmul(hid[slot, pl.ds(part * cut, cut), :], wq[...]) + bias_row
        got = got.astype(LOW)
        span = pl.ds(pl.multiple_of(slot * tok + part * cut, cut), cut)
        for index, ref in enumerate((q_s, k_s, v_s)):
            for pair in range(pairs):
                at = index * gw + pair * LANES
                ref[pair, span, :] = got[:, at : at + LANES]
        return carry

    lax.fori_loop(0, g * tiles, project, 0)
    for k in range(1, g):
        kb_copy(k, me.s_from(k)).wait_recv()
    more = [
        pltpu.make_async_copy(hid, hid_out, loc.at[8]),
        pltpu.make_async_copy(q_s, q_out, loc.at[9]),
        pltpu.make_async_copy(v_s, v_out, loc.at[11]),
    ]
    for copy in more:
        copy.start()
    saves += more

    blocks = length // rows
    per = tok // rows
    steps = pairs * blocks

    def ctx_copy(pair, k, source):
        span = pl.ds(pl.multiple_of(me.s_to(k) * tok, tok), tok)
        return send_to(
            ctx.at[pair, span],
            ctx_out.at[:, pl.ds(pl.multiple_of(source * gw + pair * LANES, LANES), LANES)],
            cs.at[0, pair, k], cs.at[1, pair, k], d, me.s_to(k),
        )

    def ctx_keep(pair):
        return pltpu.make_async_copy(
            ctx.at[pair, pl.ds(pl.multiple_of(s * tok, tok), tok)],
            ctx_out.at[:, pl.ds(pl.multiple_of(s * gw + pair * LANES, LANES), LANES)],
            kx.at[pair],
        )

    def ka_keep(pair):
        return pltpu.make_async_copy(ka, ka_out.at[pair], loc.at[10])

    events = {}
    gap = PIECE_GAP
    for p in range(len(pieces)):
        if p >= 3:
            events.setdefault(int(gap * (p - 3)), []).append(lambda p=p: piece_send(p))
        at = int(max(0, gap * (p - 1) + 1))
        events.setdefault(at, []).append(lambda p=p: piece_pass(p))
        events.setdefault(at + 3, []).append(lambda p=p: piece_share(p))
        events.setdefault(at + 7, []).append(lambda p=p: piece_far(p))
    late = [e for t in sorted(events) if t >= steps for e in events[t]]

    def attend(step, carry):
        pair = step // blocks
        turn = lax.rem(step, blocks)
        k_own = lax.rem(1 + turn // per, g)
        owner = lax.rem(s + k_own, g)
        block = owner * per + lax.rem(turn, per)
        for t in sorted(events):
            if t < steps:
                @pl.when(step == t)
                def _(t=t):
                    for event in events[t]:
                        event()

        @pl.when((turn == 0) & (step > 0))
        def _():
            ka_keep(pair - 1).wait()

        @pl.when(turn == 0)
        def _():
            lane = lax.broadcasted_iota(jnp.int32, (tok, LANES), 1)
            for j in range(g):
                span = slice(j * tok, (j + 1) * tok)
                column = jnp.broadcast_to(kb[j, 0:1, :], (LANES, tok)).T
                first, second, third = thirds(column)
                extra = jnp.where(
                    lane == 0, first,
                    jnp.where(lane == 1, second, jnp.where(lane == 2, third, 1.0)),
                )
                ka[span, :LANES] = k_s[pair, span, :]
                ka[span, LANES:] = jnp.where(lane < 6, extra, 0.0).astype(LOW)
                va[span, :LANES] = v_s[pair, span, :]
                va[span, LANES:] = jnp.where(lane < 3, 1.0, 0.0).astype(LOW)
            ka_keep(pair).start()

        span = pl.ds(pl.multiple_of(block * rows, rows), rows)
        lane = lax.broadcasted_iota(jnp.int32, (rows, LANES), 1)
        queries = q_s[pair, span, :].astype(F32) * SCALE
        ones = jnp.where(lane < 3, 1.0, 0.0)
        outs = []
        for head in range(2):
            masked = jnp.where(head_mask(rows, head), queries, 0.0)
            wide = jnp.concatenate([masked, ones], 1).astype(LOW)
            scores = matmul_right(wide, ka[...])
            row_max = jnp.max(scores, -1, keepdims=True)
            expo = jnp.exp(scores - row_max).astype(LOW)
            both = matmul(expo, va[...])
            total = both[:, LANES : LANES + 1]
            outs.append(both[:, :LANES] / total)
            first, second, third = thirds(row_max + jnp.log(total))
            qx[pair, head, span, :] = jnp.where(
                lane == 3, -first,
                jnp.where(lane == 4, -second, jnp.where(lane == 5, -third, ones)),
            ).astype(LOW)
        ctx[pair, span, :] = jnp.where(head_mask(rows, 0), outs[0], outs[1]).astype(LOW)

        for p in range(pairs):
            for k in range(1, g):
                @pl.when(step == p * blocks + k * per - 1)
                def _(p=p, k=k):
                    ctx_copy(p, k, s).start()

            @pl.when(step == (p + 1) * blocks - 1)
            def _(p=p):
                ctx_keep(p).start()
        return carry

    lax.fori_loop(0, steps, attend, 0)
    ka_keep(pairs - 1).wait()
    last = [
        pltpu.make_async_copy(qx, qx_out, loc.at[12]),
        pltpu.make_async_copy(ctx, own_ctx, loc.at[13]),
    ]
    for copy in last:
        copy.start()
    for event in late:
        event()
    for k in range(1, g):
        kb_copy(k, s).wait_send()
    for k in range(1, ny):
        for part in range(3):
            y_copy(k, part, s).wait_send()
            f_copy(k, part, me.y_from(k)).wait_send()
    c_copy(s).wait_send()
    for k in range(1, nz):
        wz_copy(k, d).wait_send()
        slot = me.z_from(k)
        wx_copy(k, wch.at[slot], slot).wait_send()
    wx_copy(0, wch_ref, d).wait_send()
    for pair in range(pairs):
        ctx_keep(pair).wait()
        for k in range(1, g):
            ctx_copy(pair, k, me.s_from(k)).wait_recv()
            ctx_copy(pair, k, s).wait_send()
    for p in range(len(pieces)):
        piece_end(p)
    for copy in saves + last + keep:
        copy.wait()


def attend_forward(hidden, chunk, bias_rows, w_out, w_up, w_down):
    n, g = lax.axis_size("dp"), lax.axis_size("seq")
    tok, width = hidden.shape
    length, gw, deep = tok * g, width // g, width // n
    pairs = gw // LANES
    count = len(weight_pieces([w.shape for w in (w_out, w_up, w_down)], g))
    anyw = pl.BlockSpec(memory_space=pl.ANY)
    low = lambda *shape: jax.ShapeDtypeStruct(shape, LOW)
    out_shape = [
        low(tok, width), low(pairs, length, LANES), low(pairs, length, LANES),
        low(pairs, length, 2 * LANES), low(pairs, length, LANES), low(pairs, 2, length, LANES),
        low(g, tok, width), low(width, 3 * gw), low(n, 16, 3 * gw),
        low(n, *w_out.shape), low(n, *w_up.shape), low(n, *w_down.shape),
    ]
    dma = lambda *shape: pltpu.SemaphoreType.DMA(shape)
    nz, ny = n // 2, max(g // 2, 2)
    vmem = lambda shape, kind=LOW: pltpu.VMEM(shape, kind)
    return pl.pallas_call(
        functools.partial(forward_kernel, n=n, g=g, rows=256),
        in_specs=[anyw] * 6,
        out_specs=[anyw] * 12,
        out_shape=out_shape,
        scratch_shapes=[
            vmem((g, tok, width)), vmem((n, deep + 16, 3 * gw)), vmem((width, 3 * gw)),
            vmem((g, 8, tok), F32), vmem((pairs, length, LANES)), vmem((pairs, length, LANES)),
            vmem((pairs, length, LANES)), vmem((length, 2 * LANES)), vmem((length, 2 * LANES)),
            vmem((pairs, length, LANES)), vmem((pairs, 2, length, LANES)),
            dma(14), dma(2, ny, 3), dma(2), dma(2, ny, 3), dma(2, g), dma(2, nz), dma(2, nz),
            dma(2, count, nz), dma(2, count, nz), dma(2, count, nz, 2),
            dma(2, count, ny, nz, 2), dma(2, count, ny, nz, 2), dma(2, pairs, g), dma(pairs),
        ],
        compiler_params=pltpu.CompilerParams(
            vmem_limit_bytes=56 * 2**20, collective_id=0, has_side_effects=True
        ),
        cost_estimate=cost(length, 4),
    )(hidden, chunk, bias_rows, w_out, w_up, w_down)


def piece_rows(n):
    return max(16, 512 // n)


def grad_pieces(shapes, n, g, wide):
    halves, quarters = [], []
    for index, (rows, cols) in enumerate(shapes):
        quarter = rows % (16 * g) == 0 and index == 2
        own = rows // g if quarter else rows // 2
        size = min(own, piece_rows(n))
        for off in range(0, own, size):
            for col in range(0, cols, wide):
                (quarters if quarter else halves).append((index, off, col, quarter))
    out = halves[:3]
    rest = halves[3:]
    for piece in quarters:
        out.append(piece)
        out += rest[:1]
        rest = rest[1:]
    return out + rest


def grad_times(pieces):
    times, lines, x_free, z_free = [], [], 0.0, 0.0
    y_free = 5.0
    at = 2
    for piece in pieces:
        first = None
        if piece[3]:
            first = 3 if not lines else lines[-1] + 2
            lines.append(first)
            y_free = max(y_free, first) + 5.0
            at = max(at, int(y_free) + 1)
        start = max(at, int(x_free - 1.0))
        x_free = max(x_free, start) + PIECE_STEPS
        side = int(x_free + 0.9)
        z_free = max(z_free, side) + PIECE_STEPS
        line = int(z_free + 0.9)
        times.append((first, start, side, line, line + 2))
        at = start + 2
    return times


def backward_kernel(
    dctx_ref, q_ref, ka_ref, v_ref, qx_ref, o_ref, hid_ref, wq_ref, vec_ref, go_ref, gu_ref,
    gd_ref,
    din_out, so_out, su_out, sd_out, sq_out, extra_out, c_land, x_land,
    q_s, ka, va, kt, qx, o_s, do_s, dh, dk_acc, dv_acc, hid, wq, vec,
    part_c, part_k, part_y, part_b, din, own_b, c_b, s_b, x_b, t_b, z_b, u_b, y_b, f_b,
    q_b, xq, tq, zq, rq, far_b, far_l,
    loc, ld, sd, sk, sy, sc, sx, sz, sg, sf, sl, sxq, szq, sgq, sfar, sfr,
    *, n, g, rows, chunk,
):
    me = Peers(n, g)
    d, s, nz, ny = me.d, me.s, me.nz, me.ny
    tok, width = dctx_ref.shape
    length = tok * g
    deep = width // n
    gw = width // g
    pairs = gw // LANES
    grads = (go_ref, gu_ref, gd_ref)
    wide = own_b.shape[3]
    size = own_b.shape[2]
    outs = (so_out, su_out, sd_out)
    pieces = grad_pieces([ref.shape[1:] for ref in grads], n, g, wide)
    times = grad_times(pieces)
    count = len(pieces)
    lands, spots = [], {}
    for p, piece in enumerate(pieces):
        for r in range(ny if piece[3] else 1):
            spots[p, r] = len(lands)
            lands.append((p, r))
    fars = [p for p in range(count) if pieces[p][3]]
    blocks = length // rows
    per = tok // rows
    steps = pairs * blocks
    me.barrier()

    def dctx_copy(pair, k, slot):
        cols = pl.ds(pl.multiple_of(me.s_to(k) * gw + pair * LANES, LANES), LANES)
        return send_to(
            dctx_ref.at[:, cols], do_s.at[pair, pl.ds(pl.multiple_of(slot * tok, tok), tok)],
            sd.at[0, pair, k], sd.at[1, pair, k], d, me.s_to(k),
        )

    def dctx_own(pair):
        cols = pl.ds(pl.multiple_of(s * gw + pair * LANES, LANES), LANES)
        return pltpu.make_async_copy(
            dctx_ref.at[:, cols], do_s.at[pair, pl.ds(pl.multiple_of(s * tok, tok), tok)],
            sl.at[pair],
        )

    def pair_loads(pair):
        return [
            pltpu.make_async_copy(q_ref.at[pair], q_s, loc.at[0]),
            pltpu.make_async_copy(ka_ref.at[pair], ka, loc.at[1]),
            pltpu.make_async_copy(v_ref.at[pair], va.at[:, pl.ds(0, LANES)], loc.at[2]),
            pltpu.make_async_copy(qx_ref.at[pair], qx, loc.at[3]),
            pltpu.make_async_copy(o_ref.at[pair], o_s, loc.at[4]),
        ]

    tail_loads = [
        pltpu.make_async_copy(hid_ref, hid, loc.at[5]),
        pltpu.make_async_copy(wq_ref, wq, loc.at[6]),
        pltpu.make_async_copy(vec_ref, vec, loc.at[7]),
    ]

    def row_of(p, core, y_at):
        index, off, col, quarter = pieces[p]
        own = grads[index].shape[1] // 2
        at = core * own + off
        if quarter:
            at = at + y_at * (own // ny)
        return pl.multiple_of(at, 16)

    def part_of(p, r, core):
        index, off, col, quarter = pieces[p]
        row = row_of(p, core, lax.rem(me.y + r, ny))
        return grads[index].at[:, pl.ds(row, size), pl.ds(col, wide)]

    def core_copy(p, r):
        i = spots[p, r]
        return send_to(
            part_of(p, r, 1 - me.c), c_land.at[i], sc.at[0, i], sc.at[1, i], d, me.cpeer
        )

    def own_load(p, r):
        i = spots[p, r] % 2
        return pltpu.make_async_copy(part_of(p, r, me.c), own_b.at[i], ld.at[0, i])

    def core_load(p, r):
        i = spots[p, r] % 2
        return pltpu.make_async_copy(c_land.at[spots[p, r]], c_b.at[i], ld.at[1, i])

    def y_copy(p, r):
        i = fars.index(p)
        return send_to(
            far_b.at[i], far_l.at[i, r - 1], sfar.at[0, i, r], sfar.at[1, i, r], d, me.y_to(r)
        )

    def side_copy(p):
        return send_to(
            s_b.at[p % 3, pl.ds(0, nz)], x_land.at[p], sx.at[0, p], sx.at[1, p], me.xpeer, s
        )

    def line_copy(p, k):
        return send_to(
            t_b.at[p % 3, lax.rem(me.z + k, nz)], z_b.at[p, k - 1], sz.at[0, p, k], sz.at[1, p, k],
            me.z_to(k), s,
        )

    def up_copy(p, k):
        return send_to(
            u_b.at[p], y_b.at[p, k], sy.at[0, p, k], sy.at[1, p, k], d, me.y_to(k)
        )

    def done_at(p, seq):
        index, off, col, quarter = pieces[p]
        row = row_of(p, lax.rem(seq, 2), seq // 2)
        return outs[index].at[pl.ds(row, size), pl.ds(col, wide)]

    def fin_hops(p):
        return range(1, g) if pieces[p][3] else (0,)

    def fin_copy(p, k, seq):
        to = me.s_to(k) if k else me.cpeer
        return send_to(f_b.at[p], done_at(p, seq), sf.at[0, p, k], sf.at[1, p, k], d, to)

    def fin_keep(p):
        return pltpu.make_async_copy(f_b.at[p], done_at(p, s), sg.at[p])

    def load(p, r):
        own_load(p, r).start()
        core_copy(p, r).wait_recv()
        core_load(p, r).start()

    def far_sum(p):
        for r in range(1, ny):
            i = spots[p, r] % 2
            own_load(p, r).wait()
            core_load(p, r).wait()

            def add(j, carry, i=i):
                total = own_b[i, j].astype(F32) + c_b[i, j].astype(F32)
                far_b[fars.index(p), j] = total.astype(LOW)
                return carry

            lax.fori_loop(0, n, add, 0)
            y_copy(p, r).start()

    def e2(p):
        slot, i = p % 3, spots[p, 0] % 2
        own_load(p, 0).wait()
        core_load(p, 0).wait()
        if pieces[p][3]:
            for r in range(1, ny):
                y_copy(p, r).wait_recv()
        if p >= 3:
            side_copy(p - 3).wait_send()

        def add(j, carry):
            for part in range(2):
                at = 2 * j + (1 - me.x if part == 0 else me.x)
                total = own_b[i, at].astype(F32) + c_b[i, at].astype(F32)
                if pieces[p][3]:
                    for r in range(1, ny):
                        total = total + far_l[fars.index(p), r - 1, at].astype(F32)
                s_b[slot, part * nz + j] = total.astype(LOW)
            return carry

        lax.fori_loop(0, nz, add, 0)
        side_copy(p).start()

    def e3(p):
        slot = p % 3
        side_copy(p).wait_recv()
        get = pltpu.make_async_copy(x_land.at[p], x_b, loc.at[8])
        get.start()
        if p >= 3:
            for k in range(1, nz):
                line_copy(p - 3, k).wait_send()
        get.wait()

        def add(j, carry):
            total = s_b[slot, nz + j].astype(F32) + x_b[j].astype(F32)
            t_b[slot, j] = total.astype(LOW)
            return carry

        lax.fori_loop(0, nz, add, 0)
        for k in range(1, nz):
            line_copy(p, k).start()

    def finish(p):
        for k in fin_hops(p):
            fin_copy(p, k, s).start()
        fin_keep(p).start()

    def e4(p):
        slot = p % 3
        for k in range(1, nz):
            line_copy(p, k).wait_recv()
        total = t_b[slot, me.z].astype(F32)
        for k in range(1, nz):
            total = total + z_b[p, k - 1].astype(F32)
        if pieces[p][3]:
            f_b[p] = total.astype(LOW)
            finish(p)
        else:
            u_b[p] = total.astype(LOW)
            for k in range(1, ny):
                up_copy(p, k).start()

    def e5(p):
        if pieces[p][3]:
            return
        for k in range(1, ny):
            up_copy(p, k).wait_recv()
        total = u_b[p].astype(F32)
        for k in range(1, ny):
            total = total + y_b[p, k].astype(F32)
        f_b[p] = total.astype(LOW)
        finish(p)

    plan = []
    for p in range(count):
        first, start, side, line, end = times[p]
        if first is not None:
            for r in range(1, ny):
                plan.append((first - 1, 5, lambda p=p, r=r: load(p, r)))
            plan.append((first, 4, lambda p=p: far_sum(p)))
        plan.append((start - 1, 5, lambda p=p: load(p, 0)))
        for r in range(ny if first is not None else 1):
            at = start if r == 0 else first
            plan.append((at - 3, 6, lambda p=p, r=r: core_copy(p, r).start()))
        plan.append((start, 3, lambda p=p: e2(p)))
        plan.append((side, 2, lambda p=p: e3(p)))
        plan.append((line, 1, lambda p=p: e4(p)))
        plan.append((end, 0, lambda p=p: e5(p)))
    plan.sort(key=lambda item: item[:2])

    for pair in range(pairs):
        dctx_own(pair).start()
        for k in range(1, g):
            dctx_copy(pair, k, s).start()
    for copy in tail_loads:
        copy.start()
    for at, order, event in plan:
        if at < 0:
            event()
    lane_l = lax.broadcasted_iota(jnp.int32, (tok, LANES), 1)
    for j in range(g):
        va[j * tok : (j + 1) * tok, LANES:] = jnp.where(lane_l < 3, 1.0, 0.0).astype(LOW)

    near = [me.y * 2, me.y * 2 + 1]
    far_slots = [lax.rem(me.y + k, ny) * 2 + i for k in range(1, ny) for i in range(2)]
    near_blocks = 2 * per
    full = steps - near_blocks

    def run_events(step):
        for t in sorted({item[0] for item in plan}):
            if 0 <= t < steps:
                @pl.when(step == t)
                def _(t=t):
                    for at, order, event in plan:
                        if at == t:
                            event()

    def block_pass(pair, block, slots):
        span = pl.ds(pl.multiple_of(block * rows, rows), rows)
        lane = lax.broadcasted_iota(jnp.int32, (rows, LANES), 1)
        queries = q_s[span, :].astype(F32) * SCALE
        upstream = do_s[pair, span, :].astype(F32)
        dots = upstream * o_s[span, :].astype(F32)
        q_wide, g_wide, q_mask, g_mask = [], [], [], []
        for head in range(2):
            mask = head_mask(rows, head)
            masked = jnp.where(mask, queries, 0.0).astype(LOW)
            g_masked = jnp.where(mask, upstream, 0.0).astype(LOW)
            delta = jnp.sum(jnp.where(mask, dots, 0.0), -1, keepdims=True)
            first, second, third = thirds(delta)
            extra = jnp.where(
                lane == 0, -first, jnp.where(lane == 1, -second, jnp.where(lane == 2, -third, 0.0))
            ).astype(LOW)
            q_mask.append(masked)
            g_mask.append(g_masked)
            q_wide.append(jnp.concatenate([masked, qx[head, span, :]], 1))
            g_wide.append(jnp.concatenate([g_masked, extra], 1))
        q_rows = jnp.concatenate(q_mask, 0)
        g_rows = jnp.concatenate(g_mask, 0)
        dq_t = [jnp.zeros((LANES, rows), F32) for _ in range(2)]
        for slot in slots:
            for base in range(0, tok, chunk):
                at = slot * tok + base
                part = slice(at, at + chunk)
                if not isinstance(at, int):
                    part = pl.ds(pl.multiple_of(at, LANES), chunk)
                p_list, ds_list = [], []
                for head in range(2):
                    probs = jnp.exp(matmul_right(ka[part, :], q_wide[head]))
                    d_scores = (probs * matmul_right(va[part, :], g_wide[head])).astype(LOW)
                    p_list.append(probs.astype(LOW))
                    ds_list.append(d_scores)
                    dq_t[head] = dq_t[head] + matmul(kt[:, part], d_scores)
                dv_acc[part, :] += matmul(jnp.concatenate(p_list, 1), g_rows)
                dk_acc[part, :] += matmul(jnp.concatenate(ds_list, 1), q_rows)
        row = lax.broadcasted_iota(jnp.int32, (LANES, rows), 0)
        return jnp.where(row < HEAD_DIM, dq_t[0], dq_t[1]) * SCALE

    def attend(step, carry):
        pair = step // blocks
        turn = lax.rem(step, blocks)
        rel = turn // per
        owner = lax.rem(s + g - rel, g)
        owner = jnp.where(pair == pairs - 1, lax.rem(me.y * 2 + 2 + rel, g), owner)
        block = owner * per + lax.rem(turn, per)

        @pl.when(turn == 0)
        def _():
            loads = pair_loads(pair)
            for copy in loads:
                copy.start()
            dk_acc[...] = jnp.zeros_like(dk_acc)
            dv_acc[...] = jnp.zeros_like(dv_acc)
            dctx_own(pair).wait()
            for copy in loads:
                copy.wait()
            for j in range(length // chunk):
                part = slice(j * chunk, (j + 1) * chunk)
                kt[:, part] = ka[part, :LANES].astype(F32).T.astype(LOW)

        run_events(step)
        for k in range(1, g):
            @pl.when(turn == jnp.where(pair == pairs - 1, 0, k * per))
            def _(k=k):
                dctx_copy(pair, k, me.s_from(k)).wait_recv()

        both = block_pass(pair, block, range(g))
        dh[pair, pl.ds(pl.multiple_of(block * rows, rows), rows), :] = both.T.astype(LOW)

        @pl.when(turn == blocks - 1)
        def _():
            dh[pairs + pair] = dk_acc[...].astype(LOW)
            dh[2 * pairs + pair] = dv_acc[...].astype(LOW)
        return carry

    lax.fori_loop(0, full, attend, 0)
    last = pairs - 1

    def keep_heads(slots):
        for slot in slots:
            span = pl.ds(pl.multiple_of(slot * tok, tok), tok)
            dh[pairs + last, span, :] = dk_acc[span, :].astype(LOW)
            dh[2 * pairs + last, span, :] = dv_acc[span, :].astype(LOW)

    def far_keys(i, carry):
        @pl.when(lax.rem(i, 2) == 0)
        def _():
            run_events(full + i // 2)

        both = block_pass(last, me.y * near_blocks + i, far_slots)
        din[pl.ds(pl.multiple_of(i * LANES, LANES), LANES), :rows] = both
        return carry

    def near_keys(i, carry):
        @pl.when(lax.rem(i, 2) == 0)
        def _():
            run_events(full + (near_blocks + i) // 2)

        block = me.y * near_blocks + i
        both = block_pass(last, block, near)
        both = both + din[pl.ds(pl.multiple_of(i * LANES, LANES), LANES), :rows]
        dh[last, pl.ds(pl.multiple_of(block * rows, rows), rows), :] = both.T.astype(LOW)
        return carry

    lax.fori_loop(0, near_blocks, far_keys, 0)
    keep_heads(far_slots)
    for copy in tail_loads:
        copy.wait()
    def heads_of(slot, tile):
        span = pl.ds(pl.multiple_of(slot * tok + tile * rows, rows), rows)
        return jnp.concatenate([dh[i, span, :] for i in range(3 * pairs)], 1)

    def part_copy(k, tile):
        span = pl.ds(pl.multiple_of(tile * rows, rows), rows)
        return send_to(
            part_c.at[k, span], part_k.at[k, span], sk.at[0, k, tile], sk.at[1, k, tile], d,
            me.cpeer,
        )

    def far_copy(k, tile):
        span = pl.ds(pl.multiple_of(tile * rows, rows), rows)
        return send_to(
            part_b.at[k - 1, span], part_y.at[k - 1, span], sfr.at[0, k, tile], sfr.at[1, k, tile],
            d, me.y_to(k),
        )

    def core_part(k):
        slot = lax.rem(me.y + k, ny) * 2 + 1 - me.c

        def tile_of(tile, carry):
            span = pl.ds(pl.multiple_of(tile * rows, rows), rows)
            part_c[k, span, :] = matmul_right(heads_of(slot, tile), wq[...]).astype(LOW)
            part_copy(k, tile).start()
            return carry

        lax.fori_loop(0, per, tile_of, 0)

    for k in range(1, ny):
        core_part(k)
    for k in range(1, ny):
        slot = lax.rem(me.y + k, ny) * 2 + me.c

        def far_tile(tile, carry, k=k, slot=slot):
            span = pl.ds(pl.multiple_of(tile * rows, rows), rows)
            total = matmul_right(heads_of(slot, tile), wq[...])
            part_copy(k, tile).wait_recv()
            total = total + part_k[k, span, :].astype(F32)
            part_b[k - 1, span, :] = total.astype(LOW)
            far_copy(k, tile).start()
            return carry

        lax.fori_loop(0, per, far_tile, 0)

    lax.fori_loop(0, near_blocks, near_keys, 0)
    keep_heads(near)
    for at, order, event in plan:
        if at >= steps and order in (3, 4, 5, 6):
            event()

    for at, order, event in plan:
        if at >= steps and order == 2:
            event()

    sums = [jnp.zeros((1, LANES), F32) for _ in range(3 * pairs)]
    for i in range(3 * pairs):
        for j in range(g):
            span = slice(j * tok, (j + 1) * tok)
            sums[i] = sums[i] + jnp.sum(dh[i, span, :].astype(F32), 0, keepdims=True)
    sums = jnp.concatenate(sums, 1)
    row16 = lax.broadcasted_iota(jnp.int32, (16, 3 * gw), 0)
    for j in range(n):
        q_b[j, deep:, :] = (vec[j].astype(F32) + jnp.where(row16 == 0, sums, 0.0)).astype(LOW)

    def qx_copy(j):
        return send_to(
            q_b.at[2 * j + 1 - me.x], xq.at[j], sxq.at[0, j], sxq.at[1, j], me.xpeer, s
        )

    def qz_copy(k):
        return send_to(
            tq.at[lax.rem(me.z + k, nz)], zq.at[k], szq.at[0, k], szq.at[1, k], me.z_to(k), s
        )

    def q_parts(source):
        parts = [(rq.at[pl.ds(deep, 16)], extra_out.at[source])]
        for i in range(3):
            at = pl.ds(pl.multiple_of(i * width + source * gw, LANES), gw)
            parts.append((rq.at[pl.ds(0, deep), pl.ds(i * gw, gw)], sq_out.at[:, at]))
        return parts

    def q_out_copies(k, source):
        return [
            send_to(src, dst, sgq.at[0, i, k], sgq.at[1, i, k], d, me.s_to(k))
            for i, (src, dst) in enumerate(q_parts(source))
        ]

    tile_w = 256
    for base in range(0, width, tile_w):
        total = jnp.zeros((tile_w, 3 * gw), F32)
        for j in range(g):
            right = jnp.concatenate(
                [dh[i, j * tok : (j + 1) * tok, :] for i in range(3 * pairs)], 1
            )
            total = total + matmul_left(hid[j, :, base : base + tile_w], right)
        for at in range(0, tile_w, deep):
            q_b[(base + at) // deep, :deep, :] = total[at : at + deep, :].astype(LOW)
        for j in range(base // deep // 2, (base + tile_w) // deep // 2):
            qx_copy(j).start()
    core_part(0)

    def own_tile(tile, carry):
        span = pl.ds(pl.multiple_of(tile * rows, rows), rows)
        din[span, :] = matmul_right(heads_of(s, tile), wq[...])
        return carry

    lax.fori_loop(0, per, own_tile, 0)

    for at, order, event in plan:
        if at >= steps and order in (0, 1):
            event()

    for j in range(nz):
        qx_copy(j).wait_recv()
        kept = q_b[2 * j + me.x].astype(F32) + xq[j].astype(F32)
        tq[j] = kept.astype(LOW)
    for k in range(1, nz):
        qz_copy(k).start()
    for k in range(1, nz):
        qz_copy(k).wait_recv()
    total = tq[me.z].astype(F32)
    for k in range(1, nz):
        total = total + zq[k].astype(F32)
    rq[...] = total.astype(LOW)
    for k in range(1, g):
        for copy in q_out_copies(k, s):
            copy.start()
    keep_q = [
        pltpu.make_async_copy(src, dst, loc.at[11 + i])
        for i, (src, dst) in enumerate(q_parts(s))
    ]
    for copy in keep_q:
        copy.start()

    def sum_tile(tile, carry):
        span = pl.ds(pl.multiple_of(tile * rows, rows), rows)
        part_copy(0, tile).wait_recv()
        for k in range(1, ny):
            far_copy(k, tile).wait_recv()
        total = din[span, :] + part_k[0, span, :].astype(F32)
        for k in range(1, ny):
            total = total + part_y[k - 1, span, :].astype(F32)
        din[span, :] = total
        return carry

    lax.fori_loop(0, per, sum_tile, 0)
    keep_d = pltpu.make_async_copy(din, din_out, loc.at[10])
    keep_d.start()

    for p, r in lands:
        core_copy(p, r).wait_send()
        if r:
            y_copy(p, r).wait_send()
    for p in range(count):
        for k in fin_hops(p):
            fin_copy(p, k, me.s_from(k) if k else me.cpeer).wait_recv()
            fin_copy(p, k, s).wait_send()
        fin_keep(p).wait()
        if not pieces[p][3]:
            for k in range(1, ny):
                up_copy(p, k).wait_send()
        if p >= count - 3:
            side_copy(p).wait_send()
            for k in range(1, nz):
                line_copy(p, k).wait_send()
    for pair in range(pairs):
        for k in range(1, g):
            dctx_copy(pair, k, s).wait_send()
    for tile in range(per):
        for k in range(ny):
            part_copy(k, tile).wait_send()
        for k in range(1, ny):
            far_copy(k, tile).wait_send()
    for j in range(nz):
        qx_copy(j).wait_send()
    for k in range(1, nz):
        qz_copy(k).wait_send()
    for k in range(1, g):
        for copy in q_out_copies(k, me.s_from(k)):
            copy.wait_recv()
        for copy in q_out_copies(k, s):
            copy.wait_send()
    for copy in keep_q:
        copy.wait()
    keep_d.wait()


def cost(length, matmuls):
    return pl.CostEstimate(
        flops=2 * 2 * matmuls * length * length * 256,
        bytes_accessed=10 * length * LANES * 2,
        transcendentals=2 * length * length,
    )


def attend_backward(d_context, queries, keys, values, q_extra, context, hidden, w_heads, vecs,
                    g_out, g_up, g_down):
    n, g = lax.axis_size("dp"), lax.axis_size("seq")
    tok, width = d_context.shape
    length, gw, deep = tok * g, width // g, width // n
    pairs = gw // LANES
    nz, ny = n // 2, max(g // 2, 2)
    wide = min(1024, width)
    size = piece_rows(n)
    shares = [g.reshape(n, -1, g.shape[1]) for g in (g_out, g_up, g_down)]
    pieces = grad_pieces([share.shape[1:] for share in shares], n, g, wide)
    count = len(pieces)
    far = max(1, sum(piece[3] for piece in pieces))
    lands = count + (g // 2 - 1) * sum(piece[3] for piece in pieces)
    anyw = pl.BlockSpec(memory_space=pl.ANY)
    low = lambda *shape: jax.ShapeDtypeStruct(shape, LOW)
    vmem = lambda *shape: pltpu.VMEM(shape, LOW)
    vmem32 = lambda *shape: pltpu.VMEM(shape, F32)
    dma = lambda *shape: pltpu.SemaphoreType.DMA(shape)
    chunk = 768 if length % 768 == 0 else 256
    tall = deep + 16
    return pl.pallas_call(
        functools.partial(backward_kernel, n=n, g=g, rows=256, chunk=chunk),
        in_specs=[anyw] * 12,
        out_specs=[anyw] * 8,
        out_shape=[
            jax.ShapeDtypeStruct((tok, width), F32), *(low(*share.shape[1:]) for share in shares),
            low(deep, 3 * width), low(g, 16, 3 * gw), low(lands, n, size, wide),
            low(count, nz, size, wide),
        ],
        scratch_shapes=[
            vmem(length, LANES), vmem(length, 2 * LANES), vmem(length, 2 * LANES),
            vmem(LANES, length), vmem(2, length, LANES), vmem(length, LANES),
            vmem(pairs, length, LANES), vmem(3 * pairs, length, LANES), vmem32(length, LANES),
            vmem32(length, LANES), vmem(g, tok, width), vmem(width, 3 * gw), vmem(n, 16, 3 * gw),
            vmem(ny, tok, width), vmem(ny, tok, width), vmem(ny - 1, tok, width),
            vmem(ny - 1, tok, width), vmem32(tok, width),
            vmem(2, n, size, wide), vmem(2, n, size, wide), vmem(3, n, size, wide),
            vmem(nz, size, wide), vmem(3, nz, size, wide), vmem(count, nz - 1, size, wide),
            vmem(count, size, wide), vmem(count, ny, size, wide), vmem(count, size, wide),
            vmem(n, tall, 3 * gw), vmem(nz, tall, 3 * gw), vmem(nz, tall, 3 * gw),
            vmem(nz, tall, 3 * gw), vmem(tall, 3 * gw), vmem(far, n, size, wide),
            vmem(far, ny - 1, n, size, wide),
            dma(15), dma(2, 2), dma(2, pairs, g), dma(2, ny, tok // 256), dma(2, count, ny),
            dma(2, lands), dma(2, count), dma(2, count, nz), dma(count), dma(2, count, g),
            dma(pairs), dma(2, nz), dma(2, nz), dma(2, 4, g), dma(2, far, ny),
            dma(2, ny, tok // 256),
        ],
        compiler_params=pltpu.CompilerParams(
            vmem_limit_bytes=63 * 2**20, collective_id=1, has_side_effects=True
        ),
        cost_estimate=cost(length, 10),
    )(d_context, queries, keys, values, q_extra, context, hidden, w_heads, vecs, *shares)


def gelu_parts(pre):
    size = jnp.abs(pre)
    t = 1.0 / (1.0 + (0.3275911 * 0.7071067811865476) * size)
    bell = jnp.exp(-0.5 * pre * pre)
    poly = t * (0.127414796 + t * (-0.142248368 + t * (
        0.7107068705 + t * (-0.7265760135 + t * 0.5307027145))))
    tail = poly * bell
    phi = jnp.where(pre >= 0, 1.0 - tail, tail)
    return phi, bell * 0.3989422804014327


def up_kernel(x_ref, wu_ref, bu_ref, wd_ref, act_ref, slope_ref, sum_ref):
    pre = matmul(x_ref[...], wu_ref[...]) + bu_ref[...]
    phi, density = gelu_parts(pre)
    activ = (pre * phi).astype(LOW)
    act_ref[...] = activ
    slope_ref[...] = (phi + pre * density).astype(LOW)
    part = matmul(activ, wd_ref[...])

    @pl.when(pl.program_id(0) == 0)
    def _():
        sum_ref[...] = part

    @pl.when(pl.program_id(0) > 0)
    def _():
        sum_ref[...] += part


def feed_forward(normed_low, w_up, bias_up, w_down):
    tok, width = normed_low.shape
    ff = w_up.shape[1]
    tile = 512
    whole = pl.BlockSpec((tok, width), lambda i: (0, 0))
    col = pl.BlockSpec((tok, tile), lambda i: (0, i))
    return pl.pallas_call(
        up_kernel,
        grid=(ff // tile,),
        in_specs=[
            whole, pl.BlockSpec((width, tile), lambda i: (0, i)),
            pl.BlockSpec((1, tile), lambda i: (0, i)), pl.BlockSpec((tile, width), lambda i: (i, 0)),
        ],
        out_specs=[col, col, whole],
        out_shape=[
            jax.ShapeDtypeStruct((tok, ff), LOW), jax.ShapeDtypeStruct((tok, ff), LOW),
            jax.ShapeDtypeStruct((tok, width), F32),
        ],
        compiler_params=pltpu.CompilerParams(vmem_limit_bytes=48 * 2**20),
    )(normed_low, w_up, bias_up[None], w_down)


def down_kernel(
    x_ref, e_ref, wu_ref, wd_ref, act_ref, slope_ref, gu_ref, gd_ref, gb_ref, sum_ref,
):
    up = e_ref[...]
    d_pre = matmul_right(up, wd_ref[...]) * slope_ref[...].astype(F32)
    gb_ref[...] = jnp.sum(d_pre, 0, keepdims=True)
    d_low = d_pre.astype(LOW)
    gd_ref[...] = matmul_left(act_ref[...], up).astype(LOW)
    gu_ref[...] = matmul_left(x_ref[...], d_low).astype(LOW)
    part = matmul_right(d_low, wu_ref[...])

    @pl.when(pl.program_id(0) == 0)
    def _():
        sum_ref[...] = part

    @pl.when(pl.program_id(0) > 0)
    def _():
        sum_ref[...] += part


def feed_backward(normed_low, d_low, w_up, w_down, activ, slope):
    tok, width = normed_low.shape
    ff = w_up.shape[1]
    tile = 512
    whole = pl.BlockSpec((tok, width), lambda i: (0, 0))
    col = pl.BlockSpec((tok, tile), lambda i: (0, i))
    up = pl.BlockSpec((width, tile), lambda i: (0, i))
    down = pl.BlockSpec((tile, width), lambda i: (i, 0))
    return pl.pallas_call(
        down_kernel,
        grid=(ff // tile,),
        in_specs=[whole, whole, up, down, col, col],
        out_specs=[up, down, pl.BlockSpec((1, tile), lambda i: (0, i)), whole],
        out_shape=[
            jax.ShapeDtypeStruct((width, ff), LOW), jax.ShapeDtypeStruct((ff, width), LOW),
            jax.ShapeDtypeStruct((1, ff), F32), jax.ShapeDtypeStruct((tok, width), F32),
        ],
        compiler_params=pltpu.CompilerParams(vmem_limit_bytes=48 * 2**20),
    )(normed_low, d_low, w_up, w_down, activ, slope)


def own_columns(piece, width, group_width):
    count = width // piece.shape[0]
    mine = lax.broadcasted_iota(jnp.int32, (count, piece.shape[0]), 0) == lax.axis_index("dp")
    row = jnp.where(mine, piece[None], jnp.zeros((), LOW)).reshape(-1)
    return lax.dynamic_slice_in_dim(row, lax.axis_index("seq") * group_width, group_width, 0)


def laid(parts, total):
    out, at = None, 0
    for part in parts:
        if part is not None:
            one = jnp.pad(part, (at, total - at - part.shape[0]))
            out = one if out is None else out + one
            at += part.shape[0]
    return out


def local(
    hidden_in, key_bias, w_qkv, bias_q, bias_v, w_out, bias_out, gain_attn, shift_attn,
    w_up, bias_up, w_down, bias_down, gain_ffn, shift_ffn, grad_out,
):
    groups = lax.axis_size("seq")
    me = lax.axis_index("seq")
    tok_rows, width = hidden_in.shape
    group_width = width // groups
    deep = w_qkv.shape[0]
    shares = lax.axis_size("dp")

    vectors = (
        bias_q, bias_v, bias_out, gain_attn, shift_attn, bias_down, gain_ffn, shift_ffn, bias_up,
    )
    line = 3 * group_width
    filled = sum(vector.shape[0] for vector in vectors)
    tall = -(-filled // line)
    packed = laid(vectors, 15 * line)
    first_row = laid([own_columns(bias_q, width, group_width)], line) + jnp.pad(
        own_columns(bias_v, width, group_width), (2 * group_width, 0)
    )
    rows16 = jnp.concatenate([first_row, packed]).reshape(16, line)
    own_w = jnp.concatenate(
        [lax.dynamic_slice_in_dim(w_qkv, i * width + me * group_width, group_width, 1) for i in range(3)], 1
    )
    chunk = jnp.concatenate([own_w, rows16], 0)
    bias_rows = jnp.broadcast_to(key_bias, (8, tok_rows))
    (context, own_context, q_all, ka_all, v_all, q_extra, hidden_all, w_heads, vec_all, f_w_out,
     f_w_up, f_w_down) = attend_forward(hidden_in, chunk, bias_rows, w_out, w_up, w_down)
    f_w_out = f_w_out.reshape(-1, w_out.shape[1])
    f_w_up = f_w_up.reshape(-1, w_up.shape[1])
    f_w_down = f_w_down.reshape(-1, w_down.shape[1])
    packed = vec_all[:, 1 : 1 + tall].reshape(vec_all.shape[0], -1).astype(F32)
    fulls, at = [], 0
    for vector in vectors:
        fulls.append(packed[:, at : at + vector.shape[0]].reshape(-1))
        at += vector.shape[0]
    (f_bias_q, f_bias_v, f_bias_out, f_gain_attn, f_shift_attn, f_bias_down, f_gain_ffn,
     f_shift_ffn, f_bias_up) = fulls

    attended = hidden_in.astype(F32) + matmul(context, f_w_out) + f_bias_out
    normed = layer_norm(attended, f_gain_attn, f_shift_attn)
    normed_low = normed.astype(LOW)
    activ, slope, branch = feed_forward(normed_low, f_w_up, f_bias_up, f_w_down)
    branch_sum = normed + branch + f_bias_down
    output = layer_norm(branch_sum, f_gain_ffn, f_shift_ffn).astype(LOW)

    upstream = grad_out.astype(F32)
    _, norm_back = jax.vjp(layer_norm, branch_sum, f_gain_ffn, f_shift_ffn)
    d_branch, g_gain_ffn, g_shift_ffn = norm_back(upstream)
    g_bias_down = jnp.sum(d_branch, 0)
    d_branch_low = d_branch.astype(LOW)
    g_w_up, g_w_down, g_bias_up, d_up = feed_backward(
        normed_low, d_branch_low, f_w_up, f_w_down, activ, slope
    )
    d_normed = d_branch + d_up
    _, attn_norm_back = jax.vjp(layer_norm, attended, f_gain_attn, f_shift_attn)
    d_attended, g_gain_attn, g_shift_attn = attn_norm_back(d_normed)
    g_bias_out = jnp.sum(d_attended, 0)
    d_attended_low = d_attended.astype(LOW)
    g_w_out = matmul_left(context, d_attended_low).astype(LOW)
    d_context = matmul_right(d_attended_low, f_w_out).astype(LOW)

    vector_grads = (
        g_bias_out, g_gain_attn, g_shift_attn, g_bias_down, g_gain_ffn, g_shift_ffn, g_bias_up,
    )
    rows = jnp.concatenate([g.reshape(shares, -1) for g in vector_grads], 1).astype(LOW)
    filled = rows.shape[1]
    tall = -(-filled // (3 * group_width))
    vecs = jnp.pad(rows, ((0, 0), (0, tall * 3 * group_width - filled)))
    vecs = jnp.pad(vecs.reshape(shares, tall, -1), ((0, 0), (1, 15 - tall), (0, 0)))
    d_in, s_w_out, s_w_up, s_w_down, s_w_qkv, heads, _, _ = attend_backward(
        d_context, q_all, ka_all, v_all, q_extra, own_context, hidden_all, w_heads, vecs,
        g_w_out, g_w_up, g_w_down,
    )
    grad_in = d_attended + d_in
    s_w_out, s_w_up, s_w_down, s_w_qkv = (
        grad.astype(F32) for grad in (s_w_out, s_w_up, s_w_down, s_w_qkv)
    )
    head_rows = heads[:, 0].astype(F32)
    at = lax.axis_index("dp") * bias_q.shape[0]
    s_bias_q = lax.dynamic_slice_in_dim(
        head_rows[:, :group_width].reshape(-1), at, bias_q.shape[0], 0
    )
    s_bias_v = lax.dynamic_slice_in_dim(
        head_rows[:, 2 * group_width :].reshape(-1), at, bias_v.shape[0], 0
    )
    own = jnp.sum(heads[:, 1 : 1 + tall].astype(F32), 0).reshape(-1)
    own_vectors, at = [], 0
    for vector in vectors[2:]:
        own_vectors.append(own[at : at + vector.shape[0]])
        at += vector.shape[0]
    (s_bias_out, s_gain_attn, s_shift_attn, s_bias_down, s_gain_ffn, s_shift_ffn,
     s_bias_up) = own_vectors
    return (
        output, grad_in, s_w_qkv, s_bias_q, s_bias_v, s_w_out, s_bias_out, s_gain_attn,
        s_shift_attn, s_w_up, s_bias_up, s_w_down, s_bias_down, s_gain_ffn, s_shift_ffn,
    )


def solution(mesh):
    tokens = P(("dp", "seq"), None)
    matrix = P("dp", None)
    vector = P("dp")
    return jax.shard_map(
        local,
        mesh=mesh,
        in_specs=(
            tokens, P("dp", "seq"), matrix, vector, vector, matrix, vector, vector, vector,
            matrix, vector, matrix, vector, vector, vector, tokens,
        ),
        out_specs=(
            tokens, tokens, matrix, vector, vector, matrix, vector, vector, vector, matrix,
            vector, matrix, vector, vector, vector,
        ),
        check_vma=False,
    )
```

```python
import functools

import jax
import jax.numpy as jnp
from jax import lax
from jax.experimental import pallas as pl
from jax.experimental.pallas import tpu as pltpu
from jax.sharding import PartitionSpec as P

HEAD_DIM = 64
LANES = 128
SCALE = HEAD_DIM**-0.5
norm_eps = 1e-05
PIECE_STEPS = 3.2
PIECE_GAP = 3.5
F32 = jnp.float32
LOW = jnp.bfloat16


def layer_norm(hidden, gain_vec, shift_vec):
    row_mean = jnp.mean(hidden, -1, keepdims=True)
    centered = hidden - row_mean
    row_var = jnp.mean(centered * centered, -1, keepdims=True)
    return centered * lax.rsqrt(row_var + norm_eps) * gain_vec + shift_vec


def gelu_exact(pre_act):
    return jax.nn.gelu(pre_act, approximate=False)


def matmul(left, right):
    return jnp.dot(left, right, preferred_element_type=F32)


def matmul_left(left, right):
    return lax.dot_general(left, right, (((0,), (0,)), ((), ())), preferred_element_type=F32)


def matmul_right(left, right):
    return lax.dot_general(left, right, (((1,), (1,)), ((), ())), preferred_element_type=F32)


def thirds(value):
    first = value.astype(LOW)
    rest = value - first.astype(F32)
    second = rest.astype(LOW)
    third = (rest - second.astype(F32)).astype(LOW)
    return first.astype(F32), second.astype(F32), third.astype(F32)


def head_mask(rows, head):
    lane = lax.broadcasted_iota(jnp.int32, (rows, LANES), 1)
    return (lane < HEAD_DIM) if head == 0 else (lane >= HEAD_DIM)


def send_to(src, dst, send_sem, recv_sem, dp, seq):
    return pltpu.make_async_remote_copy(
        src_ref=src, dst_ref=dst, send_sem=send_sem, recv_sem=recv_sem,
        device_id=(dp, seq), device_id_type=pl.DeviceIdType.MESH,
    )


class Peers:
    def __init__(self, n, g):
        self.n, self.g, self.nz, self.ny = n, g, n // 2, g // 2
        self.d = lax.axis_index("dp")
        self.s = lax.axis_index("seq")
        self.z, self.x = self.d // 2, lax.rem(self.d, 2)
        self.y, self.c = self.s // 2, lax.rem(self.s, 2)
        self.xpeer = self.z * 2 + 1 - self.x
        self.cpeer = self.y * 2 + 1 - self.c

    def z_to(self, k):
        return lax.rem(self.z + k, self.nz) * 2 + self.x

    def z_from(self, k):
        return lax.rem(self.z + self.nz - k, self.nz) * 2 + self.x

    def side(self, dp):
        return (dp // 2) * 2 + 1 - self.x

    def y_to(self, k):
        return lax.rem(self.s + 2 * k, self.g)

    def y_from(self, k):
        return lax.rem(self.s + self.g - 2 * k, self.g)

    def s_to(self, k):
        return lax.rem(self.s + k, self.g)

    def s_from(self, k):
        return lax.rem(self.s + self.g - k, self.g)

    def barrier(self):
        sem = pltpu.get_barrier_semaphore()
        targets = [(self.z_to(k), self.s) for k in range(1, self.nz)]
        targets.append((self.xpeer, self.s))
        targets += [(self.d, self.s_to(k)) for k in range(1, self.g)]
        for target in targets:
            pl.semaphore_signal(
                sem, inc=1, device_id=target, device_id_type=pl.DeviceIdType.MESH
            )
        pl.semaphore_wait(sem, len(targets))


def weight_pieces(shapes, g):
    out = []
    for index, (rows, cols) in enumerate(shapes):
        quarter = rows % (16 * g) == 0 and index == 2
        own = rows // g if quarter else rows // 2
        size = min(own, max(16, 65536 // cols))
        for off in range(0, own, size):
            out.append((index, off, size, own, quarter))
    return sorted(out, key=lambda piece: not piece[4])


def forward_kernel(
    hid_ref, wch_ref, kb_ref, wo_ref, wu_ref, wd_ref,
    ctx_out, own_ctx, q_out, ka_out, v_out, qx_out, hid_out, wq_out, vec_out, wo_out, wu_out, wd_out,
    hid, wch, wq, kb, q_s, k_s, v_s, ka, va, ctx, qx,
    loc, hy, hc, hf, kbs, wz, wx, pz, px, pc, py, pf, cs, kx,
    *, n, g, rows,
):
    me = Peers(n, g)
    d, s, nz, ny = me.d, me.s, me.nz, me.ny
    tok, width = hid_ref.shape
    length = tok * g
    deep = width // n
    gw = width // g
    pairs = gw // LANES
    cut = tok // 3
    shards = (wo_ref, wu_ref, wd_ref)
    fulls = (wo_out, wu_out, wd_out)
    pieces = weight_pieces([ref.shape for ref in shards], g)
    me.barrier()

    local = [
        pltpu.make_async_copy(hid_ref, hid.at[s], loc.at[0]),
        pltpu.make_async_copy(wch_ref, wch.at[d], loc.at[1]),
        pltpu.make_async_copy(kb_ref, kb.at[s], loc.at[2]),
    ]
    keep = [
        pltpu.make_async_copy(shards[i], fulls[i].at[d], loc.at[3 + i]) for i in range(3)
    ]

    def y_copy(k, part, slot):
        span = pl.ds(part * cut, cut)
        return send_to(
            hid_ref.at[span], hid.at[slot, span], hy.at[0, k, part], hy.at[1, k, part], d,
            me.y_to(k),
        )

    def c_copy(slot):
        return send_to(hid_ref, hid.at[slot], hc.at[0], hc.at[1], d, me.cpeer)

    def f_copy(k, part, slot):
        span = pl.ds(part * cut, cut)
        return send_to(
            hid.at[slot, span], hid.at[slot, span], hf.at[0, k, part], hf.at[1, k, part], d,
            me.cpeer,
        )

    def kb_copy(k, slot):
        return send_to(kb_ref, kb.at[slot], kbs.at[0, k], kbs.at[1, k], d, me.s_to(k))

    def wz_copy(k, slot):
        return send_to(wch_ref, wch.at[slot], wz.at[0, k], wz.at[1, k], me.z_to(k), s)

    def wx_copy(k, src, slot):
        return send_to(src, wch.at[slot], wx.at[0, k], wx.at[1, k], me.xpeer, s)

    def c_of_y(k):
        return me.y_from(k) // 2 * 2 + 1 - me.c

    for copy in local:
        copy.start()
    for k in range(1, nz):
        wz_copy(k, d).start()
    wx_copy(0, wch_ref, d).start()
    for k in range(1, g):
        kb_copy(k, s).start()
    for part in range(3):
        for k in range(1, ny):
            y_copy(k, part, s).start()
    c_copy(s).start()
    for copy in keep:
        copy.start()

    def span_of(p, seq):
        index, off, size, own, quarter = pieces[p]
        part = seq if quarter else lax.rem(seq, 2)
        return index, pl.ds(pl.multiple_of(part * own + off, 16), size)

    def block_of(k, side):
        slot = me.z_from(k) if k else d
        if side:
            slot = me.side(slot)
        return slot

    def pz_copy(p, k, slot):
        index, span = span_of(p, s)
        return send_to(
            shards[index].at[span], fulls[index].at[slot, span], pz.at[0, p, k], pz.at[1, p, k],
            me.z_to(k), s,
        )

    def px_copy(p, k, slot):
        index, span = span_of(p, s)
        src = shards[index].at[span] if k == 0 else fulls[index].at[slot, span]
        return send_to(
            src, fulls[index].at[slot, span], px.at[0, p, k], px.at[1, p, k], me.xpeer, s
        )

    def pc_copy(p, k, side, seq):
        index, span = span_of(p, seq)
        ref = fulls[index].at[block_of(k, side), span]
        return send_to(
            ref, ref, pc.at[0, p, k, side], pc.at[1, p, k, side], d, me.cpeer
        )

    def py_copy(p, j, k, side, seq):
        index, span = span_of(p, seq)
        ref = fulls[index].at[block_of(k, side), span]
        return send_to(
            ref, ref, py.at[0, p, j, k, side], py.at[1, p, j, k, side], d, me.y_to(j)
        )

    def pf_copy(p, j, k, side, seq):
        index, span = span_of(p, seq)
        ref = fulls[index].at[block_of(k, side), span]
        return send_to(
            ref, ref, pf.at[0, p, j, k, side], pf.at[1, p, j, k, side], d, me.cpeer
        )

    moves = [(k, 0) for k in range(1, nz)] + [(k, 1) for k in range(nz)]

    def spread(p, k, side):
        if pieces[p][4]:
            for j in range(1, ny):
                py_copy(p, j, k, side, s).start()
        pc_copy(p, k, side, s).start()

    def piece_send(p):
        for k in range(1, nz):
            pz_copy(p, k, d).start()
        px_copy(p, 0, d).start()

    def piece_pass(p):
        for k in range(1, nz):
            slot = me.z_from(k)
            pz_copy(p, k, slot).wait_recv()
            px_copy(p, k, slot).start()
            spread(p, k, 0)

    def piece_share(p):
        for k in range(nz):
            px_copy(p, k, block_of(k, 1)).wait_recv()
            spread(p, k, 1)

    def piece_far(p):
        if pieces[p][4]:
            for j in range(1, ny):
                for k, side in moves:
                    py_copy(p, j, k, side, me.y_from(j)).wait_recv()
                    pf_copy(p, j, k, side, me.y_from(j)).start()

    def piece_end(p):
        for k, side in moves:
            pc_copy(p, k, side, me.cpeer).wait_recv()
            pc_copy(p, k, side, s).wait_send()
            if pieces[p][4]:
                for j in range(1, ny):
                    pf_copy(p, j, k, side, c_of_y(j)).wait_recv()
                    pf_copy(p, j, k, side, me.y_from(j)).wait_send()
                    py_copy(p, j, k, side, s).wait_send()
        for k in range(1, nz):
            pz_copy(p, k, d).wait_send()
        for k in range(nz):
            px_copy(p, k, block_of(k, 0)).wait_send()

    for k in range(1, nz):
        slot = me.z_from(k)
        wz_copy(k, slot).wait_recv()
        wx_copy(k, wch.at[slot], slot).start()
    for k in range(nz):
        slot = me.side(me.z_from(k)) if k else me.xpeer
        wx_copy(k, wch_ref, slot).wait_recv()
    for copy in local:
        copy.wait()
    piece_send(0)
    if len(pieces) > 1:
        piece_send(1)
    for j in range(n):
        wq[j * deep : (j + 1) * deep, :] = wch[j, :deep, :]
    bias_row = jnp.sum(wch[:, deep : deep + 16, :].astype(F32)[:, 0:1, :], 0)
    saves = [
        pltpu.make_async_copy(wq, wq_out, loc.at[6]),
        pltpu.make_async_copy(wch.at[:, pl.ds(deep, 16)], vec_out, loc.at[7]),
    ]
    for copy in saves:
        copy.start()

    tiles = tok // cut

    def project(step, carry):
        rel = step // tiles
        part = lax.rem(step, tiles)

        @pl.when(step == tiles)
        def _():
            c_copy(me.cpeer).wait_recv()

        for k in range(1, ny):
            @pl.when(step == 2 * k * tiles)
            def _(k=k):
                if k == 1 and len(pieces) > 2:
                    piece_send(2)
                for sub in range(3):
                    y_copy(k, sub, me.y_from(k)).wait_recv()
                    f_copy(k, sub, me.y_from(k)).start()

            @pl.when(step == (2 * k + 1) * tiles)
            def _(k=k):
                for sub in range(3):
                    f_copy(k, sub, c_of_y(k)).wait_recv()

        y_at = lax.rem(me.y + ny - rel // 2, ny)
        c_at = lax.rem(me.c + rel, 2)
        slot = y_at * 2 + c_at
        got = matmul(hid[slot, pl.ds(part * cut, cut), :], wq[...]) + bias_row
        got = got.astype(LOW)
        span = pl.ds(pl.multiple_of(slot * tok + part * cut, cut), cut)
        for index, ref in enumerate((q_s, k_s, v_s)):
            for pair in range(pairs):
                at = index * gw + pair * LANES
                ref[pair, span, :] = got[:, at : at + LANES]
        return carry

    lax.fori_loop(0, g * tiles, project, 0)
    for k in range(1, g):
        kb_copy(k, me.s_from(k)).wait_recv()
    more = [
        pltpu.make_async_copy(hid, hid_out, loc.at[8]),
        pltpu.make_async_copy(q_s, q_out, loc.at[9]),
        pltpu.make_async_copy(v_s, v_out, loc.at[11]),
    ]
    for copy in more:
        copy.start()
    saves += more

    blocks = length // rows
    per = tok // rows
    steps = pairs * blocks

    def ctx_copy(pair, k, source):
        span = pl.ds(pl.multiple_of(me.s_to(k) * tok, tok), tok)
        return send_to(
            ctx.at[pair, span],
            ctx_out.at[:, pl.ds(pl.multiple_of(source * gw + pair * LANES, LANES), LANES)],
            cs.at[0, pair, k], cs.at[1, pair, k], d, me.s_to(k),
        )

    def ctx_keep(pair):
        return pltpu.make_async_copy(
            ctx.at[pair, pl.ds(pl.multiple_of(s * tok, tok), tok)],
            ctx_out.at[:, pl.ds(pl.multiple_of(s * gw + pair * LANES, LANES), LANES)],
            kx.at[pair],
        )

    def ka_keep(pair):
        return pltpu.make_async_copy(ka, ka_out.at[pair], loc.at[10])

    events = {}
    gap = PIECE_GAP
    for p in range(len(pieces)):
        if p >= 3:
            events.setdefault(int(gap * (p - 3)), []).append(lambda p=p: piece_send(p))
        at = int(max(0, gap * (p - 1) + 1))
        events.setdefault(at, []).append(lambda p=p: piece_pass(p))
        events.setdefault(at + 3, []).append(lambda p=p: piece_share(p))
        events.setdefault(at + 7, []).append(lambda p=p: piece_far(p))
    late = [e for t in sorted(events) if t >= steps for e in events[t]]

    def attend(step, carry):
        pair = step // blocks
        turn = lax.rem(step, blocks)
        k_own = lax.rem(1 + turn // per, g)
        owner = lax.rem(s + k_own, g)
        block = owner * per + lax.rem(turn, per)
        for t in sorted(events):
            if t < steps:
                @pl.when(step == t)
                def _(t=t):
                    for event in events[t]:
                        event()

        @pl.when((turn == 0) & (step > 0))
        def _():
            ka_keep(pair - 1).wait()

        @pl.when(turn == 0)
        def _():
            lane = lax.broadcasted_iota(jnp.int32, (tok, LANES), 1)
            for j in range(g):
                span = slice(j * tok, (j + 1) * tok)
                column = jnp.broadcast_to(kb[j, 0:1, :], (LANES, tok)).T
                first, second, third = thirds(column)
                extra = jnp.where(
                    lane == 0, first,
                    jnp.where(lane == 1, second, jnp.where(lane == 2, third, 1.0)),
                )
                ka[span, :LANES] = k_s[pair, span, :]
                ka[span, LANES:] = jnp.where(lane < 6, extra, 0.0).astype(LOW)
                va[span, :LANES] = v_s[pair, span, :]
                va[span, LANES:] = jnp.where(lane < 3, 1.0, 0.0).astype(LOW)
            ka_keep(pair).start()

        span = pl.ds(pl.multiple_of(block * rows, rows), rows)
        lane = lax.broadcasted_iota(jnp.int32, (rows, LANES), 1)
        queries = q_s[pair, span, :].astype(F32) * SCALE
        ones = jnp.where(lane < 3, 1.0, 0.0)
        outs = []
        for head in range(2):
            masked = jnp.where(head_mask(rows, head), queries, 0.0)
            wide = jnp.concatenate([masked, ones], 1).astype(LOW)
            scores = matmul_right(wide, ka[...])
            row_max = jnp.max(scores, -1, keepdims=True)
            expo = jnp.exp(scores - row_max).astype(LOW)
            both = matmul(expo, va[...])
            total = both[:, LANES : LANES + 1]
            outs.append(both[:, :LANES] / total)
            first, second, third = thirds(row_max + jnp.log(total))
            qx[pair, head, span, :] = jnp.where(
                lane == 3, -first,
                jnp.where(lane == 4, -second, jnp.where(lane == 5, -third, ones)),
            ).astype(LOW)
        ctx[pair, span, :] = jnp.where(head_mask(rows, 0), outs[0], outs[1]).astype(LOW)

        for p in range(pairs):
            for k in range(1, g):
                @pl.when(step == p * blocks + k * per - 1)
                def _(p=p, k=k):
                    ctx_copy(p, k, s).start()

            @pl.when(step == (p + 1) * blocks - 1)
            def _(p=p):
                ctx_keep(p).start()
        return carry

    lax.fori_loop(0, steps, attend, 0)
    ka_keep(pairs - 1).wait()
    last = [
        pltpu.make_async_copy(qx, qx_out, loc.at[12]),
        pltpu.make_async_copy(ctx, own_ctx, loc.at[13]),
    ]
    for copy in last:
        copy.start()
    for event in late:
        event()
    for k in range(1, g):
        kb_copy(k, s).wait_send()
    for k in range(1, ny):
        for part in range(3):
            y_copy(k, part, s).wait_send()
            f_copy(k, part, me.y_from(k)).wait_send()
    c_copy(s).wait_send()
    for k in range(1, nz):
        wz_copy(k, d).wait_send()
        slot = me.z_from(k)
        wx_copy(k, wch.at[slot], slot).wait_send()
    wx_copy(0, wch_ref, d).wait_send()
    for pair in range(pairs):
        ctx_keep(pair).wait()
        for k in range(1, g):
            ctx_copy(pair, k, me.s_from(k)).wait_recv()
            ctx_copy(pair, k, s).wait_send()
    for p in range(len(pieces)):
        piece_end(p)
    for copy in saves + last + keep:
        copy.wait()


def attend_forward(hidden, chunk, bias_rows, w_out, w_up, w_down):
    n, g = lax.axis_size("dp"), lax.axis_size("seq")
    tok, width = hidden.shape
    length, gw, deep = tok * g, width // g, width // n
    pairs = gw // LANES
    count = len(weight_pieces([w.shape for w in (w_out, w_up, w_down)], g))
    anyw = pl.BlockSpec(memory_space=pl.ANY)
    low = lambda *shape: jax.ShapeDtypeStruct(shape, LOW)
    out_shape = [
        low(tok, width), low(pairs, length, LANES), low(pairs, length, LANES),
        low(pairs, length, 2 * LANES), low(pairs, length, LANES), low(pairs, 2, length, LANES),
        low(g, tok, width), low(width, 3 * gw), low(n, 16, 3 * gw),
        low(n, *w_out.shape), low(n, *w_up.shape), low(n, *w_down.shape),
    ]
    dma = lambda *shape: pltpu.SemaphoreType.DMA(shape)
    nz, ny = n // 2, max(g // 2, 2)
    vmem = lambda shape, kind=LOW: pltpu.VMEM(shape, kind)
    return pl.pallas_call(
        functools.partial(forward_kernel, n=n, g=g, rows=256),
        in_specs=[anyw] * 6,
        out_specs=[anyw] * 12,
        out_shape=out_shape,
        scratch_shapes=[
            vmem((g, tok, width)), vmem((n, deep + 16, 3 * gw)), vmem((width, 3 * gw)),
            vmem((g, 8, tok), F32), vmem((pairs, length, LANES)), vmem((pairs, length, LANES)),
            vmem((pairs, length, LANES)), vmem((length, 2 * LANES)), vmem((length, 2 * LANES)),
            vmem((pairs, length, LANES)), vmem((pairs, 2, length, LANES)),
            dma(14), dma(2, ny, 3), dma(2), dma(2, ny, 3), dma(2, g), dma(2, nz), dma(2, nz),
            dma(2, count, nz), dma(2, count, nz), dma(2, count, nz, 2),
            dma(2, count, ny, nz, 2), dma(2, count, ny, nz, 2), dma(2, pairs, g), dma(pairs),
        ],
        compiler_params=pltpu.CompilerParams(
            vmem_limit_bytes=56 * 2**20, collective_id=0, has_side_effects=True
        ),
        cost_estimate=cost(length, 4),
    )(hidden, chunk, bias_rows, w_out, w_up, w_down)


def piece_rows(n):
    return max(16, 512 // n)


def grad_pieces(shapes, n, g, wide):
    halves, quarters = [], []
    for index, (rows, cols) in enumerate(shapes):
        quarter = rows % (16 * g) == 0 and index == 2
        own = rows // g if quarter else rows // 2
        size = min(own, piece_rows(n))
        for off in range(0, own, size):
            for col in range(0, cols, wide):
                (quarters if quarter else halves).append((index, off, col, quarter))
    out = halves[:3]
    rest = halves[3:]
    for piece in quarters:
        out.append(piece)
        out += rest[:1]
        rest = rest[1:]
    return out + rest


def grad_times(pieces):
    times, lines, x_free, z_free = [], [], 0.0, 0.0
    y_free = 5.0
    at = 2
    for piece in pieces:
        first = None
        if piece[3]:
            first = 3 if not lines else lines[-1] + 2
            lines.append(first)
            y_free = max(y_free, first) + 5.0
            at = max(at, int(y_free) + 1)
        start = max(at, int(x_free - 1.0))
        x_free = max(x_free, start) + PIECE_STEPS
        side = int(x_free + 0.9)
        z_free = max(z_free, side) + PIECE_STEPS
        line = int(z_free + 0.9)
        times.append((first, start, side, line, line + 2))
        at = start + 2
    return times


def backward_kernel(
    dctx_ref, q_ref, ka_ref, v_ref, qx_ref, o_ref, hid_ref, wq_ref, vec_ref, go_ref, gu_ref,
    gd_ref,
    din_out, so_out, su_out, sd_out, sq_out, extra_out, c_land, x_land,
    q_s, ka, va, kt, qx, o_s, do_s, dh, dk_acc, dv_acc, hid, wq, vec,
    part_c, part_k, part_y, part_b, din, own_b, c_b, s_b, x_b, t_b, z_b, u_b, y_b, f_b,
    q_b, xq, tq, zq, rq, far_b, far_l,
    loc, ld, sd, sk, sy, sc, sx, sz, sg, sf, sl, sxq, szq, sgq, sfar, sfr,
    *, n, g, rows, chunk,
):
    me = Peers(n, g)
    d, s, nz, ny = me.d, me.s, me.nz, me.ny
    tok, width = dctx_ref.shape
    length = tok * g
    deep = width // n
    gw = width // g
    pairs = gw // LANES
    grads = (go_ref, gu_ref, gd_ref)
    wide = own_b.shape[3]
    size = own_b.shape[2]
    outs = (so_out, su_out, sd_out)
    pieces = grad_pieces([ref.shape[1:] for ref in grads], n, g, wide)
    times = grad_times(pieces)
    count = len(pieces)
    lands, spots = [], {}
    for p, piece in enumerate(pieces):
        for r in range(ny if piece[3] else 1):
            spots[p, r] = len(lands)
            lands.append((p, r))
    fars = [p for p in range(count) if pieces[p][3]]
    blocks = length // rows
    per = tok // rows
    steps = pairs * blocks
    me.barrier()

    def dctx_copy(pair, k, slot):
        cols = pl.ds(pl.multiple_of(me.s_to(k) * gw + pair * LANES, LANES), LANES)
        return send_to(
            dctx_ref.at[:, cols], do_s.at[pair, pl.ds(pl.multiple_of(slot * tok, tok), tok)],
            sd.at[0, pair, k], sd.at[1, pair, k], d, me.s_to(k),
        )

    def dctx_own(pair):
        cols = pl.ds(pl.multiple_of(s * gw + pair * LANES, LANES), LANES)
        return pltpu.make_async_copy(
            dctx_ref.at[:, cols], do_s.at[pair, pl.ds(pl.multiple_of(s * tok, tok), tok)],
            sl.at[pair],
        )

    def pair_loads(pair):
        return [
            pltpu.make_async_copy(q_ref.at[pair], q_s, loc.at[0]),
            pltpu.make_async_copy(ka_ref.at[pair], ka, loc.at[1]),
            pltpu.make_async_copy(v_ref.at[pair], va.at[:, pl.ds(0, LANES)], loc.at[2]),
            pltpu.make_async_copy(qx_ref.at[pair], qx, loc.at[3]),
            pltpu.make_async_copy(o_ref.at[pair], o_s, loc.at[4]),
        ]

    tail_loads = [
        pltpu.make_async_copy(hid_ref, hid, loc.at[5]),
        pltpu.make_async_copy(wq_ref, wq, loc.at[6]),
        pltpu.make_async_copy(vec_ref, vec, loc.at[7]),
    ]

    def row_of(p, core, y_at):
        index, off, col, quarter = pieces[p]
        own = grads[index].shape[1] // 2
        at = core * own + off
        if quarter:
            at = at + y_at * (own // ny)
        return pl.multiple_of(at, 16)

    def part_of(p, r, core):
        index, off, col, quarter = pieces[p]
        row = row_of(p, core, lax.rem(me.y + r, ny))
        return grads[index].at[:, pl.ds(row, size), pl.ds(col, wide)]

    def core_copy(p, r):
        i = spots[p, r]
        return send_to(
            part_of(p, r, 1 - me.c), c_land.at[i], sc.at[0, i], sc.at[1, i], d, me.cpeer
        )

    def own_load(p, r):
        i = spots[p, r] % 2
        return pltpu.make_async_copy(part_of(p, r, me.c), own_b.at[i], ld.at[0, i])

    def core_load(p, r):
        i = spots[p, r] % 2
        return pltpu.make_async_copy(c_land.at[spots[p, r]], c_b.at[i], ld.at[1, i])

    def y_copy(p, r):
        i = fars.index(p)
        return send_to(
            far_b.at[i], far_l.at[i, r - 1], sfar.at[0, i, r], sfar.at[1, i, r], d, me.y_to(r)
        )

    def side_copy(p):
        return send_to(
            s_b.at[p % 3, pl.ds(0, nz)], x_land.at[p], sx.at[0, p], sx.at[1, p], me.xpeer, s
        )

    def line_copy(p, k):
        return send_to(
            t_b.at[p % 3, lax.rem(me.z + k, nz)], z_b.at[p, k - 1], sz.at[0, p, k], sz.at[1, p, k],
            me.z_to(k), s,
        )

    def up_copy(p, k):
        return send_to(
            u_b.at[p], y_b.at[p, k], sy.at[0, p, k], sy.at[1, p, k], d, me.y_to(k)
        )

    def done_at(p, seq):
        index, off, col, quarter = pieces[p]
        row = row_of(p, lax.rem(seq, 2), seq // 2)
        return outs[index].at[pl.ds(row, size), pl.ds(col, wide)]

    def fin_hops(p):
        return range(1, g) if pieces[p][3] else (0,)

    def fin_copy(p, k, seq):
        to = me.s_to(k) if k else me.cpeer
        return send_to(f_b.at[p], done_at(p, seq), sf.at[0, p, k], sf.at[1, p, k], d, to)

    def fin_keep(p):
        return pltpu.make_async_copy(f_b.at[p], done_at(p, s), sg.at[p])

    def load(p, r):
        own_load(p, r).start()
        core_copy(p, r).wait_recv()
        core_load(p, r).start()

    def far_sum(p):
        for r in range(1, ny):
            i = spots[p, r] % 2
            own_load(p, r).wait()
            core_load(p, r).wait()

            def add(j, carry, i=i):
                total = own_b[i, j].astype(F32) + c_b[i, j].astype(F32)
                far_b[fars.index(p), j] = total.astype(LOW)
                return carry

            lax.fori_loop(0, n, add, 0)
            y_copy(p, r).start()

    def e2(p):
        slot, i = p % 3, spots[p, 0] % 2
        own_load(p, 0).wait()
        core_load(p, 0).wait()
        if pieces[p][3]:
            for r in range(1, ny):
                y_copy(p, r).wait_recv()
        if p >= 3:
            side_copy(p - 3).wait_send()

        def add(j, carry):
            for part in range(2):
                at = 2 * j + (1 - me.x if part == 0 else me.x)
                total = own_b[i, at].astype(F32) + c_b[i, at].astype(F32)
                if pieces[p][3]:
                    for r in range(1, ny):
                        total = total + far_l[fars.index(p), r - 1, at].astype(F32)
                s_b[slot, part * nz + j] = total.astype(LOW)
            return carry

        lax.fori_loop(0, nz, add, 0)
        side_copy(p).start()

    def e3(p):
        slot = p % 3
        side_copy(p).wait_recv()
        get = pltpu.make_async_copy(x_land.at[p], x_b, loc.at[8])
        get.start()
        if p >= 3:
            for k in range(1, nz):
                line_copy(p - 3, k).wait_send()
        get.wait()

        def add(j, carry):
            total = s_b[slot, nz + j].astype(F32) + x_b[j].astype(F32)
            t_b[slot, j] = total.astype(LOW)
            return carry

        lax.fori_loop(0, nz, add, 0)
        for k in range(1, nz):
            line_copy(p, k).start()

    def finish(p):
        for k in fin_hops(p):
            fin_copy(p, k, s).start()
        fin_keep(p).start()

    def e4(p):
        slot = p % 3
        for k in range(1, nz):
            line_copy(p, k).wait_recv()
        total = t_b[slot, me.z].astype(F32)
        for k in range(1, nz):
            total = total + z_b[p, k - 1].astype(F32)
        if pieces[p][3]:
            f_b[p] = total.astype(LOW)
            finish(p)
        else:
            u_b[p] = total.astype(LOW)
            for k in range(1, ny):
                up_copy(p, k).start()

    def e5(p):
        if pieces[p][3]:
            return
        for k in range(1, ny):
            up_copy(p, k).wait_recv()
        total = u_b[p].astype(F32)
        for k in range(1, ny):
            total = total + y_b[p, k].astype(F32)
        f_b[p] = total.astype(LOW)
        finish(p)

    plan = []
    for p in range(count):
        first, start, side, line, end = times[p]
        if first is not None:
            for r in range(1, ny):
                plan.append((first - 1, 5, lambda p=p, r=r: load(p, r)))
            plan.append((first, 4, lambda p=p: far_sum(p)))
        plan.append((start - 1, 5, lambda p=p: load(p, 0)))
        for r in range(ny if first is not None else 1):
            at = start if r == 0 else first
            plan.append((at - 3, 6, lambda p=p, r=r: core_copy(p, r).start()))
        plan.append((start, 3, lambda p=p: e2(p)))
        plan.append((side, 2, lambda p=p: e3(p)))
        plan.append((line, 1, lambda p=p: e4(p)))
        plan.append((end, 0, lambda p=p: e5(p)))
    plan.sort(key=lambda item: item[:2])

    for pair in range(pairs):
        dctx_own(pair).start()
        for k in range(1, g):
            dctx_copy(pair, k, s).start()
    for copy in tail_loads:
        copy.start()
    for at, order, event in plan:
        if at < 0:
            event()
    lane_l = lax.broadcasted_iota(jnp.int32, (tok, LANES), 1)
    for j in range(g):
        va[j * tok : (j + 1) * tok, LANES:] = jnp.where(lane_l < 3, 1.0, 0.0).astype(LOW)

    near = [me.y * 2, me.y * 2 + 1]
    far_slots = [lax.rem(me.y + k, ny) * 2 + i for k in range(1, ny) for i in range(2)]
    near_blocks = 2 * per
    full = steps - near_blocks

    def run_events(step):
        for t in sorted({item[0] for item in plan}):
            if 0 <= t < steps:
                @pl.when(step == t)
                def _(t=t):
                    for at, order, event in plan:
                        if at == t:
                            event()

    def block_pass(pair, block, slots):
        span = pl.ds(pl.multiple_of(block * rows, rows), rows)
        lane = lax.broadcasted_iota(jnp.int32, (rows, LANES), 1)
        queries = q_s[span, :].astype(F32) * SCALE
        upstream = do_s[pair, span, :].astype(F32)
        dots = upstream * o_s[span, :].astype(F32)
        q_wide, g_wide, q_mask, g_mask = [], [], [], []
        for head in range(2):
            mask = head_mask(rows, head)
            masked = jnp.where(mask, queries, 0.0).astype(LOW)
            g_masked = jnp.where(mask, upstream, 0.0).astype(LOW)
            delta = jnp.sum(jnp.where(mask, dots, 0.0), -1, keepdims=True)
            first, second, third = thirds(delta)
            extra = jnp.where(
                lane == 0, -first, jnp.where(lane == 1, -second, jnp.where(lane == 2, -third, 0.0))
            ).astype(LOW)
            q_mask.append(masked)
            g_mask.append(g_masked)
            q_wide.append(jnp.concatenate([masked, qx[head, span, :]], 1))
            g_wide.append(jnp.concatenate([g_masked, extra], 1))
        q_rows = jnp.concatenate(q_mask, 0)
        g_rows = jnp.concatenate(g_mask, 0)
        dq_t = [jnp.zeros((LANES, rows), F32) for _ in range(2)]
        for slot in slots:
            for base in range(0, tok, chunk):
                at = slot * tok + base
                part = slice(at, at + chunk)
                if not isinstance(at, int):
                    part = pl.ds(pl.multiple_of(at, LANES), chunk)
                p_list, ds_list = [], []
                for head in range(2):
                    probs = jnp.exp(matmul_right(ka[part, :], q_wide[head]))
                    d_scores = (probs * matmul_right(va[part, :], g_wide[head])).astype(LOW)
                    p_list.append(probs.astype(LOW))
                    ds_list.append(d_scores)
                    dq_t[head] = dq_t[head] + matmul(kt[:, part], d_scores)
                dv_acc[part, :] += matmul(jnp.concatenate(p_list, 1), g_rows)
                dk_acc[part, :] += matmul(jnp.concatenate(ds_list, 1), q_rows)
        row = lax.broadcasted_iota(jnp.int32, (LANES, rows), 0)
        return jnp.where(row < HEAD_DIM, dq_t[0], dq_t[1]) * SCALE

    def attend(step, carry):
        pair = step // blocks
        turn = lax.rem(step, blocks)
        rel = turn // per
        owner = lax.rem(s + g - rel, g)
        owner = jnp.where(pair == pairs - 1, lax.rem(me.y * 2 + 2 + rel, g), owner)
        block = owner * per + lax.rem(turn, per)

        @pl.when(turn == 0)
        def _():
            loads = pair_loads(pair)
            for copy in loads:
                copy.start()
            dk_acc[...] = jnp.zeros_like(dk_acc)
            dv_acc[...] = jnp.zeros_like(dv_acc)
            dctx_own(pair).wait()
            for copy in loads:
                copy.wait()
            for j in range(length // chunk):
                part = slice(j * chunk, (j + 1) * chunk)
                kt[:, part] = ka[part, :LANES].astype(F32).T.astype(LOW)

        run_events(step)
        for k in range(1, g):
            @pl.when(turn == jnp.where(pair == pairs - 1, 0, k * per))
            def _(k=k):
                dctx_copy(pair, k, me.s_from(k)).wait_recv()

        both = block_pass(pair, block, range(g))
        dh[pair, pl.ds(pl.multiple_of(block * rows, rows), rows), :] = both.T.astype(LOW)

        @pl.when(turn == blocks - 1)
        def _():
            dh[pairs + pair] = dk_acc[...].astype(LOW)
            dh[2 * pairs + pair] = dv_acc[...].astype(LOW)
        return carry

    lax.fori_loop(0, full, attend, 0)
    last = pairs - 1

    def keep_heads(slots):
        for slot in slots:
            span = pl.ds(pl.multiple_of(slot * tok, tok), tok)
            dh[pairs + last, span, :] = dk_acc[span, :].astype(LOW)
            dh[2 * pairs + last, span, :] = dv_acc[span, :].astype(LOW)

    def far_keys(i, carry):
        @pl.when(lax.rem(i, 2) == 0)
        def _():
            run_events(full + i // 2)

        both = block_pass(last, me.y * near_blocks + i, far_slots)
        din[pl.ds(pl.multiple_of(i * LANES, LANES), LANES), :rows] = both
        return carry

    def near_keys(i, carry):
        @pl.when(lax.rem(i, 2) == 0)
        def _():
            run_events(full + (near_blocks + i) // 2)

        block = me.y * near_blocks + i
        both = block_pass(last, block, near)
        both = both + din[pl.ds(pl.multiple_of(i * LANES, LANES), LANES), :rows]
        dh[last, pl.ds(pl.multiple_of(block * rows, rows), rows), :] = both.T.astype(LOW)
        return carry

    lax.fori_loop(0, near_blocks, far_keys, 0)
    keep_heads(far_slots)
    for copy in tail_loads:
        copy.wait()
    def heads_of(slot, tile):
        span = pl.ds(pl.multiple_of(slot * tok + tile * rows, rows), rows)
        return jnp.concatenate([dh[i, span, :] for i in range(3 * pairs)], 1)

    def part_copy(k, tile):
        span = pl.ds(pl.multiple_of(tile * rows, rows), rows)
        return send_to(
            part_c.at[k, span], part_k.at[k, span], sk.at[0, k, tile], sk.at[1, k, tile], d,
            me.cpeer,
        )

    def far_copy(k, tile):
        span = pl.ds(pl.multiple_of(tile * rows, rows), rows)
        return send_to(
            part_b.at[k - 1, span], part_y.at[k - 1, span], sfr.at[0, k, tile], sfr.at[1, k, tile],
            d, me.y_to(k),
        )

    def core_part(k):
        slot = lax.rem(me.y + k, ny) * 2 + 1 - me.c

        def tile_of(tile, carry):
            span = pl.ds(pl.multiple_of(tile * rows, rows), rows)
            part_c[k, span, :] = matmul_right(heads_of(slot, tile), wq[...]).astype(LOW)
            part_copy(k, tile).start()
            return carry

        lax.fori_loop(0, per, tile_of, 0)

    for k in range(1, ny):
        core_part(k)
    for k in range(1, ny):
        slot = lax.rem(me.y + k, ny) * 2 + me.c

        def far_tile(tile, carry, k=k, slot=slot):
            span = pl.ds(pl.multiple_of(tile * rows, rows), rows)
            total = matmul_right(heads_of(slot, tile), wq[...])
            part_copy(k, tile).wait_recv()
            total = total + part_k[k, span, :].astype(F32)
            part_b[k - 1, span, :] = total.astype(LOW)
            far_copy(k, tile).start()
            return carry

        lax.fori_loop(0, per, far_tile, 0)

    lax.fori_loop(0, near_blocks, near_keys, 0)
    keep_heads(near)
    for at, order, event in plan:
        if at >= steps and order in (3, 4, 5, 6):
            event()

    sums = [jnp.zeros((1, LANES), F32) for _ in range(3 * pairs)]
    for i in range(3 * pairs):
        for j in range(g):
            span = slice(j * tok, (j + 1) * tok)
            sums[i] = sums[i] + jnp.sum(dh[i, span, :].astype(F32), 0, keepdims=True)
    sums = jnp.concatenate(sums, 1)
    row16 = lax.broadcasted_iota(jnp.int32, (16, 3 * gw), 0)
    for j in range(n):
        q_b[j, deep:, :] = (vec[j].astype(F32) + jnp.where(row16 == 0, sums, 0.0)).astype(LOW)

    def qx_copy(j):
        return send_to(
            q_b.at[2 * j + 1 - me.x], xq.at[j], sxq.at[0, j], sxq.at[1, j], me.xpeer, s
        )

    def qz_copy(k):
        return send_to(
            tq.at[lax.rem(me.z + k, nz)], zq.at[k], szq.at[0, k], szq.at[1, k], me.z_to(k), s
        )

    def q_parts(source):
        parts = [(rq.at[pl.ds(deep, 16)], extra_out.at[source])]
        for i in range(3):
            at = pl.ds(pl.multiple_of(i * width + source * gw, LANES), gw)
            parts.append((rq.at[pl.ds(0, deep), pl.ds(i * gw, gw)], sq_out.at[:, at]))
        return parts

    def q_out_copies(k, source):
        return [
            send_to(src, dst, sgq.at[0, i, k], sgq.at[1, i, k], d, me.s_to(k))
            for i, (src, dst) in enumerate(q_parts(source))
        ]

    tile_w = 256
    for base in range(0, width, tile_w):
        total = jnp.zeros((tile_w, 3 * gw), F32)
        for j in range(g):
            right = jnp.concatenate(
                [dh[i, j * tok : (j + 1) * tok, :] for i in range(3 * pairs)], 1
            )
            total = total + matmul_left(hid[j, :, base : base + tile_w], right)
        for at in range(0, tile_w, deep):
            q_b[(base + at) // deep, :deep, :] = total[at : at + deep, :].astype(LOW)
        for j in range(base // deep // 2, (base + tile_w) // deep // 2):
            qx_copy(j).start()
    for at, order, event in plan:
        if at >= steps and order == 2:
            event()

    core_part(0)

    def own_tile(tile, carry):
        span = pl.ds(pl.multiple_of(tile * rows, rows), rows)
        din[span, :] = matmul_right(heads_of(s, tile), wq[...])
        return carry

    lax.fori_loop(0, per, own_tile, 0)

    for at, order, event in plan:
        if at >= steps and order in (0, 1):
            event()

    for j in range(nz):
        qx_copy(j).wait_recv()
        kept = q_b[2 * j + me.x].astype(F32) + xq[j].astype(F32)
        tq[j] = kept.astype(LOW)
    for k in range(1, nz):
        qz_copy(k).start()
    for k in range(1, nz):
        qz_copy(k).wait_recv()
    total = tq[me.z].astype(F32)
    for k in range(1, nz):
        total = total + zq[k].astype(F32)
    rq[...] = total.astype(LOW)
    for k in range(1, g):
        for copy in q_out_copies(k, s):
            copy.start()
    keep_q = [
        pltpu.make_async_copy(src, dst, loc.at[11 + i])
        for i, (src, dst) in enumerate(q_parts(s))
    ]
    for copy in keep_q:
        copy.start()

    def sum_tile(tile, carry):
        span = pl.ds(pl.multiple_of(tile * rows, rows), rows)
        part_copy(0, tile).wait_recv()
        for k in range(1, ny):
            far_copy(k, tile).wait_recv()
        total = din[span, :] + part_k[0, span, :].astype(F32)
        for k in range(1, ny):
            total = total + part_y[k - 1, span, :].astype(F32)
        din[span, :] = total
        return carry

    lax.fori_loop(0, per, sum_tile, 0)
    keep_d = pltpu.make_async_copy(din, din_out, loc.at[10])
    keep_d.start()

    for p, r in lands:
        core_copy(p, r).wait_send()
        if r:
            y_copy(p, r).wait_send()
    for p in range(count):
        for k in fin_hops(p):
            fin_copy(p, k, me.s_from(k) if k else me.cpeer).wait_recv()
            fin_copy(p, k, s).wait_send()
        fin_keep(p).wait()
        if not pieces[p][3]:
            for k in range(1, ny):
                up_copy(p, k).wait_send()
        if p >= count - 3:
            side_copy(p).wait_send()
            for k in range(1, nz):
                line_copy(p, k).wait_send()
    for pair in range(pairs):
        for k in range(1, g):
            dctx_copy(pair, k, s).wait_send()
    for tile in range(per):
        for k in range(ny):
            part_copy(k, tile).wait_send()
        for k in range(1, ny):
            far_copy(k, tile).wait_send()
    for j in range(nz):
        qx_copy(j).wait_send()
    for k in range(1, nz):
        qz_copy(k).wait_send()
    for k in range(1, g):
        for copy in q_out_copies(k, me.s_from(k)):
            copy.wait_recv()
        for copy in q_out_copies(k, s):
            copy.wait_send()
    for copy in keep_q:
        copy.wait()
    keep_d.wait()


def cost(length, matmuls):
    return pl.CostEstimate(
        flops=2 * 2 * matmuls * length * length * 256,
        bytes_accessed=10 * length * LANES * 2,
        transcendentals=2 * length * length,
    )


def attend_backward(d_context, queries, keys, values, q_extra, context, hidden, w_heads, vecs,
                    g_out, g_up, g_down):
    n, g = lax.axis_size("dp"), lax.axis_size("seq")
    tok, width = d_context.shape
    length, gw, deep = tok * g, width // g, width // n
    pairs = gw // LANES
    nz, ny = n // 2, max(g // 2, 2)
    wide = min(1024, width)
    size = piece_rows(n)
    shares = [g.reshape(n, -1, g.shape[1]) for g in (g_out, g_up, g_down)]
    pieces = grad_pieces([share.shape[1:] for share in shares], n, g, wide)
    count = len(pieces)
    far = max(1, sum(piece[3] for piece in pieces))
    lands = count + (g // 2 - 1) * sum(piece[3] for piece in pieces)
    anyw = pl.BlockSpec(memory_space=pl.ANY)
    low = lambda *shape: jax.ShapeDtypeStruct(shape, LOW)
    vmem = lambda *shape: pltpu.VMEM(shape, LOW)
    vmem32 = lambda *shape: pltpu.VMEM(shape, F32)
    dma = lambda *shape: pltpu.SemaphoreType.DMA(shape)
    chunk = 768 if length % 768 == 0 else 256
    tall = deep + 16
    return pl.pallas_call(
        functools.partial(backward_kernel, n=n, g=g, rows=256, chunk=chunk),
        in_specs=[anyw] * 12,
        out_specs=[anyw] * 8,
        out_shape=[
            jax.ShapeDtypeStruct((tok, width), F32), *(low(*share.shape[1:]) for share in shares),
            low(deep, 3 * width), low(g, 16, 3 * gw), low(lands, n, size, wide),
            low(count, nz, size, wide),
        ],
        scratch_shapes=[
            vmem(length, LANES), vmem(length, 2 * LANES), vmem(length, 2 * LANES),
            vmem(LANES, length), vmem(2, length, LANES), vmem(length, LANES),
            vmem(pairs, length, LANES), vmem(3 * pairs, length, LANES), vmem32(length, LANES),
            vmem32(length, LANES), vmem(g, tok, width), vmem(width, 3 * gw), vmem(n, 16, 3 * gw),
            vmem(ny, tok, width), vmem(ny, tok, width), vmem(ny - 1, tok, width),
            vmem(ny - 1, tok, width), vmem32(tok, width),
            vmem(2, n, size, wide), vmem(2, n, size, wide), vmem(3, n, size, wide),
            vmem(nz, size, wide), vmem(3, nz, size, wide), vmem(count, nz - 1, size, wide),
            vmem(count, size, wide), vmem(count, ny, size, wide), vmem(count, size, wide),
            vmem(n, tall, 3 * gw), vmem(nz, tall, 3 * gw), vmem(nz, tall, 3 * gw),
            vmem(nz, tall, 3 * gw), vmem(tall, 3 * gw), vmem(far, n, size, wide),
            vmem(far, ny - 1, n, size, wide),
            dma(15), dma(2, 2), dma(2, pairs, g), dma(2, ny, tok // 256), dma(2, count, ny),
            dma(2, lands), dma(2, count), dma(2, count, nz), dma(count), dma(2, count, g),
            dma(pairs), dma(2, nz), dma(2, nz), dma(2, 4, g), dma(2, far, ny),
            dma(2, ny, tok // 256),
        ],
        compiler_params=pltpu.CompilerParams(
            vmem_limit_bytes=63 * 2**20, collective_id=1, has_side_effects=True
        ),
        cost_estimate=cost(length, 10),
    )(d_context, queries, keys, values, q_extra, context, hidden, w_heads, vecs, *shares)


def gelu_parts(pre):
    size = jnp.abs(pre)
    t = 1.0 / (1.0 + (0.3275911 * 0.7071067811865476) * size)
    bell = jnp.exp(-0.5 * pre * pre)
    poly = t * (0.127414796 + t * (-0.142248368 + t * (
        0.7107068705 + t * (-0.7265760135 + t * 0.5307027145))))
    tail = poly * bell
    phi = jnp.where(pre >= 0, 1.0 - tail, tail)
    return phi, bell * 0.3989422804014327


def up_kernel(x_ref, wu_ref, bu_ref, wd_ref, act_ref, slope_ref, sum_ref):
    pre = matmul(x_ref[...], wu_ref[...]) + bu_ref[...]
    phi, density = gelu_parts(pre)
    activ = (pre * phi).astype(LOW)
    act_ref[...] = activ
    slope_ref[...] = (phi + pre * density).astype(LOW)
    part = matmul(activ, wd_ref[...])

    @pl.when(pl.program_id(0) == 0)
    def _():
        sum_ref[...] = part

    @pl.when(pl.program_id(0) > 0)
    def _():
        sum_ref[...] += part


def feed_forward(normed_low, w_up, bias_up, w_down):
    tok, width = normed_low.shape
    ff = w_up.shape[1]
    tile = 512
    whole = pl.BlockSpec((tok, width), lambda i: (0, 0))
    col = pl.BlockSpec((tok, tile), lambda i: (0, i))
    return pl.pallas_call(
        up_kernel,
        grid=(ff // tile,),
        in_specs=[
            whole, pl.BlockSpec((width, tile), lambda i: (0, i)),
            pl.BlockSpec((1, tile), lambda i: (0, i)), pl.BlockSpec((tile, width), lambda i: (i, 0)),
        ],
        out_specs=[col, col, whole],
        out_shape=[
            jax.ShapeDtypeStruct((tok, ff), LOW), jax.ShapeDtypeStruct((tok, ff), LOW),
            jax.ShapeDtypeStruct((tok, width), F32),
        ],
        compiler_params=pltpu.CompilerParams(vmem_limit_bytes=48 * 2**20),
    )(normed_low, w_up, bias_up[None], w_down)


def down_kernel(
    x_ref, e_ref, wu_ref, wd_ref, act_ref, slope_ref, gu_ref, gd_ref, gb_ref, sum_ref,
):
    up = e_ref[...]
    d_pre = matmul_right(up, wd_ref[...]) * slope_ref[...].astype(F32)
    gb_ref[...] = jnp.sum(d_pre, 0, keepdims=True)
    d_low = d_pre.astype(LOW)
    gd_ref[...] = matmul_left(act_ref[...], up).astype(LOW)
    gu_ref[...] = matmul_left(x_ref[...], d_low).astype(LOW)
    part = matmul_right(d_low, wu_ref[...])

    @pl.when(pl.program_id(0) == 0)
    def _():
        sum_ref[...] = part

    @pl.when(pl.program_id(0) > 0)
    def _():
        sum_ref[...] += part


def feed_backward(normed_low, d_low, w_up, w_down, activ, slope):
    tok, width = normed_low.shape
    ff = w_up.shape[1]
    tile = 512
    whole = pl.BlockSpec((tok, width), lambda i: (0, 0))
    col = pl.BlockSpec((tok, tile), lambda i: (0, i))
    up = pl.BlockSpec((width, tile), lambda i: (0, i))
    down = pl.BlockSpec((tile, width), lambda i: (i, 0))
    return pl.pallas_call(
        down_kernel,
        grid=(ff // tile,),
        in_specs=[whole, whole, up, down, col, col],
        out_specs=[up, down, pl.BlockSpec((1, tile), lambda i: (0, i)), whole],
        out_shape=[
            jax.ShapeDtypeStruct((width, ff), LOW), jax.ShapeDtypeStruct((ff, width), LOW),
            jax.ShapeDtypeStruct((1, ff), F32), jax.ShapeDtypeStruct((tok, width), F32),
        ],
        compiler_params=pltpu.CompilerParams(vmem_limit_bytes=48 * 2**20),
    )(normed_low, d_low, w_up, w_down, activ, slope)


def own_columns(piece, width, group_width):
    count = width // piece.shape[0]
    mine = lax.broadcasted_iota(jnp.int32, (count, piece.shape[0]), 0) == lax.axis_index("dp")
    row = jnp.where(mine, piece[None], jnp.zeros((), LOW)).reshape(-1)
    return lax.dynamic_slice_in_dim(row, lax.axis_index("seq") * group_width, group_width, 0)


def laid(parts, total):
    out, at = None, 0
    for part in parts:
        if part is not None:
            one = jnp.pad(part, (at, total - at - part.shape[0]))
            out = one if out is None else out + one
            at += part.shape[0]
    return out


def local(
    hidden_in, key_bias, w_qkv, bias_q, bias_v, w_out, bias_out, gain_attn, shift_attn,
    w_up, bias_up, w_down, bias_down, gain_ffn, shift_ffn, grad_out,
):
    groups = lax.axis_size("seq")
    me = lax.axis_index("seq")
    tok_rows, width = hidden_in.shape
    group_width = width // groups
    deep = w_qkv.shape[0]
    shares = lax.axis_size("dp")

    vectors = (
        bias_q, bias_v, bias_out, gain_attn, shift_attn, bias_down, gain_ffn, shift_ffn, bias_up,
    )
    line = 3 * group_width
    filled = sum(vector.shape[0] for vector in vectors)
    tall = -(-filled // line)
    packed = laid(vectors, 15 * line)
    first_row = laid([own_columns(bias_q, width, group_width)], line) + jnp.pad(
        own_columns(bias_v, width, group_width), (2 * group_width, 0)
    )
    rows16 = jnp.concatenate([first_row, packed]).reshape(16, line)
    own_w = jnp.concatenate(
        [lax.dynamic_slice_in_dim(w_qkv, i * width + me * group_width, group_width, 1) for i in range(3)], 1
    )
    chunk = jnp.concatenate([own_w, rows16], 0)
    bias_rows = jnp.broadcast_to(key_bias, (8, tok_rows))
    (context, own_context, q_all, ka_all, v_all, q_extra, hidden_all, w_heads, vec_all, f_w_out,
     f_w_up, f_w_down) = attend_forward(hidden_in, chunk, bias_rows, w_out, w_up, w_down)
    f_w_out = f_w_out.reshape(-1, w_out.shape[1])
    f_w_up = f_w_up.reshape(-1, w_up.shape[1])
    f_w_down = f_w_down.reshape(-1, w_down.shape[1])
    packed = vec_all[:, 1 : 1 + tall].reshape(vec_all.shape[0], -1).astype(F32)
    fulls, at = [], 0
    for vector in vectors:
        fulls.append(packed[:, at : at + vector.shape[0]].reshape(-1))
        at += vector.shape[0]
    (f_bias_q, f_bias_v, f_bias_out, f_gain_attn, f_shift_attn, f_bias_down, f_gain_ffn,
     f_shift_ffn, f_bias_up) = fulls

    attended = hidden_in.astype(F32) + matmul(context, f_w_out) + f_bias_out
    normed = layer_norm(attended, f_gain_attn, f_shift_attn)
    normed_low = normed.astype(LOW)
    activ, slope, branch = feed_forward(normed_low, f_w_up, f_bias_up, f_w_down)
    branch_sum = normed + branch + f_bias_down
    output = layer_norm(branch_sum, f_gain_ffn, f_shift_ffn).astype(LOW)

    upstream = grad_out.astype(F32)
    _, norm_back = jax.vjp(layer_norm, branch_sum, f_gain_ffn, f_shift_ffn)
    d_branch, g_gain_ffn, g_shift_ffn = norm_back(upstream)
    g_bias_down = jnp.sum(d_branch, 0)
    d_branch_low = d_branch.astype(LOW)
    g_w_up, g_w_down, g_bias_up, d_up = feed_backward(
        normed_low, d_branch_low, f_w_up, f_w_down, activ, slope
    )
    d_normed = d_branch + d_up
    _, attn_norm_back = jax.vjp(layer_norm, attended, f_gain_attn, f_shift_attn)
    d_attended, g_gain_attn, g_shift_attn = attn_norm_back(d_normed)
    g_bias_out = jnp.sum(d_attended, 0)
    d_attended_low = d_attended.astype(LOW)
    g_w_out = matmul_left(context, d_attended_low).astype(LOW)
    d_context = matmul_right(d_attended_low, f_w_out).astype(LOW)

    vector_grads = (
        g_bias_out, g_gain_attn, g_shift_attn, g_bias_down, g_gain_ffn, g_shift_ffn, g_bias_up,
    )
    rows = jnp.concatenate([g.reshape(shares, -1) for g in vector_grads], 1).astype(LOW)
    filled = rows.shape[1]
    tall = -(-filled // (3 * group_width))
    vecs = jnp.pad(rows, ((0, 0), (0, tall * 3 * group_width - filled)))
    vecs = jnp.pad(vecs.reshape(shares, tall, -1), ((0, 0), (1, 15 - tall), (0, 0)))
    d_in, s_w_out, s_w_up, s_w_down, s_w_qkv, heads, _, _ = attend_backward(
        d_context, q_all, ka_all, v_all, q_extra, own_context, hidden_all, w_heads, vecs,
        g_w_out, g_w_up, g_w_down,
    )
    grad_in = d_attended + d_in
    s_w_out, s_w_up, s_w_down, s_w_qkv = (
        grad.astype(F32) for grad in (s_w_out, s_w_up, s_w_down, s_w_qkv)
    )
    head_rows = heads[:, 0].astype(F32)
    at = lax.axis_index("dp") * bias_q.shape[0]
    s_bias_q = lax.dynamic_slice_in_dim(
        head_rows[:, :group_width].reshape(-1), at, bias_q.shape[0], 0
    )
    s_bias_v = lax.dynamic_slice_in_dim(
        head_rows[:, 2 * group_width :].reshape(-1), at, bias_v.shape[0], 0
    )
    own = jnp.sum(heads[:, 1 : 1 + tall].astype(F32), 0).reshape(-1)
    own_vectors, at = [], 0
    for vector in vectors[2:]:
        own_vectors.append(own[at : at + vector.shape[0]])
        at += vector.shape[0]
    (s_bias_out, s_gain_attn, s_shift_attn, s_bias_down, s_gain_ffn, s_shift_ffn,
     s_bias_up) = own_vectors
    return (
        output, grad_in, s_w_qkv, s_bias_q, s_bias_v, s_w_out, s_bias_out, s_gain_attn,
        s_shift_attn, s_w_up, s_bias_up, s_w_down, s_bias_down, s_gain_ffn, s_shift_ffn,
    )


def solution(mesh):
    tokens = P(("dp", "seq"), None)
    matrix = P("dp", None)
    vector = P("dp")
    return jax.shard_map(
        local,
        mesh=mesh,
        in_specs=(
            tokens, P("dp", "seq"), matrix, vector, vector, matrix, vector, vector, vector,
            matrix, vector, matrix, vector, vector, vector, tokens,
        ),
        out_specs=(
            tokens, tokens, matrix, vector, vector, matrix, vector, vector, vector, matrix,
            vector, matrix, vector, vector, vector,
        ),
        check_vma=False,
    )
```
